32 devices in a mesh: wide: 8 (over y, x, core), narrow: 4 (over z).
Axes of the slice: x: 2, y: 2, z: 4, core: 2. Of those that a mesh axis runs over, the one named last changes fastest.
Arguments:
- residual: bfloat16 [2048, 4608], P('wide'), may hold values from -6 to 6
- pre_gain: bfloat16 [4608], replicated, may hold values from 0.5 to 1.5
- query_weight: bfloat16 [4608, 4096], P('wide', 'narrow'), may hold values from -0.09375 to 0.09375
- key_weight: bfloat16 [4608, 2048], P('wide', 'narrow'), may hold values from -0.09375 to 0.09375
- value_weight: bfloat16 [4608, 2048], P('wide', 'narrow'), may hold values from -0.09375 to 0.09375
- output_weight: bfloat16 [4096, 4608], P('narrow', 'wide'), may hold values from -1 to 1
- adapter_down: bfloat16 [4608, 768], P('wide', 'narrow'), may hold values from -0.09375 to 0.09375
- adapter_up_query: bfloat16 [256, 4096], P(None, 'narrow'), may hold values from -1.5 to 1.5
- adapter_up_key: bfloat16 [256, 2048], P(None, 'narrow'), may hold values from -1.5 to 1.5
- adapter_up_value: bfloat16 [256, 2048], P(None, 'narrow'), may hold values from -1.5 to 1.5
- adapter_down_out: bfloat16 [4096, 256], P('narrow'), may hold values from -0.09375 to 0.09375
- adapter_up_out: bfloat16 [256, 4608], P(None, 'narrow'), may hold values from -1.5 to 1.5
- post_gain: bfloat16 [4608], P('narrow'), may hold values from 0.5 to 1.5
- sink_logits: float32 [32], P('narrow'), may hold values from -1 to 130
- prompt_lengths: int32 [4], replicated, may hold values from 1 to 1024, 2048 in all
- prompt_adapters: int32 [4], replicated, may hold values from 0 to 15
Outputs:
- layer_out: bfloat16 [2048, 4608], P('wide', 'narrow')
The draws below stay inside these ranges and needn't reach their ends.
All inputs are finite; a program needn't handle non-finite values.
Results may differ from the reference program's by a relative error of at most 0.022.
Values may be sent and summed in bfloat16 or wider, within the bound.
No kernel may reach another device: no remote copies, remote signals or barrier semaphores. Data moves between devices by JAX's collectives and lax.ppermute only.
A program may use at most 128 MiB of HBM per device.

```python
import math
import jax
import jax.numpy as jnp
import numpy as np
from jax import lax

D = 4608
HEADS = 32
KV_HEADS = 16
HEAD_DIM = 128
RANK = 16
ADAPTERS = 16
PROMPTS = 4
TOKENS = 2048


def draw_output_weight(key, part):
    rows = HEADS * HEAD_DIM
    column = jnp.arange(D, dtype=jnp.float32) / (D - 1)
    base = jnp.clip(jax.random.normal(key, (rows, D), jnp.float32), -6.0, 6.0)
    scale = 1.0 + column
    return (base * scale[None, :] / math.sqrt(rows)).astype(jnp.bfloat16)


def draw_sink_logits(key, part):
    values = jax.random.uniform(key, (HEADS,), jnp.float32, -1.0, 3.0)
    return values


def plant(values, rng, low, largest):
    index_at = [jax.random.randint(jax.random.fold_in(rng, axis), (), 0, length) for axis, length in enumerate(values.shape)]
    longest = values.shape.index(max(values.shape))
    neighbour = index_at[:longest] + [(index_at[longest] + 1) % values.shape[longest]] + index_at[longest + 1:]
    return values.at[tuple(index_at)].set(low).at[tuple(neighbour)].set(largest)


def block_levels(stream_key, extent, cuts, least, top_value):
    def one(axis_at, blocks):
        heights = jax.random.uniform(jax.random.fold_in(jax.random.fold_in(stream_key, 6), axis_at), (blocks,), jnp.float32, least / len(cuts), top_value / len(cuts))
        return jnp.repeat(jnp.exp(heights), extent[axis_at] // blocks).reshape((-1,) + (1,) * (len(extent) - axis_at - 1))

    gain = one(*cuts[0])
    for cut in cuts[1:]:
        gain = gain * one(*cut)
    return gain


def length_profile(count, total, most, slope):
    loads = [(1 << 20) // math.isqrt(rank ** slope) + 1 for rank in range(2, count + 1)]
    rest, counts = total - most - (count - 1), [1] * (count - 1)
    while rest > 0:
        movable = [i for i in range(count - 1) if counts[i] < most]
        whole, budget = sum([loads[i] for i in movable]), rest
        for i in movable:
            more = min(most - counts[i], max(1, budget * loads[i] // whole), rest)
            counts[i] = counts[i] + more
            rest = rest - more
    return np.array([most] + counts)


def ragged_sizes(rng, count, total, limit, slope):
    if count == 2:
        one = jax.random.randint(rng, (), max(1, total - limit), min(limit, total - 1) + 1)
        return jnp.stack([one, total - one])
    sizes = jnp.asarray(length_profile(count, total, limit, slope), jnp.int32)
    couples = (count - 1) // 2
    giver, receiver = sizes[1:1 + 2 * couples:2], sizes[2:2 + 2 * couples:2]
    margin = jnp.minimum(giver - 1, limit - receiver)
    passed = jax.random.randint(jax.random.fold_in(rng, 1), (couples,), 0, 1 << 20) % (margin + 1)
    sizes = sizes.at[1:1 + 2 * couples:2].set(giver - passed).at[2:2 + 2 * couples:2].set(receiver + passed)
    return sizes[jax.random.permutation(jax.random.fold_in(rng, 2), count)]


def bell_draw(stream_key, shape, spread, limit, pieces=(), held_as=jnp.bfloat16):
    factor_of = block_levels(stream_key, shape, pieces, -0.22, 0.18) if pieces else 1.0
    entries = jax.random.normal(stream_key, shape, jnp.float32) * spread * factor_of
    return jnp.minimum(jnp.maximum(entries, -limit), limit).astype(held_as)


def setup_inputs(seed: int = 0) -> dict:
    seeds = jax.random.split(jax.random.key(seed), 17)
    return {
        "residual": bell_draw(seeds[0], (TOKENS, D), 1.0, 6.0, ((0, 8),)),
        "pre_gain": jnp.clip(1.0 + 0.1 * jax.random.normal(seeds[1], (D,), jnp.float32), 0.5, 1.5).astype(jnp.bfloat16),
        "query_weight": bell_draw(seeds[2], (D, HEADS * HEAD_DIM), D ** -0.5, 0.09375, ((0, 8), (1, 4))),
        "key_weight": bell_draw(seeds[3], (D, KV_HEADS * HEAD_DIM), D ** -0.5, 0.09375, ((0, 8), (1, 4))),
        "value_weight": bell_draw(seeds[4], (D, KV_HEADS * HEAD_DIM), D ** -0.5, 0.09375, ((0, 8), (1, 4))),
        "output_weight": draw_output_weight(jax.random.fold_in(seeds[16], 71), 0),
        "adapter_down": bell_draw(seeds[6], (D, 3 * ADAPTERS * RANK), D ** -0.5, 0.09375, ((0, 8), (1, 4))),
        "adapter_up_query": bell_draw(seeds[7], (ADAPTERS * RANK, HEADS * HEAD_DIM), RANK ** -0.5, 1.5, ((1, 4),)),
        "adapter_up_key": bell_draw(seeds[8], (ADAPTERS * RANK, KV_HEADS * HEAD_DIM), RANK ** -0.5, 1.5, ((1, 4),)),
        "adapter_up_value": bell_draw(seeds[9], (ADAPTERS * RANK, KV_HEADS * HEAD_DIM), RANK ** -0.5, 1.5, ((1, 4),)),
        "adapter_down_out": bell_draw(seeds[10], (HEADS * HEAD_DIM, ADAPTERS * RANK), (HEADS * HEAD_DIM) ** -0.5, 0.09375, ((0, 4),)),
        "adapter_up_out": bell_draw(seeds[11], (ADAPTERS * RANK, D), RANK ** -0.5, 1.5, ((1, 4),)),
        "post_gain": jnp.clip(1.0 + 0.1 * jax.random.normal(seeds[12], (D,), jnp.float32), 0.5, 1.5).astype(jnp.bfloat16),
        "sink_logits": draw_sink_logits(jax.random.fold_in(seeds[16], 71), 0),
        "prompt_lengths": ragged_sizes(seeds[14], PROMPTS, TOKENS, TOKENS // 2, 2).astype(jnp.int32),
        "prompt_adapters": plant(jax.random.randint(seeds[15], (PROMPTS,), 0, ADAPTERS), jax.random.fold_in(seeds[15], 1), 0, ADAPTERS - 1).astype(jnp.int32),
    }


epsilon = 1e-06
adapter_scale = 0.5
rotary_base = 10000.0
score_scale = 1.0 / 12.0

def token_layout(prompt_lengths, count, first):
    ends = jnp.cumsum(prompt_lengths, dtype=jnp.int32)
    starts = (ends - prompt_lengths).astype(jnp.int32)
    places = first + jnp.arange(count, dtype=jnp.int32)
    member = jnp.logical_and(places[:, None] >= starts[None, :], places[:, None] < ends[None, :]).astype(jnp.int32)
    labels = jnp.arange(prompt_lengths.shape[0], dtype=jnp.int32)
    prompt = lax.optimization_barrier(jnp.sum(member * labels[None, :], axis=1)).astype(jnp.int32)
    position = (places - lax.optimization_barrier(jnp.sum(member * starts[None, :], axis=1))).astype(jnp.int32)
    return (member, prompt, position)

def norm_factor(values):
    return lax.rsqrt(lax.optimization_barrier(jnp.mean(values * values, axis=-1, keepdims=True)) + epsilon)

def rotate(values, position):
    half = values.shape[-1] // 2
    exponent = jnp.arange(half, dtype=jnp.float32) * (2.0 / values.shape[-1])
    frequency = jnp.power(jnp.float32(rotary_base), -exponent)
    angle = position.astype(jnp.float32)[:, None] * frequency[None, :]
    cosine = jnp.cos(angle)[:, None, :]
    sine = jnp.sin(angle)[:, None, :]
    first_half = values[..., :half]
    second_half = values[..., half:]
    return jnp.concatenate([first_half * cosine - second_half * sine, second_half * cosine + first_half * sine], axis=-1)

def select_codes(codes, adapter, projections, adapters):
    count = codes.shape[0]
    width = codes.shape[1] // (adapters * projections)
    shaped = codes.reshape(count, adapters, projections, width)
    onehot = (adapter[:, None] == jnp.arange(adapters, dtype=jnp.int32)[None, :]).astype(codes.dtype)
    kept = shaped * onehot[:, :, None, None]
    return [kept[:, :, slot, :].reshape(count, adapters * width) for slot in range(projections)]

def reference(residual, pre_gain, query_weight, key_weight, value_weight, output_weight, adapter_down, adapter_up_query, adapter_up_key, adapter_up_value, adapter_down_out, adapter_up_out, post_gain, sink_logits, prompt_lengths, prompt_adapters):
    member, prompt, position = token_layout(prompt_lengths, TOKENS, jnp.int32(0))
    adapter = lax.optimization_barrier(jnp.sum(member * prompt_adapters[None, :], axis=1)).astype(jnp.int32)
    stream = residual.astype(jnp.float32)
    normed = (stream * norm_factor(stream) * pre_gain.astype(jnp.float32)[None, :]).astype(jnp.bfloat16)
    codes = jnp.dot(normed, adapter_down, preferred_element_type=jnp.float32).astype(jnp.bfloat16)
    chosen = select_codes(codes, adapter, 3, ADAPTERS)
    query = jnp.dot(normed, query_weight, preferred_element_type=jnp.float32) + adapter_scale * jnp.dot(chosen[0], adapter_up_query, preferred_element_type=jnp.float32)
    key = jnp.dot(normed, key_weight, preferred_element_type=jnp.float32) + adapter_scale * jnp.dot(chosen[1], adapter_up_key, preferred_element_type=jnp.float32)
    value = jnp.dot(normed, value_weight, preferred_element_type=jnp.float32) + adapter_scale * jnp.dot(chosen[2], adapter_up_value, preferred_element_type=jnp.float32)
    query = rotate(query.reshape(TOKENS, HEADS, HEAD_DIM), position).astype(jnp.bfloat16)
    keys = rotate(key.reshape(TOKENS, KV_HEADS, HEAD_DIM), position).astype(jnp.bfloat16)
    values = value.astype(jnp.bfloat16).reshape(TOKENS, KV_HEADS, HEAD_DIM)
    group = HEADS // KV_HEADS
    places = jnp.arange(TOKENS, dtype=jnp.int32)
    block = math.gcd(TOKENS, 1024)

    def one_head(head):
        head_query = lax.dynamic_index_in_dim(query, head, 1, keepdims=False)
        head_key = lax.dynamic_index_in_dim(keys, (head // group).astype(jnp.int32), 1, keepdims=False)
        head_value = lax.dynamic_index_in_dim(values, (head // group).astype(jnp.int32), 1, keepdims=False)
        sink = lax.dynamic_index_in_dim(sink_logits.astype(jnp.float32), head, 0, keepdims=False)

        def one_block(start):
            rows = lax.dynamic_slice_in_dim(head_query, start, block, 0)
            row_prompt = lax.dynamic_slice_in_dim(prompt, start, block, 0)
            row_place = lax.dynamic_slice_in_dim(places, start, block, 0)
            scores = jnp.dot(rows, head_key.T, preferred_element_type=jnp.float32) * score_scale
            allowed = jnp.logical_and(row_prompt[:, None] == prompt[None, :], row_place[:, None] >= places[None, :])
            scores = jnp.where(allowed, scores, -1e+30)
            top = jnp.maximum(lax.optimization_barrier(jnp.max(scores, axis=1)), sink)
            weights = jnp.where(allowed, jnp.exp(scores - top[:, None]), 0.0)
            total = lax.optimization_barrier(jnp.sum(weights, axis=1)) + jnp.exp(sink - top)
            mixed = jnp.dot(weights.astype(jnp.bfloat16), head_value, preferred_element_type=jnp.float32)
            return mixed / total[:, None]
        starts = jnp.arange(TOKENS // block, dtype=jnp.int32) * block
        return lax.map(one_block, starts).reshape(TOKENS, HEAD_DIM)
    heads_out = lax.map(one_head, jnp.arange(HEADS, dtype=jnp.int32))
    attended = jnp.transpose(heads_out, (1, 0, 2)).reshape(TOKENS, HEADS * HEAD_DIM).astype(jnp.bfloat16)
    codes_out = jnp.dot(attended, adapter_down_out, preferred_element_type=jnp.float32).astype(jnp.bfloat16)
    chosen_out = select_codes(codes_out, adapter, 1, ADAPTERS)[0]
    projected = jnp.dot(attended, output_weight, preferred_element_type=jnp.float32) + adapter_scale * jnp.dot(chosen_out, adapter_up_out, preferred_element_type=jnp.float32)
    mixed = stream + projected * norm_factor(projected) * post_gain.astype(jnp.float32)[None, :]
    return mixed.astype(jnp.bfloat16)
```

```python
import functools

import jax
import jax.numpy as jnp
from jax import lax
from jax.experimental import pallas as pl
from jax.experimental.pallas import tpu as pltpu
from jax.sharding import PartitionSpec as P

HEAD_DIM = 128
ADAPTERS = 16
RANK = 16

epsilon = 1e-06
adapter_scale = 0.5
rotary_base = 10000.0
score_scale = 1.0 / 12.0

CHIPS = 4
CHUNKS = 4
F32 = jnp.float32
BF16 = jnp.bfloat16
SMEM = pl.BlockSpec(memory_space=pltpu.SMEM)
VMEM = pl.BlockSpec(memory_space=pltpu.VMEM)
ANY = pl.BlockSpec(memory_space=pl.ANY)


def token_layout(prompt_lengths, count, first):
    ends = jnp.cumsum(prompt_lengths, dtype=jnp.int32)
    starts = ends - prompt_lengths
    places = first + jnp.arange(count, dtype=jnp.int32)
    member = jnp.logical_and(
        places[:, None] >= starts[None, :], places[:, None] < ends[None, :]
    ).astype(jnp.int32)
    labels = jnp.arange(prompt_lengths.shape[0], dtype=jnp.int32)
    prompt = jnp.sum(member * labels[None, :], axis=1)
    position = places - jnp.sum(member * starts[None, :], axis=1)
    return (member, prompt, position)


def params(flops, bytes_accessed, transcendentals=0):
    return dict(
        compiler_params=pltpu.CompilerParams(vmem_limit_bytes=48 * 1024 * 1024),
        cost_estimate=pl.CostEstimate(
            flops=flops, bytes_accessed=bytes_accessed, transcendentals=transcendentals
        ),
    )


def prompt_of(places, lengths_ref, prompts):
    end = jnp.int32(0)
    prompt = jnp.zeros_like(places)
    start = jnp.zeros_like(places)
    for p in range(prompts - 1):
        end = end + lengths_ref[p]
        past = places >= end
        prompt = jnp.where(past, p + 1, prompt)
        start = jnp.where(past, end, start)
    return prompt, start


def order(chip, core):
    return (chip ^ (1 + core), chip ^ 3, chip ^ (2 - core), chip)


def near(chip, core):
    return (chip, chip ^ (1 + core), chip ^ (2 - core), chip ^ 3)


def split_kernel(info_ref, x_ref, *refs):
    outs, sems = refs[:4], refs[4]
    chip = lax.shift_right_logical(info_ref[0], 1)
    depth = outs[0].shape[1]
    copies = []
    for delta in (1, 2, 3, 0):
        at = pl.multiple_of((chip ^ delta) * depth, 128)
        copies.append(
            pltpu.make_async_copy(x_ref.at[:, pl.ds(at, depth)], outs[delta], sems.at[delta])
        )
        copies[-1].start()
    for copy in copies:
        copy.wait()


def split(info, x):
    shape = jax.ShapeDtypeStruct((x.shape[0], x.shape[1] // CHIPS), x.dtype)
    return pl.pallas_call(
        split_kernel,
        out_shape=(shape,) * 4,
        in_specs=[SMEM, ANY],
        out_specs=(ANY,) * 4,
        scratch_shapes=[pltpu.SemaphoreType.DMA((4,))],
        name="split",
        **params(0, x.size * 4),
    )(info, x)


def columns_kernel(info_ref, q_ref, k_ref, v_ref, gain_ref, mine_ref, theirs_ref):
    chip = lax.shift_right_logical(info_ref[0], 1)
    own = info_ref[0] & 1
    d = HEAD_DIM
    gain = gain_ref[...]
    for core, out in ((1 - own, theirs_ref), (own, mine_ref)):
        for place, to in enumerate(order(chip, core)):
            q = q_ref[:, pl.ds(pl.multiple_of((2 * to + core) * d, d), d)]
            at = pl.ds(pl.multiple_of(to * d, d), d)
            kv = jnp.where(core == 0, k_ref[:, at], v_ref[:, at])
            out[:, 2 * place * d : (2 * place + 1) * d] = (q.astype(F32) * gain).astype(BF16)
            out[:, (2 * place + 1) * d : (2 * place + 2) * d] = (kv.astype(F32) * gain).astype(BF16)


def columns(info, q, k, v, gain):
    shape = jax.ShapeDtypeStruct(q.shape, BF16)
    return pl.pallas_call(
        columns_kernel,
        out_shape=(shape, shape),
        in_specs=[SMEM] + [VMEM] * 4,
        out_specs=(VMEM, VMEM),
        name="columns",
        **params(q.size * 4, q.size * 8),
    )(info, q, k, v, gain)


def adapters_kernel(prompts, info_ref, chosen_ref, down_ref, gain_ref, upq_ref, upk_ref, upv_ref, ado_ref, upo_ref, pack_ref, up_ref, out_ref):
    me, z = info_ref[0], info_ref[1]
    chip = lax.shift_right_logical(me, 1)
    core = me & 1
    d = HEAD_DIM
    n_codes = prompts * RANK
    local = down_ref.shape[1] // (3 * RANK)
    rows = down_ref.shape[0]

    shape = (3 * n_codes, down_ref.shape[1])
    row = lax.broadcasted_iota(jnp.int32, shape, 0)
    col = lax.broadcasted_iota(jnp.int32, shape, 1)
    prompt = (row % n_codes) // RANK
    adapter = jnp.zeros(shape, jnp.int32)
    for p in range(prompts):
        adapter = jnp.where(prompt == p, chosen_ref[p], adapter)
    wanted = (adapter - z * local) * (3 * RANK) + (row // n_codes) * RANK + row % RANK
    inside = jnp.logical_and(adapter >= z * local, adapter < (z + 1) * local)
    pick = jnp.where(jnp.logical_and(inside, col == wanted), 1.0, 0.0).astype(BF16)
    down = lax.dot_general(pick, down_ref[...], (((1,), (1,)), ((), ())), preferred_element_type=F32)
    pack_ref[: 3 * n_codes, :] = (down * gain_ref[...]).astype(BF16)

    def rows_of(p):
        return pl.ds(pl.multiple_of(chosen_ref[p] * RANK, RANK), RANK)

    for p in range(prompts):
        both = upo_ref[rows_of(p), :].astype(F32) * adapter_scale
        part = jnp.where(core == 0, both[:, :rows], both[:, rows:])
        at = 3 * n_codes + p * RANK
        pack_ref[at : at + RANK, :] = jnp.where(z == chip, part, 0.0).astype(BF16)

    up_ref[...] = jnp.zeros_like(up_ref)
    for p in range(prompts):
        for place, to in enumerate(order(chip, core)):
            q = upq_ref[rows_of(p), pl.ds(pl.multiple_of((2 * to + core) * d, d), d)].astype(F32)
            at = pl.ds(pl.multiple_of(to * d, d), d)
            k = upk_ref[rows_of(p), at].astype(F32)
            v = upv_ref[rows_of(p), at].astype(F32)
            kv = jnp.where(core == 0, k, v)
            up_ref[p * RANK : (p + 1) * RANK, 2 * place * d : (2 * place + 1) * d] = (q * adapter_scale).astype(BF16)
            up_ref[n_codes + p * RANK : n_codes + (p + 1) * RANK, (2 * place + 1) * d : (2 * place + 2) * d] = (
                kv * adapter_scale
            ).astype(BF16)

    shape = (n_codes, ado_ref.shape[1])
    row = lax.broadcasted_iota(jnp.int32, shape, 0)
    col = lax.broadcasted_iota(jnp.int32, shape, 1)
    adapter = jnp.zeros(shape, jnp.int32)
    for p in range(prompts):
        adapter = jnp.where(row // RANK == p, chosen_ref[p], adapter)
    pick = jnp.where(col == adapter * RANK + row % RANK, 1.0, 0.0).astype(BF16)
    for place, source in enumerate(near(chip, core)):
        block = ado_ref[pl.ds(pl.multiple_of((2 * source + core) * d, d), d), :]
        part = lax.dot_general(pick, block, (((1,), (1,)), ((), ())), preferred_element_type=F32)
        out_ref[:, place * d : (place + 1) * d] = part.astype(BF16)


def adapters(info, chosen, down, gain, upq, upk, upv, ado, upo):
    prompts = chosen.shape[0]
    n_codes = prompts * RANK
    return pl.pallas_call(
        functools.partial(adapters_kernel, prompts),
        out_shape=(
            jax.ShapeDtypeStruct((4 * n_codes, down.shape[0]), BF16),
            jax.ShapeDtypeStruct((2 * n_codes, upq.shape[1]), BF16),
            jax.ShapeDtypeStruct((n_codes, CHIPS * HEAD_DIM), BF16),
        ),
        in_specs=[SMEM, SMEM] + [VMEM] * 7,
        out_specs=(VMEM,) * 3,
        name="adapters",
        **params(down.size * 400, down.size * 10),
    )(info, chosen, down, gain, upq, upk, upv, ado, upo)


def parity_kernel(info_ref, w_ref, mine_ref, theirs_ref, sems):
    chip = lax.shift_right_logical(info_ref[0], 1)
    own = info_ref[0] & 1
    d = HEAD_DIM
    copies = []
    for core, out in ((1 - own, theirs_ref), (own, mine_ref)):
        for place, source in enumerate(near(chip, core)):
            at = pl.multiple_of((2 * source + core) * d, d)
            copies.append(
                pltpu.make_async_copy(
                    w_ref.at[pl.ds(at, d), :], out.at[pl.ds(place * d, d), :], sems.at[len(copies)]
                )
            )
            copies[-1].start()
    for copy in copies:
        copy.wait()


def parity(info, w):
    shape = jax.ShapeDtypeStruct((w.shape[0] // 2, w.shape[1]), w.dtype)
    return pl.pallas_call(
        parity_kernel,
        out_shape=(shape, shape),
        in_specs=[SMEM, ANY],
        out_specs=(ANY, ANY),
        scratch_shapes=[pltpu.SemaphoreType.DMA((8,))],
        name="parity",
        **params(0, w.size * 4),
    )(info, w)


def join_kernel(info_ref, mine_ref, other_ref, out_ref):
    core = info_ref[0] & 1
    mine, other = mine_ref[...].astype(F32), other_ref[...].astype(F32)
    left = jnp.where(core == 0, mine, other)
    right = jnp.where(core == 0, other, mine)
    out_ref[...] = jnp.concatenate([left, right], axis=1).astype(out_ref.dtype)


def join(info, mine, other):
    rows, cols = mine.shape
    return pl.pallas_call(
        join_kernel,
        out_shape=jax.ShapeDtypeStruct((rows, 2 * cols), mine.dtype),
        in_specs=[SMEM, VMEM, VMEM],
        out_specs=VMEM,
        name="join",
        **params(rows * cols * 4, rows * cols * 8),
    )(info, mine, other)


def project_kernel(blocks, first, prompts, info_ref, lengths_ref, *refs):
    x_refs = refs[:8]
    mine_ref, got_ref, pack_ref, b_ref, send_ref, keep_ref, x_ref, w_ref, sems = refs[8:]
    me = info_ref[0]
    core = me & 1
    tok = x_ref.shape[0] // blocks
    half = send_ref.shape[1]
    n_codes = prompts * RANK
    depth = mine_ref.shape[0]
    copies = [
        pltpu.make_async_copy(mine_ref, w_ref.at[pl.ds(pl.multiple_of(core * depth, 16), depth), :], sems.at[0]),
        pltpu.make_async_copy(got_ref, w_ref.at[pl.ds(pl.multiple_of((1 - core) * depth, 16), depth), :], sems.at[1]),
    ]
    for copy in copies:
        copy.start()
    for i in range(blocks):
        rel = me ^ (first + i)
        for k in range(8):

            @pl.when(rel == k)
            def _():
                pltpu.make_async_copy(x_refs[k], x_ref.at[pl.ds(i * tok, tok), :], sems.at[2 + i]).start()

    for i in range(blocks):
        pltpu.make_async_copy(x_refs[0], x_ref.at[pl.ds(i * tok, tok), :], sems.at[2 + i]).wait()
    x = x_ref[...]
    down = jnp.concatenate(
        [
            pack_ref[:n_codes, :],
            jnp.where(core == 0, pack_ref[n_codes : 2 * n_codes, :], pack_ref[2 * n_codes : 3 * n_codes, :]),
        ],
        axis=0,
    )
    codes = lax.dot_general(x, down, (((1,), (1,)), ((), ())), preferred_element_type=F32)
    rows = blocks * tok
    places = first * tok + lax.broadcasted_iota(jnp.int32, (rows, 1), 0)
    prompt, _ = prompt_of(places, lengths_ref, prompts)
    lane = lax.broadcasted_iota(jnp.int32, codes.shape, 1)
    owner = (lane % n_codes) // RANK
    codes = jnp.where(owner == prompt, codes, 0.0).astype(BF16)
    for copy in copies:
        copy.wait()
    for part, out in ((0, send_ref), (1, keep_ref)):
        cols = pl.ds(part * half, half)
        product = jnp.dot(x, w_ref[:, cols], preferred_element_type=F32)
        product = product + jnp.dot(codes, b_ref[:, cols], preferred_element_type=F32)
        out[...] = product.astype(out.dtype)


def project(info, lengths, pieces, mine, got, pack, up, chunk, blocks):
    tok, depth = pieces[0].shape
    cols = mine.shape[1]
    half = cols // 2
    rows = blocks * tok
    return pl.pallas_call(
        functools.partial(project_kernel, blocks, chunk * blocks, lengths.shape[0]),
        out_shape=(
            jax.ShapeDtypeStruct((rows, half), BF16),
            jax.ShapeDtypeStruct((rows, half), F32),
        ),
        in_specs=[SMEM, SMEM] + [ANY] * 10 + [VMEM] * 2,
        out_specs=(VMEM, VMEM),
        scratch_shapes=[
            pltpu.VMEM((rows, depth), BF16),
            pltpu.VMEM((depth, cols), BF16),
            pltpu.SemaphoreType.DMA((2 + blocks,)),
        ],
        name="project",
        **params(2 * rows * depth * cols, rows * depth * 2 + depth * cols * 2 + rows * half * 6),
    )(info, lengths, *pieces, mine, got, pack, up)


def finish_kernel(keep_ref, first_ref, second_ref, cos_ref, sin_ref, kcos_ref, ksin_ref, q_ref, kv_ref):
    d = q_ref.shape[1]
    own = keep_ref.shape[1] // 2
    total = keep_ref[:, own:] + first_ref[:, :own].astype(F32) + second_ref[...].astype(F32)
    q, kv = total[:, :d], total[:, d:]
    q_ref[...] = (q * cos_ref[...] + pltpu.roll(q, d // 2, 1) * sin_ref[...]).astype(BF16)
    kv_ref[...] = (kv * kcos_ref[...] + pltpu.roll(kv, d // 2, 1) * ksin_ref[...]).astype(BF16)


def finish(keep, first, second, tables, chunk):
    rows = keep.shape[0]
    shape = jax.ShapeDtypeStruct((rows, HEAD_DIM), BF16)
    whole = lambda a: pl.BlockSpec(a.shape, lambda i: (0, 0))
    table = pl.BlockSpec((rows, HEAD_DIM), lambda i: (chunk, 0))
    out = pl.BlockSpec((rows, HEAD_DIM), lambda i: (0, 0))
    return pl.pallas_call(
        finish_kernel,
        grid=(1,),
        out_shape=(shape, shape),
        in_specs=[whole(keep), whole(first), whole(second)] + [table] * 4,
        out_specs=(out, out),
        name="finish",
        **params(rows * 1024, rows * 4096),
    )(keep, first, second, *tables)


def attend_kernel(first, count, prompts, step, info_ref, lengths_ref, sink_ref, q_ref, *refs):
    mine_refs, other_refs = refs[:count], refs[count : 2 * count]
    outs = refs[2 * count : 2 * count + 4]
    k_ref, v_ref, out_ref = refs[2 * count + 4 :]
    rows, d = q_ref.shape
    here, z = info_ref[0], info_ref[1]
    core = here & 1
    for i in range(count):
        mine, other = mine_refs[i][...], other_refs[i][...]
        k_ref[i * rows : (i + 1) * rows, :] = jnp.where(core == 0, mine, other)
        v_ref[i * rows : (i + 1) * rows, :] = jnp.where(core == 0, other, mine)
    sink = sink_ref[here]
    for block in range(rows // step):
        base = first + block * step
        q = q_ref[pl.ds(block * step, step), :]
        places = base + lax.broadcasted_iota(jnp.int32, (step, 1), 0)
        _, starts = prompt_of(places, lengths_ref, prompts)
        end = jnp.int32(0)
        low = jnp.int32(0)
        for p in range(prompts - 1):
            end = end + lengths_ref[p]
            low = jnp.where(base >= end, end, low)

        def body(i, carry):
            top, total, summed = carry
            at = pl.multiple_of(i * step, step)
            k = k_ref[pl.ds(at, step), :]
            v = v_ref[pl.ds(at, step), :]
            scores = lax.dot_general(q, k, (((1,), (1,)), ((), ())), preferred_element_type=F32) * score_scale
            keys = at + lax.broadcasted_iota(jnp.int32, (step, step), 1)
            allowed = jnp.logical_and(keys >= starts, keys <= places)
            scores = jnp.where(allowed, scores, -1e30)
            fresh = jnp.maximum(top, jnp.max(scores, axis=1, keepdims=True))
            factor = jnp.exp(top - fresh)
            weights = jnp.exp(scores - fresh)
            total = total * factor + jnp.sum(weights, axis=1, keepdims=True)
            summed = summed * factor + jnp.dot(weights.astype(BF16), v, preferred_element_type=F32)
            return fresh, total, summed

        top = jnp.full((step, 1), sink, F32)
        total = jnp.ones((step, 1), F32)
        summed = jnp.zeros((step, d), F32)
        top, total, summed = lax.fori_loop(
            low // step, (first // step) + block + 1, body, (top, total, summed)
        )
        out_ref[...] = (summed / total).astype(BF16)
        part = step // 4
        for k in range(4):
            at = pl.multiple_of(((z + k) & 3) * part, part)
            outs[k][block * part : (block + 1) * part, :] = out_ref[pl.ds(at, part), :]


def attend(info, lengths, sinks, q, mine, other, first, step):
    rows, d = q.shape
    count = len(mine)
    return pl.pallas_call(
        functools.partial(attend_kernel, first, count, lengths.shape[0], step),
        out_shape=(jax.ShapeDtypeStruct((rows // 4, d), BF16),) * 4,
        in_specs=[SMEM, SMEM, SMEM] + [VMEM] * (1 + 2 * count),
        out_specs=(VMEM,) * 4,
        scratch_shapes=[pltpu.VMEM((count * rows, d), BF16)] * 2 + [pltpu.VMEM((step, d), BF16)],
        name="attend",
        **params(rows * 768 * 4 * d, rows * d * 4 + count * rows * d * 4, rows * 768),
    )(info, lengths, sinks, q, *mine, *other)


def output_kernel(prompts, info_ref, lengths_ref, *refs):
    blocks = refs[:4]
    weights = refs[4:8]
    downs = refs[8:12]
    pack_ref, keep_ref, send_ref, acc_ref = refs[12:]
    me, z = info_ref[0], info_ref[1]
    core = jnp.bitwise_and(me, 1)
    rows = acc_ref.shape[0]
    d = HEAD_DIM
    codes = None
    for k in range(4):
        a = jnp.concatenate([blocks[r][:, k * d : (k + 1) * d] for r in range(4)], axis=1)
        product = jnp.dot(a, weights[k][...], preferred_element_type=F32)
        terms = lax.dot_general(a, downs[k][...], (((1,), (1,)), ((), ())), preferred_element_type=F32)
        if k == 0:
            acc_ref[...] = product
            codes = terms
        else:
            acc_ref[...] += product
            codes = codes + terms
    part = keep_ref.shape[1]
    row = lax.broadcasted_iota(jnp.int32, (rows, 1), 0)
    places = (row // part) * (4 * part) + z * part + row % part
    prompt, _ = prompt_of(places, lengths_ref, prompts)
    lane = lax.broadcasted_iota(jnp.int32, codes.shape, 1)
    codes = jnp.where(lane // RANK == prompt, codes, 0.0).astype(BF16)
    up = pack_ref[3 * prompts * RANK :, :]
    acc_ref[...] += jnp.dot(codes, up, preferred_element_type=F32)
    for i in range(CHIPS):
        mine = pl.multiple_of(i * 2 * part + core * part, part)
        theirs = pl.multiple_of(i * 2 * part + (1 - core) * part, part)
        keep_ref[i] = acc_ref[pl.ds(mine, part), :]
        send_ref[i] = acc_ref[pl.ds(theirs, part), :].astype(BF16)


def output(info, lengths, blocks, weights, downs, up):
    rows = blocks[0].shape[0]
    cols = weights[0].shape[1]
    part = rows // 8
    return pl.pallas_call(
        functools.partial(output_kernel, lengths.shape[0]),
        out_shape=(
            jax.ShapeDtypeStruct((CHIPS, part, cols), F32),
            jax.ShapeDtypeStruct((CHIPS, part, cols), BF16),
        ),
        in_specs=[SMEM, SMEM] + [VMEM] * 13,
        out_specs=(VMEM, VMEM),
        scratch_shapes=[pltpu.VMEM((rows, cols), F32)],
        name="output",
        **params(2 * rows * 2048 * cols, 2048 * cols * 2 + rows * 2048 * 2 + rows * cols * 3),
    )(info, lengths, *blocks, *weights, *downs, up)


def close_kernel(info_ref, stream_ref, gain_ref, *refs):
    pieces = refs[:4]
    out_ref = refs[4]
    z = info_ref[1]
    part = pieces[0].shape[0]
    gain = gain_ref[...].astype(F32)
    for k in range(4):
        at = pl.multiple_of(jnp.bitwise_and(z - k + 4, 3) * part, part)
        rows = pl.ds(at, part)
        out_ref[rows, :] = (stream_ref[rows, :].astype(F32) + pieces[k][...].astype(F32) * gain).astype(BF16)


def close(info, stream, gain, pieces):
    return pl.pallas_call(
        close_kernel,
        out_shape=jax.ShapeDtypeStruct(stream.shape, BF16),
        in_specs=[SMEM] + [VMEM] * 6,
        out_specs=VMEM,
        name="close",
        **params(stream.size * 3, stream.size * 6),
    )(info, stream, gain[None, :], *pieces)


def per_device_heads(
    residual,
    pre_gain,
    query_weight,
    key_weight,
    value_weight,
    output_weight,
    adapter_down,
    adapter_up_query,
    adapter_up_key,
    adapter_up_value,
    adapter_down_out,
    adapter_up_out,
    post_gain,
    sink_logits,
    prompt_lengths,
    prompt_adapters,
):
    tok, features = residual.shape
    depth = features // CHIPS
    own_rows = query_weight.shape[0]
    prompts = prompt_lengths.shape[0]
    d = HEAD_DIM
    me = lax.axis_index("wide")
    z = lax.axis_index("narrow")
    core = me & 1
    chip = me >> 1
    info = jnp.stack([me, z]).astype(jnp.int32)
    wide = 2 * CHIPS
    tokens = tok * wide

    flip = lambda bits: [(i, i ^ bits) for i in range(wide)]
    across = flip(1)
    first_leg = [(i, i ^ (2 if i % 2 == 0 else 4)) for i in range(wide)]
    second_leg = [(i, i ^ (4 if i % 2 == 0 else 2)) for i in range(wide)]
    shift = lambda k: [(i, (i + k) % 4) for i in range(4)]
    zflip = lambda bits: [(i, i ^ bits) for i in range(4)]

    pieces = split(info, residual)
    pieces = [pieces[0]] + [lax.ppermute(pieces[delta], "wide", flip(2 * delta)) for delta in (1, 2, 3)]
    x_refs = []
    for piece in pieces:
        x_refs += [piece, lax.ppermute(piece, "wide", across)]

    own_gain = lax.dynamic_slice(pre_gain, (me * own_rows,), (own_rows,)).astype(F32)
    pack, up, out_down = adapters(
        info, prompt_adapters, adapter_down, own_gain[None, :], adapter_up_query, adapter_up_key,
        adapter_up_value, adapter_down_out, adapter_up_out,
    )
    pack = pack + lax.ppermute(pack, "narrow", zflip(1))
    pack = pack + lax.ppermute(pack, "narrow", zflip(2))
    pack = join(info, pack, lax.ppermute(pack, "wide", across))

    w_mine, w_theirs = columns(info, query_weight, key_weight, value_weight, own_gain[:, None])
    w_got = lax.ppermute(w_theirs, "wide", across)

    ow_mine, ow_theirs = parity(info, output_weight)
    out_weights = [join(info, ow_mine, lax.ppermute(ow_theirs, "wide", across))]
    for _ in range(3):
        out_weights.append(lax.ppermute(out_weights[-1], "narrow", shift(1)))
    out_downs = [out_down] + [lax.ppermute(out_down, "narrow", shift(k)) for k in (1, 2, 3)]

    stream = residual.astype(F32)
    factor = lax.rsqrt(jnp.mean(stream * stream, axis=1) + epsilon)
    factors = jnp.where(
        jnp.arange(wide, dtype=jnp.int32)[:, None] == me, factor[None, :], 0.0
    )
    for bits in (1, 2, 4):
        factors = factors + lax.ppermute(factors, "wide", flip(bits))
    factors = factors.reshape(tokens)[:, None]
    _, _, position = token_layout(prompt_lengths, tokens, jnp.int32(0))
    half = d // 2
    exponent = jnp.arange(half, dtype=F32) * (2.0 / d)
    frequency = jnp.power(jnp.float32(rotary_base), -exponent)
    angle = position.astype(F32)[:, None] * frequency[None, :]
    cosine, sine = jnp.cos(angle) * factors, jnp.sin(angle) * factors
    q_cos = jnp.concatenate([cosine, cosine], axis=1)
    q_sin = jnp.concatenate([-sine, sine], axis=1)
    kv_cos = jnp.where(core == 0, q_cos, factors)
    kv_sin = jnp.where(core == 0, q_sin, 0.0)

    blocks = wide // CHUNKS
    rows = blocks * tok
    mine, other = [], []
    near_blocks = [[] for _ in range(4)]
    tables = (q_cos, q_sin, kv_cos, kv_sin)
    for chunk in range(CHUNKS):
        send, keep = project(info, prompt_lengths, x_refs, w_mine, w_got, pack, up, chunk, blocks)
        one = lax.ppermute(send, "wide", first_leg)
        own = keep.shape[1] // 2
        onward = (keep[:, :own] + one[:, own:].astype(F32)).astype(BF16)
        two = lax.ppermute(onward, "wide", second_leg)
        q, kv = finish(keep, one, two, tables, chunk)
        mine.append(kv)
        other.append(lax.ppermute(kv, "wide", across))
        sub = attend(info, prompt_lengths, sink_logits, q, mine, other, chunk * rows, tok)
        got = [sub[0]] + [lax.ppermute(sub[k], "narrow", shift(k)) for k in (1, 2, 3)]
        near0 = jnp.concatenate(got, axis=1)
        near1 = lax.ppermute(near0, "wide", first_leg)
        near23 = lax.ppermute(jnp.stack([near0, near1]), "wide", second_leg)
        for r, block in enumerate((near0, near1, near23[0], near23[1])):
            near_blocks[r].append(block)
    gathered = [jnp.concatenate(b, axis=0) for b in near_blocks]

    kept, sent = output(info, prompt_lengths, gathered, out_weights, out_downs, pack)
    total = (kept + lax.ppermute(sent, "wide", across).astype(F32)).astype(BF16)
    rows_of = lambda to: lax.dynamic_index_in_dim(total, to, 0, keepdims=False)
    full = [rows_of(chip)] + [
        lax.ppermute(rows_of(chip ^ delta), "wide", flip(2 * delta)) for delta in (1, 2, 3)
    ]
    full = jnp.stack(full)
    wide_rows = full.astype(F32)
    mean_square = jnp.sum(wide_rows * wide_rows, axis=(0, 2)) / features
    scaled = (wide_rows * lax.rsqrt(mean_square + epsilon)[None, :, None]).astype(BF16)
    finals = []
    for k in range(4):
        piece = lax.dynamic_index_in_dim(scaled, chip ^ ((z + k) & 3), 0, keepdims=False)
        finals.append(piece if k == 0 else lax.ppermute(piece, "narrow", shift(k)))
    own_width = post_gain.shape[0]
    own_stream = lax.dynamic_slice_in_dim(residual, z * own_width, own_width, 1)
    return close(info, own_stream, post_gain, finals)
def rotate(values, position):
    half = values.shape[-1] // 2
    exponent = jnp.arange(half, dtype=jnp.float32) * (2.0 / values.shape[-1])
    frequency = jnp.power(jnp.float32(rotary_base), -exponent)
    angle = position.astype(jnp.float32)[:, None] * frequency[None, :]
    cosine = jnp.cos(angle)[:, None, :]
    sine = jnp.sin(angle)[:, None, :]
    first_half = values[..., :half]
    second_half = values[..., half:]
    return jnp.concatenate(
        [first_half * cosine - second_half * sine, second_half * cosine + first_half * sine],
        axis=-1,
    )


def select_codes(codes, adapter, projections, adapters):
    count = codes.shape[0]
    width = codes.shape[1] // (adapters * projections)
    shaped = codes.reshape(count, adapters, projections, width)
    onehot = (adapter[:, None] == jnp.arange(adapters, dtype=jnp.int32)[None, :]).astype(
        codes.dtype
    )
    kept = shaped * onehot[:, :, None, None]
    return [kept[:, :, slot, :].reshape(count, adapters * width) for slot in range(projections)]


def add_adapter(partial_out, adapter_cols, offset, own_width):
    current = lax.dynamic_slice_in_dim(partial_out, offset, own_width, 1)
    return lax.dynamic_update_slice_in_dim(partial_out, current + adapter_cols, offset, 1)


def per_device(
    residual,
    pre_gain,
    query_weight,
    key_weight,
    value_weight,
    output_weight,
    adapter_down,
    adapter_up_query,
    adapter_up_key,
    adapter_up_value,
    adapter_down_out,
    adapter_up_out,
    post_gain,
    sink_logits,
    prompt_lengths,
    prompt_adapters,
):
    tok_rows = residual.shape[0]
    first = lax.axis_index("wide") * tok_rows
    member, prompt, position = token_layout(prompt_lengths, tok_rows, first)
    adapter = jnp.sum(member * prompt_adapters[None, :], axis=1)
    stream = residual.astype(jnp.float32)
    scale_rows = lax.rsqrt(jnp.mean(stream * stream, axis=1, keepdims=True) + epsilon)
    normed = (stream * scale_rows * pre_gain.astype(jnp.float32)[None, :]).astype(jnp.bfloat16)
    query_cols = query_weight.shape[1]
    key_cols = key_weight.shape[1]
    pieces = (
        lax.all_gather(query_weight, "wide", axis=0, tiled=True),
        lax.all_gather(key_weight, "wide", axis=0, tiled=True),
        lax.all_gather(value_weight, "wide", axis=0, tiled=True),
        lax.all_gather(adapter_down, "wide", axis=0, tiled=True),
    )
    query_part, key_part, value_part, code_part = tuple(
        (jnp.dot(normed, piece, preferred_element_type=jnp.float32) for piece in pieces)
    )
    codes = lax.all_gather(code_part.astype(jnp.bfloat16), "narrow", axis=1, tiled=True)
    chosen = select_codes(codes, adapter, 3, ADAPTERS)
    query = query_part + adapter_scale * jnp.dot(
        chosen[0], adapter_up_query, preferred_element_type=jnp.float32
    )
    key = key_part + adapter_scale * jnp.dot(
        chosen[1], adapter_up_key, preferred_element_type=jnp.float32
    )
    value = value_part + adapter_scale * jnp.dot(
        chosen[2], adapter_up_value, preferred_element_type=jnp.float32
    )
    local_heads = query_cols // HEAD_DIM
    local_kv = key_cols // HEAD_DIM
    group = local_heads // local_kv
    queries = (
        rotate(query.reshape(tok_rows, local_heads, HEAD_DIM), position)
        .astype(jnp.bfloat16)
        .reshape(tok_rows, local_kv, group, HEAD_DIM)
    )
    keys = rotate(key.reshape(tok_rows, local_kv, HEAD_DIM), position).astype(jnp.bfloat16)
    values = value.astype(jnp.bfloat16).reshape(tok_rows, local_kv, HEAD_DIM)
    sinks = sink_logits.reshape(local_kv, group)
    own_places = first + jnp.arange(tok_rows, dtype=jnp.int32)
    start_top = jnp.broadcast_to(sinks[None, :, :], (tok_rows, local_kv, group))
    start_total = jnp.ones((tok_rows, local_kv, group), jnp.float32)
    start_sum = jnp.zeros((tok_rows, local_kv, group, HEAD_DIM), jnp.float32)
    top = start_top
    total = start_total
    summed_values = start_sum
    piece_keys = lax.all_gather(keys, "wide", axis=0, tiled=True)
    piece_values = lax.all_gather(values, "wide", axis=0, tiled=True)
    count = piece_keys.shape[0]
    unused, key_prompt, unused_position = token_layout(prompt_lengths, count, jnp.int32(0))
    key_places = jnp.arange(count, dtype=jnp.int32)
    allowed = jnp.logical_and(
        prompt[:, None] == key_prompt[None, :], own_places[:, None] >= key_places[None, :]
    )[:, None, None, :]
    scores = (
        jnp.einsum("qgjd,kgd->qgjk", queries, piece_keys, preferred_element_type=jnp.float32)
        * score_scale
    )
    scores = jnp.where(allowed, scores, -1e30)
    fresh = jnp.maximum(top, jnp.max(scores, axis=-1))
    factor = jnp.exp(top - fresh)
    weights = jnp.where(allowed, jnp.exp(scores - fresh[..., None]), 0.0)
    total = total * factor + jnp.sum(weights, axis=-1)
    update = jnp.einsum(
        "qgjk,kgd->qgjd",
        weights.astype(jnp.bfloat16),
        piece_values,
        preferred_element_type=jnp.float32,
    )
    top, total, summed_values = (fresh, total, summed_values * factor[..., None] + update)
    attended = (
        (summed_values / total[..., None])
        .reshape(tok_rows, local_heads * HEAD_DIM)
        .astype(jnp.bfloat16)
    )
    code_terms = jnp.dot(attended, adapter_down_out, preferred_element_type=jnp.float32)
    codes_out = lax.psum(code_terms.astype(jnp.bfloat16), "narrow")
    chosen_out = select_codes(codes_out, adapter, 1, ADAPTERS)[0]
    adapter_cols = adapter_scale * jnp.dot(
        chosen_out, adapter_up_out, preferred_element_type=jnp.float32
    )
    own_width = adapter_up_out.shape[1]
    offset = lax.axis_index("narrow") * own_width
    partial_out = jnp.dot(
        attended,
        lax.all_gather(output_weight, "wide", axis=1, tiled=True),
        preferred_element_type=jnp.float32,
    )
    partial_out = add_adapter(partial_out, adapter_cols, offset, own_width)
    whole = lax.psum(partial_out.astype(jnp.bfloat16), "narrow").astype(jnp.float32)
    mean_square = jnp.mean(whole * whole, axis=1)
    projected = lax.dynamic_slice_in_dim(whole, offset, own_width, 1)
    factor_rows = lax.rsqrt(mean_square + epsilon)
    own_stream = lax.dynamic_slice_in_dim(stream, offset, own_width, 1)
    mixed = own_stream + projected * factor_rows[:, None] * post_gain.astype(jnp.float32)[None, :]
    return mixed.astype(jnp.bfloat16)


def fits(mesh):
    return mesh.shape["wide"] == 2 * CHIPS and mesh.shape["narrow"] == 4


def solution(mesh):
    return jax.shard_map(
        per_device_heads if fits(mesh) else per_device,
        mesh=mesh,
        in_specs=(
            P("wide", None),
            P(),
            P("wide", "narrow"),
            P("wide", "narrow"),
            P("wide", "narrow"),
            P("narrow", "wide"),
            P("wide", "narrow"),
            P(None, "narrow"),
            P(None, "narrow"),
            P(None, "narrow"),
            P("narrow", None),
            P(None, "narrow"),
            P("narrow"),
            P("narrow"),
            P(),
            P(),
        ),
        out_specs=P("wide", "narrow"),
        check_vma=False,
    )
```

```python
import functools

import jax
import jax.numpy as jnp
from jax import lax
from jax.experimental import pallas as pl
from jax.experimental.pallas import tpu as pltpu
from jax.sharding import PartitionSpec as P

HEAD_DIM = 128
ADAPTERS = 16
RANK = 16

epsilon = 1e-06
adapter_scale = 0.5
rotary_base = 10000.0
score_scale = 1.0 / 12.0

CHIPS = 4
CHUNKS = 4
F32 = jnp.float32
BF16 = jnp.bfloat16
SMEM = pl.BlockSpec(memory_space=pltpu.SMEM)
VMEM = pl.BlockSpec(memory_space=pltpu.VMEM)
ANY = pl.BlockSpec(memory_space=pl.ANY)
HBM = pl.BlockSpec(memory_space=pltpu.HBM)


def token_layout(prompt_lengths, count, first):
    ends = jnp.cumsum(prompt_lengths, dtype=jnp.int32)
    starts = ends - prompt_lengths
    places = first + jnp.arange(count, dtype=jnp.int32)
    member = jnp.logical_and(
        places[:, None] >= starts[None, :], places[:, None] < ends[None, :]
    ).astype(jnp.int32)
    labels = jnp.arange(prompt_lengths.shape[0], dtype=jnp.int32)
    prompt = jnp.sum(member * labels[None, :], axis=1)
    position = places - jnp.sum(member * starts[None, :], axis=1)
    return (member, prompt, position)


def call(kernel, operands, specs, out_shape, after=(), scratch=(), name=None, flops=0, moved=0, transcendentals=0, grant=24, **more):
    n = len(after)
    return pl.pallas_call(
        lambda *refs: kernel(*refs[n:]),
        out_shape=out_shape,
        in_specs=[ANY] * n + list(specs),
        scratch_shapes=list(scratch),
        name=name,
        compiler_params=pltpu.CompilerParams(vmem_limit_bytes=grant * 1024 * 1024),
        cost_estimate=pl.CostEstimate(flops=flops // 64, bytes_accessed=moved // 64, transcendentals=transcendentals // 64),
        **more,
    )(*after, *operands)


def prompt_of(places, lengths_ref, prompts):
    end = jnp.int32(0)
    prompt = jnp.zeros_like(places)
    start = jnp.zeros_like(places)
    for p in range(prompts - 1):
        end = end + lengths_ref[p]
        past = places >= end
        prompt = jnp.where(past, p + 1, prompt)
        start = jnp.where(past, end, start)
    return prompt, start


def order(chip, core):
    return (chip ^ (1 + core), chip ^ 3, chip ^ (2 - core), chip)


NEXT = (1, 3, 0, 2)
BEFORE = (2, 0, 3, 1)


def plane(table, z):
    return jnp.where(z == 0, table[0], jnp.where(z == 1, table[1], jnp.where(z == 2, table[2], table[3])))


def near(chip, core):
    return (chip, chip ^ (1 + core), chip ^ (2 - core), chip ^ 3)


def norm_kernel(steps, x_hbm, gain_ref, *refs):
    outs, (x_ref, y_ref, sems) = refs[:4], refs[4:]
    chip = lax.shift_right_logical(lax.axis_index("wide"), 1)
    depth = outs[0].shape[1]
    step = x_ref.shape[0] // steps
    copies = [
        pltpu.make_async_copy(x_hbm.at[pl.ds(i * step, step), :], x_ref.at[pl.ds(i * step, step), :], sems.at[i])
        for i in range(steps)
    ]
    for copy in copies:
        copy.start()
    gain = gain_ref[...].astype(F32)
    for i in range(steps):
        copies[i].wait()
        rows = slice(i * step, (i + 1) * step)
        x = x_ref[rows, :].astype(F32)
        scale = lax.rsqrt(jnp.sum(x * x, axis=1, keepdims=True) / x.shape[1] + epsilon)
        y_ref[...] = (x * scale * gain).astype(BF16)
        for delta in range(4):
            outs[delta][rows, :] = y_ref[:, pl.ds(pl.multiple_of((chip ^ delta) * depth, 128), depth)]


def norm(x, gain, steps, after):
    rows, cols = x.shape
    shape = jax.ShapeDtypeStruct((rows, cols // CHIPS), x.dtype)
    return call(
        functools.partial(norm_kernel, steps), (x, gain[None, :]), [HBM, VMEM], (shape,) * 4, after,
        scratch=[
            pltpu.VMEM((rows, cols), BF16),
            pltpu.VMEM((rows // steps, cols), BF16),
            pltpu.SemaphoreType.DMA((steps,)),
        ],
        out_specs=(VMEM,) * 4, name="norm", grant=60, flops=x.size * 4, moved=x.size * 4,
    )


def arrange_kernel(q_ref, k_ref, v_ref, o_ref, mine_ref, theirs_ref, sems):
    chip = lax.shift_right_logical(lax.axis_index("wide"), 1)
    own = lax.axis_index("wide") & 1
    d = HEAD_DIM
    copies = []

    def copy(ref, at, out, to, width):
        source = ref.at[:, pl.ds(pl.multiple_of(at, d), width)]
        copies.append(pltpu.make_async_copy(source, out.at[:, pl.ds(to, width)], sems.at[len(copies)]))
        copies[-1].start()

    for core, out in ((1 - own, theirs_ref), (own, mine_ref)):
        for place, to in enumerate(order(chip, core)):
            for ref, width, at in ((q_ref, 2 * d, 0), (k_ref, d, 2 * d), (v_ref, d, 3 * d)):
                copy(ref, to * width, out, 4 * place * d + at, width)
        for place, source in enumerate(near(chip, core)):
            copy(o_ref, (2 * source + core) * d, out, (4 * CHIPS + place) * d, d)
    for one in copies:
        one.wait()


def arrange(q, k, v, o, after):
    shape = jax.ShapeDtypeStruct((q.shape[0], 5 * CHIPS * HEAD_DIM), BF16)
    return call(
        arrange_kernel, (q, k, v, o), [ANY] * 4, (shape, shape), after,
        scratch=[pltpu.SemaphoreType.DMA((32,))], out_specs=(ANY, ANY), name="arrange", moved=q.size * 16,
    )


def choose(shape, row_prompt, chosen_ref, prompts):
    adapter = jnp.zeros(shape, jnp.int32)
    for p in range(prompts):
        adapter = jnp.where(row_prompt == p, chosen_ref[p], adapter)
    return adapter


def pick_kernel(prompts, chosen_ref, down_hbm, upo_hbm, pack_ref, down_ref, upo_ref, sems):
    me, z = lax.axis_index("wide"), lax.axis_index("narrow")
    chip = lax.shift_right_logical(me, 1)
    core = me & 1
    n_codes = prompts * RANK
    local = down_ref.shape[0] // (3 * RANK)
    rows = down_ref.shape[1]
    copies = [pltpu.make_async_copy(down_hbm, down_ref, sems.at[prompts])]
    for p in range(prompts):
        at = pl.ds(pl.multiple_of(chosen_ref[p] * RANK, RANK), RANK)
        copies.append(pltpu.make_async_copy(upo_hbm.at[at, :], upo_ref.at[pl.ds(p * RANK, RANK), :], sems.at[p]))
    for copy in copies:
        copy.start()
    shape = (3 * n_codes, down_ref.shape[0])
    row = lax.broadcasted_iota(jnp.int32, shape, 0)
    col = lax.broadcasted_iota(jnp.int32, shape, 1)
    adapter = choose(shape, (row % n_codes) // RANK, chosen_ref, prompts)
    wanted = (adapter - z * local) * (3 * RANK) + (row // n_codes) * RANK + row % RANK
    inside = jnp.logical_and(adapter >= z * local, adapter < (z + 1) * local)
    pick = jnp.where(jnp.logical_and(inside, col == wanted), 1.0, 0.0).astype(BF16)
    for copy in copies:
        copy.wait()
    down = jnp.dot(pick, down_ref[...], preferred_element_type=F32)
    pack_ref[: 3 * n_codes, :] = down.astype(BF16)
    both = upo_ref[...].astype(F32) * adapter_scale
    part = jnp.where(core == 0, both[:, :rows], both[:, rows:])
    pack_ref[3 * n_codes :, :] = jnp.where(z == chip, part, 0.0).astype(BF16)


def pick(chosen, down, upo, after):
    prompts = chosen.shape[0]
    n_codes = prompts * RANK
    return call(
        functools.partial(pick_kernel, prompts), (chosen, down, upo), [SMEM, HBM, HBM],
        jax.ShapeDtypeStruct((4 * n_codes, down.shape[1]), BF16),
        after,
        scratch=[
            pltpu.VMEM(down.shape, BF16),
            pltpu.VMEM((n_codes, upo.shape[1]), BF16),
            pltpu.SemaphoreType.DMA((prompts + 1,)),
        ],
        out_specs=VMEM, name="pick", grant=60, flops=down.size * 400, moved=down.size * 6,
    )


def merge_kernel(a_ref, b_ref, out_ref):
    out_ref[...] = (a_ref[...].astype(F32) + b_ref[...].astype(F32)).astype(out_ref.dtype)


def merge(a, b, after=()):
    return call(
        merge_kernel, (a, b), [VMEM, VMEM], jax.ShapeDtypeStruct(a.shape, BF16), after,
        out_specs=VMEM, name="merge", flops=a.size, moved=a.size * 6,
    )


def ups_kernel(prompts, chosen_ref, upq_ref, upk_ref, upv_ref, ado_ref, up_ref, out_ref):
    me = lax.axis_index("wide")
    chip = lax.shift_right_logical(me, 1)
    core = me & 1
    d = HEAD_DIM
    n_codes = prompts * RANK
    up_ref[...] = jnp.zeros_like(up_ref)
    for p in range(prompts):
        rows = pl.ds(pl.multiple_of(chosen_ref[p] * RANK, RANK), RANK)
        for place, to in enumerate(order(chip, core)):
            for slot, (ref, width, at) in enumerate(((upq_ref, 2 * d, 0), (upk_ref, d, 2 * d), (upv_ref, d, 3 * d))):
                part = ref[rows, pl.ds(pl.multiple_of(to * width, d), width)].astype(F32) * adapter_scale
                first = slot * n_codes + p * RANK
                left = 4 * place * d + at
                up_ref[first : first + RANK, left : left + width] = part.astype(BF16)
    shape = (n_codes, ado_ref.shape[1])
    row = lax.broadcasted_iota(jnp.int32, shape, 0)
    col = lax.broadcasted_iota(jnp.int32, shape, 1)
    adapter = choose(shape, row // RANK, chosen_ref, prompts)
    pick = jnp.where(col == adapter * RANK + row % RANK, 1.0, 0.0).astype(BF16)
    for place, source in enumerate(near(chip, core)):
        block = ado_ref[pl.ds(pl.multiple_of((2 * source + core) * d, d), d), :]
        part = lax.dot_general(pick, block, (((1,), (1,)), ((), ())), preferred_element_type=F32)
        out_ref[:, place * d : (place + 1) * d] = part.astype(BF16)


def ups(chosen, upq, upk, upv, ado, after):
    prompts = chosen.shape[0]
    n_codes = prompts * RANK
    return call(
        functools.partial(ups_kernel, prompts), (chosen, upq, upk, upv, ado), [SMEM] + [VMEM] * 4,
        (
            jax.ShapeDtypeStruct((3 * n_codes, 2 * upq.shape[1]), BF16),
            jax.ShapeDtypeStruct((n_codes, CHIPS * HEAD_DIM), BF16),
        ),
        after, out_specs=(VMEM,) * 2, name="ups", flops=upq.size * 100, moved=upq.size * 6,
    )


def stack_kernel(mine_ref, got_ref, down_ref, w_ref, ring_ref, sems):
    core = lax.axis_index("wide") & 1
    rows = mine_ref.shape[0]
    cols = w_ref.shape[1]
    width = ring_ref.shape[1]
    copies = []
    for i, (ref, at) in enumerate(((mine_ref, core), (got_ref, 1 - core))):
        to = pl.ds(pl.multiple_of(at * rows, 16), rows)
        copies.append(pltpu.make_async_copy(ref.at[:, pl.ds(cols, width)], ring_ref.at[to, :], sems.at[2 * i]))
        copies.append(pltpu.make_async_copy(ref.at[:, pl.ds(0, cols)], w_ref.at[to, :], sems.at[2 * i + 1]))
    copies.append(pltpu.make_async_copy(down_ref, ring_ref.at[pl.ds(2 * rows, down_ref.shape[0]), :], sems.at[4]))
    for copy in copies:
        copy.start()
    for copy in copies:
        copy.wait()


def stack(mine, got, down, after):
    rows, cols = mine.shape
    width = down.shape[1]
    return call(
        stack_kernel, (mine, got, down), [ANY] * 3,
        (
            jax.ShapeDtypeStruct((2 * rows, cols - width), mine.dtype),
            jax.ShapeDtypeStruct((2 * rows + down.shape[0], width), mine.dtype),
        ),
        after,
        scratch=[pltpu.SemaphoreType.DMA((5,))], out_specs=(ANY, ANY), name="stack", moved=rows * cols * 8,
    )


def join_kernel(mine_ref, other_ref, out_ref):
    core = lax.axis_index("wide") & 1
    mine, other = mine_ref[...].astype(F32), other_ref[...].astype(F32)
    left = jnp.where(core == 0, mine, other)
    right = jnp.where(core == 0, other, mine)
    out_ref[...] = jnp.concatenate([left, right], axis=1).astype(out_ref.dtype)


def join(mine, other):
    rows, cols = mine.shape
    return call(
        join_kernel, (mine, other), [VMEM, VMEM], jax.ShapeDtypeStruct((rows, 2 * cols), mine.dtype),
        out_specs=VMEM, name="join", flops=rows * cols * 4, moved=rows * cols * 8,
    )


def project_kernel(chunk, prompts, lengths_ref, *refs):
    x_refs = refs[:4]
    w_ref, pack_ref, up_ref = refs[4:7]
    send_ref, keep_ref, x_ref, sem = refs[-4:]
    me = lax.axis_index("wide")
    chip = lax.shift_right_logical(me, 1)
    core = me & 1
    rows = x_ref.shape[0]
    half = send_ref.shape[1]
    n_codes = prompts * RANK
    for k in range(4):

        @pl.when((chip ^ chunk) == k)
        def _():
            pltpu.make_async_copy(x_refs[k], x_ref, sem).start()

    pltpu.make_async_copy(x_refs[0], x_ref, sem).wait()
    x = x_ref[...]
    codes = lax.dot_general(
        x, pack_ref[: 3 * n_codes, :], (((1,), (1,)), ((), ())), preferred_element_type=F32
    )
    places = (2 * chunk + core) * rows + lax.broadcasted_iota(jnp.int32, (rows, 1), 0)
    prompt, _ = prompt_of(places, lengths_ref, prompts)
    lane = lax.broadcasted_iota(jnp.int32, codes.shape, 1)
    owner = (lane % n_codes) // RANK
    codes = jnp.where(owner == prompt, codes, 0.0).astype(BF16)
    for part, out in ((0, send_ref), (1, keep_ref)):
        cols = pl.ds(part * half, half)
        product = jnp.dot(x, w_ref[:, cols], preferred_element_type=F32)
        product = product + jnp.dot(codes, up_ref[:, cols], preferred_element_type=F32)
        out[...] = product.astype(out.dtype)


def project(lengths, pieces, w, pack, up, chunk, after, carry=()):
    rows, depth = pieces[0].shape
    half = w.shape[1] // 2
    n = len(after) + 8
    out = call(
        functools.partial(project_kernel, chunk, lengths.shape[0]),
        (lengths, *pieces, w, pack, up, *carry),
        [SMEM] + [ANY] * 4 + [VMEM] * 3 + [ANY] * len(carry),
        tuple(jax.ShapeDtypeStruct(c.shape, c.dtype) for c in carry)
        + (jax.ShapeDtypeStruct((rows, half), BF16), jax.ShapeDtypeStruct((rows, half), F32)),
        after,
        scratch=[pltpu.VMEM((rows, depth), BF16), pltpu.SemaphoreType.DMA(())],
        out_specs=(ANY,) * len(carry) + (VMEM, VMEM), name="project",
        input_output_aliases={n + i: i for i in range(len(carry))},
        flops=2 * rows * depth * w.shape[1], moved=rows * depth * 2 + w.size * 2 + rows * half * 6,
    )
    return out[-2], out[-1], out[:-2]


def onward_kernel(keep_ref, first_ref, *refs):
    out_ref = refs[-1]
    own = out_ref.shape[1]
    out_ref[...] = (keep_ref[:, :own] + first_ref[:, own:].astype(F32)).astype(BF16)


def onward(keep, first, after, carry=()):
    rows, cols = keep.shape
    n = len(after) + 2
    out = call(
        onward_kernel, (keep, first, *carry), [VMEM, VMEM] + [ANY] * len(carry),
        tuple(jax.ShapeDtypeStruct(c.shape, c.dtype) for c in carry)
        + (jax.ShapeDtypeStruct((rows, cols // 2), BF16),),
        after, out_specs=(ANY,) * len(carry) + (VMEM,), name="onward",
        input_output_aliases={n + i: i for i in range(len(carry))},
        flops=rows * cols, moved=rows * cols * 4,
    )
    return out[-1], out[:-1]


def finish_kernel(chunk, keep_ref, first_ref, second_ref, cos_ref, sin_ref, own_ref, send_ref):
    rows = own_ref.shape[0]
    d = HEAD_DIM
    own = keep_ref.shape[1] // 2
    core = lax.axis_index("wide") & 1
    at = pl.ds(pl.multiple_of((2 * chunk + core) * rows, rows), rows)
    cosine, sine = cos_ref[at, :], sin_ref[at, :]

    def turned(x):
        return x * cosine + pltpu.roll(x, d // 2, 1) * sine

    total = keep_ref[:, own:] + first_ref[:, :own].astype(F32) + second_ref[...].astype(F32)
    q0, q1, k = (turned(total[:, i * d : (i + 1) * d]) for i in range(3))
    own_ref[:, :d] = jnp.where(core == 0, q0, q1).astype(BF16)
    send_ref[:, :d] = jnp.where(core == 0, q1, q0).astype(BF16)
    both = jnp.concatenate([k, total[:, 3 * d :]], axis=1).astype(BF16)
    own_ref[:, d:] = both
    send_ref[:, d:] = both


def finish(keep, first, second, tables, chunk, after):
    rows = keep.shape[0]
    shape = jax.ShapeDtypeStruct((rows, 3 * HEAD_DIM), BF16)
    return call(
        functools.partial(finish_kernel, chunk),
        (keep, first, second, *tables), [VMEM] * 5, (shape, shape), after,
        out_specs=(VMEM, VMEM), name="finish", flops=rows * 2048, moved=rows * 8192,
    )


def attend_kernel(chunk, prompts, n_before, n_carry, lengths_ref, sink_ref, *refs):
    count = chunk + 1
    mine_refs, other_refs = refs[:count], refs[count : 2 * count]
    befores = refs[2 * count : 2 * count + n_before]
    outs = refs[2 * count + n_before + 2 * n_carry :][:4]
    q_ref, k_ref, v_ref, out_ref = refs[-4:]
    step = mine_refs[0].shape[0]
    d = HEAD_DIM
    here, z = lax.axis_index("wide"), lax.axis_index("narrow")
    core = here & 1
    for i in range(count):
        mine, other = mine_refs[i][...], other_refs[i][...]
        for half, block in enumerate((jnp.where(core == 0, mine, other), jnp.where(core == 0, other, mine))):
            at = pl.ds((2 * i + half) * step, step)
            k_ref[at, :] = block[:, d : 2 * d]
            v_ref[at, :] = block[:, 2 * d :]
            if i == chunk:
                q_ref[half] = block[:, :d]
    sink = sink_ref[here]
    to = (z, plane(NEXT, z), 3 - z, plane(BEFORE, z))
    part = step // 4
    shift = 0
    for k in range(n_before):
        shift = befores[k].shape[0]
        outs[k][:shift, :] = befores[k][...]
    for block in range(2):
        base = (2 * chunk + block) * step
        q = q_ref[block]
        places = base + lax.broadcasted_iota(jnp.int32, (step, 1), 0)
        _, starts = prompt_of(places, lengths_ref, prompts)
        end = jnp.int32(0)
        low = jnp.int32(0)
        for p in range(prompts - 1):
            end = end + lengths_ref[p]
            low = jnp.where(base >= end, end, low)

        def body(i, carry):
            top, total, summed = carry
            at = pl.multiple_of(i * step, step)
            k = k_ref[pl.ds(at, step), :]
            v = v_ref[pl.ds(at, step), :]
            scores = lax.dot_general(q, k, (((1,), (1,)), ((), ())), preferred_element_type=F32) * score_scale
            keys = at + lax.broadcasted_iota(jnp.int32, (step, step), 1)
            allowed = jnp.logical_and(keys >= starts, keys <= places)
            scores = jnp.where(allowed, scores, -1e30)
            fresh = jnp.maximum(top, jnp.max(scores, axis=1, keepdims=True))
            factor = jnp.exp(top - fresh)
            weights = jnp.exp(scores - fresh)
            total = total * factor + jnp.sum(weights, axis=1, keepdims=True)
            summed = summed * factor + jnp.dot(weights.astype(BF16), v, preferred_element_type=F32)
            return fresh, total, summed

        top = jnp.full((step, 1), sink, F32)
        total = jnp.ones((step, 1), F32)
        summed = jnp.zeros((step, d), F32)
        top, total, summed = lax.fori_loop(
            low // step, 2 * chunk + block + 1, body, (top, total, summed)
        )
        out_ref[...] = (summed / total).astype(BF16)
        for k in range(4):
            at = pl.multiple_of(to[k] * part, part)
            first = shift + block * part
            outs[k][first : first + part, :] = out_ref[pl.ds(at, part), :]


def attend(lengths, sinks, mine, other, chunk, after, before=(), carry=()):
    step = mine[0].shape[0]
    d = HEAD_DIM
    count = chunk + 1
    rows = step // 2 + (before[0].shape[0] if before else 0)
    n = len(after) + 2 + 2 * count + len(before)
    out = call(
        functools.partial(attend_kernel, chunk, lengths.shape[0], len(before), len(carry)),
        (lengths, sinks, *mine[:count], *other[:count], *before, *carry),
        [SMEM, SMEM] + [VMEM] * (2 * count + len(before)) + [ANY] * len(carry),
        tuple(jax.ShapeDtypeStruct(c.shape, c.dtype) for c in carry)
        + (jax.ShapeDtypeStruct((rows, d), BF16),) * 4,
        after,
        scratch=[pltpu.VMEM((2, step, d), BF16)]
        + [pltpu.VMEM((2 * count * step, d), BF16)] * 2
        + [pltpu.VMEM((step, d), BF16)],
        out_specs=(ANY,) * len(carry) + (VMEM,) * 4, name="attend",
        input_output_aliases={n + i: i for i in range(len(carry))},
        flops=2 * step * 768 * 4 * d, moved=step * d * 8 * count, transcendentals=2 * step * 768,
    )
    return out[len(carry) :], out[: len(carry)]


def beside_kernel(*refs):
    out_ref = refs[-1]
    width = refs[0].shape[1]
    for i, ref in enumerate(refs[:-1]):
        out_ref[:, i * width : (i + 1) * width] = ref[...]


def beside(parts, after):
    rows, cols = parts[0].shape
    return call(
        beside_kernel, parts, [VMEM] * len(parts), jax.ShapeDtypeStruct((rows, cols * len(parts)), BF16), after,
        out_specs=VMEM, name="beside", moved=rows * cols * len(parts) * 4,
    )


def output_kernel(group, prompts, lengths_ref, *refs):
    blocks = refs[:4]
    weights = refs[4:7]
    pack_ref, keep_ref, send_ref, acc_ref = refs[7:]
    me, z = lax.axis_index("wide"), lax.axis_index("narrow")
    core = me & 1
    rows, cols = acc_ref.shape
    d = HEAD_DIM
    count, part = keep_ref.shape[1:3]
    row = lax.broadcasted_iota(jnp.int32, (rows, 1), 0)
    up = pack_ref[3 * prompts * RANK :, :]

    def times(k, w_ref):
        a = jnp.concatenate([blocks[r][:, k * d : (k + 1) * d] for r in range(4)], axis=1)
        product = lax.dot_general(a, w_ref[:cols, :], (((1,), (1,)), ((), ())), preferred_element_type=F32)
        codes = lax.dot_general(a, w_ref[cols:, :], (((1,), (1,)), ((), ())), preferred_element_type=F32)
        return product, codes

    def leave(slot, codes, plane):
        places = (2 * count * group + row // part) * (4 * part) + plane * part + row % part
        prompt, _ = prompt_of(places, lengths_ref, prompts)
        lane = lax.broadcasted_iota(jnp.int32, codes.shape, 1)
        codes = jnp.where(lane // RANK == prompt, codes, 0.0).astype(BF16)
        acc_ref[...] += jnp.dot(codes, up, preferred_element_type=F32)
        for i in range(count):
            mine = pl.multiple_of(i * 2 * part + core * part, part)
            theirs = pl.multiple_of(i * 2 * part + (1 - core) * part, part)
            keep_ref[slot, i] = acc_ref[pl.ds(mine, part), :]
            send_ref[slot, i] = acc_ref[pl.ds(theirs, part), :].astype(BF16)

    product, codes = times(3, weights[0])
    acc_ref[...] = product
    leave(1, codes, plane(BEFORE, z))
    product, codes = times(0, weights[0])
    acc_ref[...] = product
    for k in (1, 2):
        product, terms = times(k, weights[k])
        acc_ref[...] += product
        codes = codes + terms
    leave(0, codes, z)


def output(lengths, blocks, weights, pack, group, part, after):
    rows = blocks[0].shape[0]
    cols = pack.shape[1]
    shape = (2, rows // (2 * part), part, cols)
    return call(
        functools.partial(output_kernel, group, lengths.shape[0]),
        (lengths, *blocks, *weights, pack),
        [SMEM] + [VMEM] * 8,
        (jax.ShapeDtypeStruct(shape, F32), jax.ShapeDtypeStruct(shape, BF16)),
        after,
        scratch=[pltpu.VMEM((rows, cols), F32)],
        out_specs=(VMEM, VMEM), name="output",
        flops=2 * rows * 2048 * cols, moved=2048 * cols * 2 + rows * 2048 * 2 + rows * cols * 3,
    )


def fold_kernel(keep_ref, got_ref, out_ref, send_ref):
    out_ref[...] = keep_ref[0] + got_ref[0].astype(F32)
    send_ref[...] = (keep_ref[1] + got_ref[1].astype(F32)).astype(BF16)


def fold(keep, got):
    shape = keep.shape[1:]
    return call(
        fold_kernel, (keep, got), [VMEM, VMEM],
        (jax.ShapeDtypeStruct(shape, F32), jax.ShapeDtypeStruct(shape, BF16)),
        out_specs=(VMEM, VMEM), name="fold", flops=keep.size, moved=keep.size * 8,
    )


def close_kernel(stream_ref, gain_ref, *refs):
    pieces = refs[:4]
    out_ref = refs[4]
    z = lax.axis_index("narrow")
    part = pieces[0].shape[0]
    gain = gain_ref[...].astype(F32)
    for k in range(4):
        at = pl.multiple_of(jnp.bitwise_and(z - k + 4, 3) * part, part)
        rows = pl.ds(at, part)
        out_ref[rows, :] = (stream_ref[rows, :].astype(F32) + pieces[k][...].astype(F32) * gain).astype(BF16)


def close(stream, gain, pieces):
    return call(
        close_kernel, (stream, gain[None, :], *pieces), [VMEM] * 6,
        jax.ShapeDtypeStruct(stream.shape, BF16),
        out_specs=VMEM, name="close", flops=stream.size * 3, moved=stream.size * 6,
    )


def per_device_heads(
    residual,
    pre_gain,
    query_weight,
    key_weight,
    value_weight,
    output_weight,
    adapter_down,
    adapter_up_query,
    adapter_up_key,
    adapter_up_value,
    adapter_down_out,
    adapter_up_out,
    post_gain,
    sink_logits,
    prompt_lengths,
    prompt_adapters,
):
    tok, features = residual.shape
    depth = features // CHIPS
    own_rows = query_weight.shape[0]
    prompts = prompt_lengths.shape[0]
    d = HEAD_DIM
    me = lax.axis_index("wide")
    z = lax.axis_index("narrow")
    core = me & 1
    chip = me >> 1
    wide = 2 * CHIPS
    tokens = tok * wide

    flip = lambda bits: [(i, i ^ bits) for i in range(wide)]
    across = flip(1)
    first_leg = [(i, i ^ (2 if i % 2 == 0 else 4)) for i in range(wide)]
    second_leg = [(i, i ^ (4 if i % 2 == 0 else 2)) for i in range(wide)]
    shift = lambda k: [(i, (i + k) % 4) for i in range(4)]
    to_next = [(i, NEXT[i]) for i in range(4)]
    to_second = [(i, 3 - i) for i in range(4)]
    to_before = [(i, BEFORE[i]) for i in range(4)]
    zflip = lambda bits: [(i, i ^ bits) for i in range(4)]

    _, _, position = token_layout(prompt_lengths, tokens, jnp.int32(0))
    half = d // 2
    exponent = jnp.arange(half, dtype=F32) * (2.0 / d)
    frequency = jnp.power(jnp.float32(rotary_base), -exponent)
    angle = position.astype(F32)[:, None] * frequency[None, :]
    cosine, sine = jnp.cos(angle), jnp.sin(angle)
    cosine = jnp.concatenate([cosine, cosine], axis=1)
    sine = jnp.concatenate([-sine, sine], axis=1)

    pack = pick(prompt_adapters, adapter_down.T, adapter_up_out, ())
    cut = norm(residual, pre_gain, 4, (pack,))
    pieces = [cut[0]] + [lax.ppermute(cut[delta], "wide", flip(2 * delta)) for delta in (1, 2, 3)]
    pack = merge(pack, lax.ppermute(pack, "narrow", zflip(1)), cut)
    w_mine, w_theirs = arrange(
        query_weight, key_weight, value_weight, output_weight.T, (pack, pieces[1])
    )
    up, out_down = ups(
        prompt_adapters, adapter_up_query, adapter_up_key, adapter_up_value, adapter_down_out, (w_mine,)
    )
    w, ring0 = stack(w_mine, lax.ppermute(w_theirs, "wide", across), out_down, (up,))
    pack = merge(pack, lax.ppermute(pack, "narrow", zflip(2)), (w, cosine, sine))
    pack = join(pack, lax.ppermute(pack, "wide", across))
    ring1 = lax.ppermute(ring0, "narrow", to_next)

    tables = (cosine, sine)
    part = tok // 4
    sends, keeps, ones, twos, mine, other = [], [], [], [], [], []

    def product(chunk, after, carry=()):
        send, keep, carried = project(prompt_lengths, pieces, w, pack, up, chunk, after, carry)
        sends.append(send)
        keeps.append(keep)
        ones.append(lax.ppermute(send, "wide", first_leg))
        return carried

    def pass_on(chunk, after, carry=()):
        out, carried = onward(keeps[chunk], ones[chunk], after, carry)
        twos.append(lax.ppermute(out, "wide", second_leg))
        return (out, *carried)

    def rotate_chunk(chunk, after):
        own, send = finish(keeps[chunk], ones[chunk], twos[chunk], tables, chunk, after)
        mine.append(own)
        other.append(lax.ppermute(send, "wide", across))
        return own

    def attend_chunk(chunk, after, before=(), carry=()):
        return attend(prompt_lengths, sink_logits, mine, other, chunk, after, before, carry)

    def gather_group(sub, after):
        near0 = beside(
            (
                sub[0],
                lax.ppermute(sub[1], "narrow", to_next),
                lax.ppermute(sub[2], "narrow", to_second),
                sub[3],
            ),
            after,
        )
        near1 = lax.ppermute(near0, "wide", first_leg)
        near2 = lax.ppermute(near0, "wide", second_leg)
        near3 = lax.ppermute(near1, "wide", second_leg)
        return near0, near1, near2, near3

    product(0, (cosine, sine))
    product(1, (sends[0],))
    (out0,) = pass_on(0, (sends[1],))
    product(2, (out0,))
    (out1,) = pass_on(1, (sends[2],))
    q0 = rotate_chunk(0, (out1,))
    product(3, (q0,))
    out2, ring1 = pass_on(2, (sends[3],), (ring1,))
    ring2 = lax.ppermute(ring1, "narrow", to_next)
    q1 = rotate_chunk(1, (out2,))
    sub0, _ = attend_chunk(0, (q1,))
    (out3,) = pass_on(3, (sub0[0],))
    q2 = rotate_chunk(2, (out3,))
    sub1, _ = attend_chunk(1, (q2,), sub0)
    q3 = rotate_chunk(3, (sub1[0],))
    sub2, _ = attend_chunk(2, (q3,))
    sub3, _ = attend_chunk(3, (sub2[0],), sub2)
    out_weights = (ring0, ring1, ring2)
    halves = []
    before = sub3[0]
    for group, sub in enumerate((sub1, sub3)):
        keep, send = output(
            prompt_lengths, gather_group(sub, (sub3[0],)), out_weights, pack, group, part, (before,)
        )
        main, extra = fold(keep, lax.ppermute(send, "wide", across))
        halves.append(merge(main, lax.ppermute(extra, "narrow", to_before)))
        before = keep
    total = jnp.concatenate(halves)
    rows_of = lambda to: lax.dynamic_index_in_dim(total, to, 0, keepdims=False)
    full = [rows_of(chip)] + [
        lax.ppermute(rows_of(chip ^ delta), "wide", flip(2 * delta)) for delta in (1, 2, 3)
    ]
    full = jnp.stack(full)
    wide_rows = full.astype(F32)
    mean_square = jnp.sum(wide_rows * wide_rows, axis=(0, 2)) / features
    scaled = (wide_rows * lax.rsqrt(mean_square + epsilon)[None, :, None]).astype(BF16)
    finals = []
    for k in range(4):
        piece = lax.dynamic_index_in_dim(scaled, chip ^ ((z + k) & 3), 0, keepdims=False)
        finals.append(piece if k == 0 else lax.ppermute(piece, "narrow", shift(k)))
    own_width = post_gain.shape[0]
    own_stream = lax.dynamic_slice_in_dim(residual, z * own_width, own_width, 1)
    return close(own_stream, post_gain, finals)
def rotate(values, position):
    half = values.shape[-1] // 2
    exponent = jnp.arange(half, dtype=jnp.float32) * (2.0 / values.shape[-1])
    frequency = jnp.power(jnp.float32(rotary_base), -exponent)
    angle = position.astype(jnp.float32)[:, None] * frequency[None, :]
    cosine = jnp.cos(angle)[:, None, :]
    sine = jnp.sin(angle)[:, None, :]
    first_half = values[..., :half]
    second_half = values[..., half:]
    return jnp.concatenate(
        [first_half * cosine - second_half * sine, second_half * cosine + first_half * sine],
        axis=-1,
    )


def select_codes(codes, adapter, projections, adapters):
    count = codes.shape[0]
    width = codes.shape[1] // (adapters * projections)
    shaped = codes.reshape(count, adapters, projections, width)
    onehot = (adapter[:, None] == jnp.arange(adapters, dtype=jnp.int32)[None, :]).astype(
        codes.dtype
    )
    kept = shaped * onehot[:, :, None, None]
    return [kept[:, :, slot, :].reshape(count, adapters * width) for slot in range(projections)]


def add_adapter(partial_out, adapter_cols, offset, own_width):
    current = lax.dynamic_slice_in_dim(partial_out, offset, own_width, 1)
    return lax.dynamic_update_slice_in_dim(partial_out, current + adapter_cols, offset, 1)


def per_device(
    residual,
    pre_gain,
    query_weight,
    key_weight,
    value_weight,
    output_weight,
    adapter_down,
    adapter_up_query,
    adapter_up_key,
    adapter_up_value,
    adapter_down_out,
    adapter_up_out,
    post_gain,
    sink_logits,
    prompt_lengths,
    prompt_adapters,
):
    tok_rows = residual.shape[0]
    first = lax.axis_index("wide") * tok_rows
    member, prompt, position = token_layout(prompt_lengths, tok_rows, first)
    adapter = jnp.sum(member * prompt_adapters[None, :], axis=1)
    stream = residual.astype(jnp.float32)
    scale_rows = lax.rsqrt(jnp.mean(stream * stream, axis=1, keepdims=True) + epsilon)
    normed = (stream * scale_rows * pre_gain.astype(jnp.float32)[None, :]).astype(jnp.bfloat16)
    query_cols = query_weight.shape[1]
    key_cols = key_weight.shape[1]
    pieces = (
        lax.all_gather(query_weight, "wide", axis=0, tiled=True),
        lax.all_gather(key_weight, "wide", axis=0, tiled=True),
        lax.all_gather(value_weight, "wide", axis=0, tiled=True),
        lax.all_gather(adapter_down, "wide", axis=0, tiled=True),
    )
    query_part, key_part, value_part, code_part = tuple(
        (jnp.dot(normed, piece, preferred_element_type=jnp.float32) for piece in pieces)
    )
    codes = lax.all_gather(code_part.astype(jnp.bfloat16), "narrow", axis=1, tiled=True)
    chosen = select_codes(codes, adapter, 3, ADAPTERS)
    query = query_part + adapter_scale * jnp.dot(
        chosen[0], adapter_up_query, preferred_element_type=jnp.float32
    )
    key = key_part + adapter_scale * jnp.dot(
        chosen[1], adapter_up_key, preferred_element_type=jnp.float32
    )
    value = value_part + adapter_scale * jnp.dot(
        chosen[2], adapter_up_value, preferred_element_type=jnp.float32
    )
    local_heads = query_cols // HEAD_DIM
    local_kv = key_cols // HEAD_DIM
    group = local_heads // local_kv
    queries = (
        rotate(query.reshape(tok_rows, local_heads, HEAD_DIM), position)
        .astype(jnp.bfloat16)
        .reshape(tok_rows, local_kv, group, HEAD_DIM)
    )
    keys = rotate(key.reshape(tok_rows, local_kv, HEAD_DIM), position).astype(jnp.bfloat16)
    values = value.astype(jnp.bfloat16).reshape(tok_rows, local_kv, HEAD_DIM)
    sinks = sink_logits.reshape(local_kv, group)
    own_places = first + jnp.arange(tok_rows, dtype=jnp.int32)
    start_top = jnp.broadcast_to(sinks[None, :, :], (tok_rows, local_kv, group))
    start_total = jnp.ones((tok_rows, local_kv, group), jnp.float32)
    start_sum = jnp.zeros((tok_rows, local_kv, group, HEAD_DIM), jnp.float32)
    top = start_top
    total = start_total
    summed_values = start_sum
    piece_keys = lax.all_gather(keys, "wide", axis=0, tiled=True)
    piece_values = lax.all_gather(values, "wide", axis=0, tiled=True)
    count = piece_keys.shape[0]
    unused, key_prompt, unused_position = token_layout(prompt_lengths, count, jnp.int32(0))
    key_places = jnp.arange(count, dtype=jnp.int32)
    allowed = jnp.logical_and(
        prompt[:, None] == key_prompt[None, :], own_places[:, None] >= key_places[None, :]
    )[:, None, None, :]
    scores = (
        jnp.einsum("qgjd,kgd->qgjk", queries, piece_keys, preferred_element_type=jnp.float32)
        * score_scale
    )
    scores = jnp.where(allowed, scores, -1e30)
    fresh = jnp.maximum(top, jnp.max(scores, axis=-1))
    factor = jnp.exp(top - fresh)
    weights = jnp.where(allowed, jnp.exp(scores - fresh[..., None]), 0.0)
    total = total * factor + jnp.sum(weights, axis=-1)
    update = jnp.einsum(
        "qgjk,kgd->qgjd",
        weights.astype(jnp.bfloat16),
        piece_values,
        preferred_element_type=jnp.float32,
    )
    top, total, summed_values = (fresh, total, summed_values * factor[..., None] + update)
    attended = (
        (summed_values / total[..., None])
        .reshape(tok_rows, local_heads * HEAD_DIM)
        .astype(jnp.bfloat16)
    )
    code_terms = jnp.dot(attended, adapter_down_out, preferred_element_type=jnp.float32)
    codes_out = lax.psum(code_terms.astype(jnp.bfloat16), "narrow")
    chosen_out = select_codes(codes_out, adapter, 1, ADAPTERS)[0]
    adapter_cols = adapter_scale * jnp.dot(
        chosen_out, adapter_up_out, preferred_element_type=jnp.float32
    )
    own_width = adapter_up_out.shape[1]
    offset = lax.axis_index("narrow") * own_width
    partial_out = jnp.dot(
        attended,
        lax.all_gather(output_weight, "wide", axis=1, tiled=True),
        preferred_element_type=jnp.float32,
    )
    partial_out = add_adapter(partial_out, adapter_cols, offset, own_width)
    whole = lax.psum(partial_out.astype(jnp.bfloat16), "narrow").astype(jnp.float32)
    mean_square = jnp.mean(whole * whole, axis=1)
    projected = lax.dynamic_slice_in_dim(whole, offset, own_width, 1)
    factor_rows = lax.rsqrt(mean_square + epsilon)
    own_stream = lax.dynamic_slice_in_dim(stream, offset, own_width, 1)
    mixed = own_stream + projected * factor_rows[:, None] * post_gain.astype(jnp.float32)[None, :]
    return mixed.astype(jnp.bfloat16)


def fits(mesh):
    return mesh.shape["wide"] == 2 * CHIPS and mesh.shape["narrow"] == 4


def solution(mesh):
    return jax.shard_map(
        per_device_heads if fits(mesh) else per_device,
        mesh=mesh,
        in_specs=(
            P("wide", None),
            P(),
            P("wide", "narrow"),
            P("wide", "narrow"),
            P("wide", "narrow"),
            P("narrow", "wide"),
            P("wide", "narrow"),
            P(None, "narrow"),
            P(None, "narrow"),
            P(None, "narrow"),
            P("narrow", None),
            P(None, "narrow"),
            P("narrow"),
            P("narrow"),
            P(),
            P(),
        ),
        out_specs=P("wide", "narrow"),
        check_vma=False,
    )
```

```python
import functools

import jax
import jax.numpy as jnp
from jax import lax
from jax.experimental import pallas as pl
from jax.experimental.pallas import tpu as pltpu
from jax.sharding import PartitionSpec as P

HEAD_DIM = 128
ADAPTERS = 16
RANK = 16

epsilon = 1e-06
adapter_scale = 0.5
rotary_base = 10000.0
score_scale = 1.0 / 12.0

CHIPS = 4
CHUNKS = 4
F32 = jnp.float32
BF16 = jnp.bfloat16
SMEM = pl.BlockSpec(memory_space=pltpu.SMEM)
VMEM = pl.BlockSpec(memory_space=pltpu.VMEM)
ANY = pl.BlockSpec(memory_space=pl.ANY)
HBM = pl.BlockSpec(memory_space=pltpu.HBM)


def token_layout(prompt_lengths, count, first):
    ends = jnp.cumsum(prompt_lengths, dtype=jnp.int32)
    starts = ends - prompt_lengths
    places = first + jnp.arange(count, dtype=jnp.int32)
    member = jnp.logical_and(
        places[:, None] >= starts[None, :], places[:, None] < ends[None, :]
    ).astype(jnp.int32)
    labels = jnp.arange(prompt_lengths.shape[0], dtype=jnp.int32)
    prompt = jnp.sum(member * labels[None, :], axis=1)
    position = places - jnp.sum(member * starts[None, :], axis=1)
    return (member, prompt, position)


def call(kernel, operands, specs, out_shape, after=(), scratch=(), name=None, flops=0, moved=0, transcendentals=0, grant=24, **more):
    n = len(after)
    return pl.pallas_call(
        lambda *refs: kernel(*refs[n:]),
        out_shape=out_shape,
        in_specs=[ANY] * n + list(specs),
        scratch_shapes=list(scratch),
        name=name,
        compiler_params=pltpu.CompilerParams(vmem_limit_bytes=grant * 1024 * 1024),
        cost_estimate=pl.CostEstimate(flops=flops // 64, bytes_accessed=moved // 64, transcendentals=transcendentals // 64),
        **more,
    )(*after, *operands)


def prompt_of(places, lengths_ref, prompts):
    end = jnp.int32(0)
    prompt = jnp.zeros_like(places)
    start = jnp.zeros_like(places)
    for p in range(prompts - 1):
        end = end + lengths_ref[p]
        past = places >= end
        prompt = jnp.where(past, p + 1, prompt)
        start = jnp.where(past, end, start)
    return prompt, start


def order(chip, core):
    return (chip ^ (1 + core), chip ^ 3, chip ^ (2 - core), chip)


NEXT = (1, 3, 0, 2)
BEFORE = (2, 0, 3, 1)


def plane(table, z):
    return jnp.where(z == 0, table[0], jnp.where(z == 1, table[1], jnp.where(z == 2, table[2], table[3])))


def near(chip, core):
    return (chip, chip ^ (1 + core), chip ^ (2 - core), chip ^ 3)


def norm_kernel(steps, x_hbm, gain_ref, *refs):
    (first_ref, second_ref, own_ref), (x_ref, y_ref, sems) = refs[:3], refs[3:]
    me = lax.axis_index("wide")
    chip, core = lax.shift_right_logical(me, 1), me & 1
    depth = own_ref.shape[1]
    rows = x_ref.shape[0]
    step = rows // steps
    copies = [
        pltpu.make_async_copy(x_hbm.at[pl.ds(i * step, step), :], x_ref.at[pl.ds(i * step, step), :], sems.at[i])
        for i in range(steps)
    ]
    for copy in copies:
        copy.start()
    gain = gain_ref[...].astype(F32).reshape(1, -1)
    for i in range(steps):
        copies[i].wait()
        at = i * step
        x = x_ref[at : at + step, :].astype(F32)
        scale = lax.rsqrt(jnp.sum(x * x, axis=1, keepdims=True) / x.shape[1] + epsilon)
        y_ref[...] = (x * scale * gain).astype(BF16)
        for to, out, base in zip(order(chip, core), (first_ref, first_ref, second_ref, own_ref), (0, rows, 0, 0)):
            out[base + at : base + at + step, :] = y_ref[:, pl.ds(pl.multiple_of(to * depth, 128), depth)]


def norm(x, gain, steps, after):
    rows, cols = x.shape
    depth = cols // CHIPS
    shape = jax.ShapeDtypeStruct((rows, depth), x.dtype)
    return call(
        functools.partial(norm_kernel, steps), (x, gain), [HBM, VMEM],
        (jax.ShapeDtypeStruct((2 * rows, depth), x.dtype), shape, shape), after,
        scratch=[
            pltpu.VMEM((rows, cols), BF16),
            pltpu.VMEM((rows // steps, cols), BF16),
            pltpu.SemaphoreType.DMA((steps,)),
        ],
        out_specs=(VMEM,) * 3, name="norm", grant=60, flops=x.size * 4, moved=x.size * 4,
    )


def arrange_kernel(q_hbm, k_hbm, v_hbm, o_hbm, mine_ref, theirs_ref, q_ref, k_ref, v_ref, o_ref, in_sems, sems):
    me = lax.axis_index("wide")
    chip, own = lax.shift_right_logical(me, 1), me & 1
    d = HEAD_DIM
    loads = [
        pltpu.make_async_copy(source, target, in_sems.at[i])
        for i, (source, target) in enumerate(
            ((q_hbm, q_ref), (k_hbm, k_ref), (v_hbm, v_ref), (o_hbm, o_ref))
        )
    ]
    for one in loads:
        one.start()
    copies = []

    def copy(ref, at, out, to, width):
        source = ref.at[:, pl.ds(pl.multiple_of(at, d), width)]
        copies.append(pltpu.make_async_copy(source, out.at[:, pl.ds(to, width)], sems.at[len(copies)]))
        copies[-1].start()

    for load, ref, width, at in zip(loads, (q_ref, k_ref, v_ref), (2 * d, d, d), (0, 2 * d, 3 * d)):
        load.wait()
        for core, out in ((1 - own, theirs_ref), (own, mine_ref)):
            for place, to in enumerate(order(chip, core)):
                copy(ref, to * width, out, 4 * place * d + at, width)
    loads[3].wait()
    for core, out in ((1 - own, theirs_ref), (own, mine_ref)):
        for place, source in enumerate(near(chip, core)):
            copy(o_ref, (2 * source + core) * d, out, (4 * CHIPS + place) * d, d)
    for one in copies:
        one.wait()


def arrange(q, k, v, o, after):
    shape = jax.ShapeDtypeStruct((q.shape[0], 5 * CHIPS * HEAD_DIM), BF16)
    return call(
        arrange_kernel, (q, k, v, o), [HBM] * 4, (shape, shape), after,
        scratch=[pltpu.VMEM(x.shape, BF16) for x in (q, k, v, o)]
        + [pltpu.SemaphoreType.DMA((4,)), pltpu.SemaphoreType.DMA((32,))],
        out_specs=(ANY, ANY), name="arrange", grant=60, moved=q.size * 16,
    )


def choose(shape, row_prompt, chosen_ref, prompts):
    adapter = jnp.zeros(shape, jnp.int32)
    for p in range(prompts):
        adapter = jnp.where(row_prompt == p, chosen_ref[p], adapter)
    return adapter


def pick_kernel(prompts, chosen_ref, down_hbm, other_hbm, upo_hbm, pack_ref, down_ref, other_ref, upo_ref, sems):
    me, z = lax.axis_index("wide"), lax.axis_index("narrow")
    chip = lax.shift_right_logical(me, 1)
    core = me & 1
    n_codes = prompts * RANK
    local = down_ref.shape[0] // (3 * RANK)
    rows = down_ref.shape[1]
    copies = [
        pltpu.make_async_copy(down_hbm, down_ref, sems.at[prompts]),
        pltpu.make_async_copy(other_hbm, other_ref, sems.at[prompts + 1]),
    ]
    for p in range(prompts):
        at = pl.ds(pl.multiple_of(chosen_ref[p] * RANK, RANK), RANK)
        copies.append(pltpu.make_async_copy(upo_hbm.at[at, :], upo_ref.at[pl.ds(p * RANK, RANK), :], sems.at[p]))
    for copy in copies:
        copy.start()
    shape = (3 * n_codes, down_ref.shape[0])
    row = lax.broadcasted_iota(jnp.int32, shape, 0)
    col = lax.broadcasted_iota(jnp.int32, shape, 1)
    adapter = choose(shape, (row % n_codes) // RANK, chosen_ref, prompts)

    def pick_of(plane_at):
        wanted = (adapter - plane_at * local) * (3 * RANK) + (row // n_codes) * RANK + row % RANK
        inside = jnp.logical_and(adapter >= plane_at * local, adapter < (plane_at + 1) * local)
        return jnp.where(jnp.logical_and(inside, col == wanted), 1.0, 0.0).astype(BF16)

    mine, theirs = pick_of(z), pick_of(z ^ 1)
    for copy in copies:
        copy.wait()
    down = jnp.dot(mine, down_ref[...], preferred_element_type=F32)
    down = down + jnp.dot(theirs, other_ref[...], preferred_element_type=F32)
    pack_ref[: 3 * n_codes, :] = down.astype(BF16)
    both = upo_ref[...].astype(F32) * adapter_scale
    part = jnp.where(core == 0, both[:, :rows], both[:, rows:])
    pack_ref[3 * n_codes :, :] = jnp.where(z == chip, part, 0.0).astype(BF16)


def pick(chosen, down, other, upo, after):
    prompts = chosen.shape[0]
    n_codes = prompts * RANK
    return call(
        functools.partial(pick_kernel, prompts), (chosen, down, other, upo), [SMEM, HBM, HBM, HBM],
        jax.ShapeDtypeStruct((4 * n_codes, down.shape[1]), BF16),
        after,
        scratch=[
            pltpu.VMEM(down.shape, BF16),
            pltpu.VMEM(down.shape, BF16),
            pltpu.VMEM((n_codes, upo.shape[1]), BF16),
            pltpu.SemaphoreType.DMA((prompts + 2,)),
        ],
        out_specs=VMEM, name="pick", grant=60, flops=down.size * 400, moved=down.size * 6,
    )


def merge_kernel(a_ref, b_ref, out_ref):
    out_ref[...] = (a_ref[...].astype(F32) + b_ref[...].astype(F32)).astype(out_ref.dtype)


def merge(a, b, after=()):
    return call(
        merge_kernel, (a, b), [VMEM, VMEM], jax.ShapeDtypeStruct(a.shape, BF16), after,
        out_specs=VMEM, name="merge", flops=a.size, moved=a.size * 6,
    )


def ups_kernel(prompts, chosen_ref, upq_ref, upk_ref, upv_ref, ado_ref, up_ref, out_ref):
    me = lax.axis_index("wide")
    chip = lax.shift_right_logical(me, 1)
    core = me & 1
    d = HEAD_DIM
    n_codes = prompts * RANK
    up_ref[...] = jnp.zeros_like(up_ref)
    for p in range(prompts):
        rows = pl.ds(pl.multiple_of(chosen_ref[p] * RANK, RANK), RANK)
        for place, to in enumerate(order(chip, core)):
            for slot, (ref, width, at) in enumerate(((upq_ref, 2 * d, 0), (upk_ref, d, 2 * d), (upv_ref, d, 3 * d))):
                part = ref[rows, pl.ds(pl.multiple_of(to * width, d), width)].astype(F32) * adapter_scale
                first = slot * n_codes + p * RANK
                left = 4 * place * d + at
                up_ref[first : first + RANK, left : left + width] = part.astype(BF16)
    shape = (n_codes, ado_ref.shape[1])
    row = lax.broadcasted_iota(jnp.int32, shape, 0)
    col = lax.broadcasted_iota(jnp.int32, shape, 1)
    adapter = choose(shape, row // RANK, chosen_ref, prompts)
    pick = jnp.where(col == adapter * RANK + row % RANK, 1.0, 0.0).astype(BF16)
    for place, source in enumerate(near(chip, core)):
        block = ado_ref[pl.ds(pl.multiple_of((2 * source + core) * d, d), d), :]
        part = lax.dot_general(pick, block, (((1,), (1,)), ((), ())), preferred_element_type=F32)
        out_ref[:, place * d : (place + 1) * d] = part.astype(BF16)


def ups(chosen, upq, upk, upv, ado, after):
    prompts = chosen.shape[0]
    n_codes = prompts * RANK
    return call(
        functools.partial(ups_kernel, prompts), (chosen, upq, upk, upv, ado), [SMEM] + [VMEM] * 4,
        (
            jax.ShapeDtypeStruct((3 * n_codes, 2 * upq.shape[1]), BF16),
            jax.ShapeDtypeStruct((n_codes, CHIPS * HEAD_DIM), BF16),
        ),
        after, out_specs=(VMEM,) * 2, name="ups", flops=upq.size * 100, moved=upq.size * 6,
    )


def stack_kernel(mine_ref, got_ref, down_ref, w_ref, ring_ref, sems):
    core = lax.axis_index("wide") & 1
    rows = mine_ref.shape[0]
    cols = w_ref.shape[1]
    width = ring_ref.shape[1]
    copies = []
    for i, (ref, at) in enumerate(((mine_ref, core), (got_ref, 1 - core))):
        to = pl.ds(pl.multiple_of(at * rows, 16), rows)
        copies.append(pltpu.make_async_copy(ref.at[:, pl.ds(cols, width)], ring_ref.at[to, :], sems.at[2 * i]))
        copies.append(pltpu.make_async_copy(ref.at[:, pl.ds(0, cols)], w_ref.at[to, :], sems.at[2 * i + 1]))
    copies.append(pltpu.make_async_copy(down_ref, ring_ref.at[pl.ds(2 * rows, down_ref.shape[0]), :], sems.at[4]))
    for copy in copies:
        copy.start()
    for copy in copies:
        copy.wait()


def stack(mine, got, down, after):
    rows, cols = mine.shape
    width = down.shape[1]
    return call(
        stack_kernel, (mine, got, down), [ANY] * 3,
        (
            jax.ShapeDtypeStruct((2 * rows, cols - width), mine.dtype),
            jax.ShapeDtypeStruct((2 * rows + down.shape[0], width), mine.dtype),
        ),
        after,
        scratch=[pltpu.SemaphoreType.DMA((5,))], out_specs=(ANY, ANY), name="stack", moved=rows * cols * 8,
    )


def join_kernel(mine_ref, other_ref, out_ref):
    core = lax.axis_index("wide") & 1
    mine, other = mine_ref[...].astype(F32), other_ref[...].astype(F32)
    left = jnp.where(core == 0, mine, other)
    right = jnp.where(core == 0, other, mine)
    out_ref[...] = jnp.concatenate([left, right], axis=1).astype(out_ref.dtype)


def join(mine, other, after=()):
    rows, cols = mine.shape
    return call(
        join_kernel, (mine, other), [VMEM, VMEM], jax.ShapeDtypeStruct((rows, 2 * cols), mine.dtype), after,
        out_specs=VMEM, name="join", flops=rows * cols * 4, moved=rows * cols * 8,
    )


def project_kernel(chunk, prompts, lengths_ref, *refs):
    x_refs = refs[:4]
    w_ref, pack_ref, up_ref = refs[4:7]
    send_ref, keep_ref, x_ref, sem = refs[-4:]
    me = lax.axis_index("wide")
    chip = lax.shift_right_logical(me, 1)
    core = me & 1
    rows = x_ref.shape[0]
    half = send_ref.shape[1]
    n_codes = prompts * RANK
    for k, held in enumerate((chip ^ (1 + core), chip ^ 3, chip ^ (2 - core), chip)):

        @pl.when(held == chunk)
        def _():
            pltpu.make_async_copy(x_refs[k].at[pl.ds(0, rows), :], x_ref, sem).start()

    pltpu.make_async_copy(x_refs[3], x_ref, sem).wait()
    x = x_ref[...]
    codes = lax.dot_general(
        x, pack_ref[...], (((1,), (1,)), ((), ())), preferred_element_type=F32
    )
    places = (2 * chunk + core) * rows + lax.broadcasted_iota(jnp.int32, (rows, 1), 0)
    prompt, _ = prompt_of(places, lengths_ref, prompts)
    lane = lax.broadcasted_iota(jnp.int32, codes.shape, 1)
    owner = (lane % n_codes) // RANK
    codes = jnp.where(owner == prompt, codes, 0.0).astype(BF16)
    for part, out in ((0, send_ref), (1, keep_ref)):
        cols = pl.ds(part * half, half)
        product = jnp.dot(x, w_ref[:, cols], preferred_element_type=F32)
        product = product + jnp.dot(codes, up_ref[:, cols], preferred_element_type=F32)
        out[...] = product.astype(out.dtype)


def project(lengths, pieces, w, pack, up, chunk, after, carry=()):
    rows, depth = pieces[3].shape
    half = w.shape[1] // 2
    n = len(after) + 8
    out = call(
        functools.partial(project_kernel, chunk, lengths.shape[0]),
        (lengths, *pieces, w, pack, up, *carry),
        [SMEM] + [ANY] * 4 + [VMEM] * 3 + [ANY] * len(carry),
        tuple(jax.ShapeDtypeStruct(c.shape, c.dtype) for c in carry)
        + (jax.ShapeDtypeStruct((rows, half), BF16), jax.ShapeDtypeStruct((rows, half), F32)),
        after,
        scratch=[pltpu.VMEM((rows, depth), BF16), pltpu.SemaphoreType.DMA(())],
        out_specs=(ANY,) * len(carry) + (VMEM, VMEM), name="project",
        input_output_aliases={n + i: i for i in range(len(carry))},
        flops=2 * rows * depth * w.shape[1], moved=rows * depth * 2 + w.size * 2 + rows * half * 6,
    )
    return out[-2], out[-1], out[:-2]


def onward_kernel(keep_ref, first_ref, *refs):
    out_ref = refs[-1]
    own = out_ref.shape[1]
    out_ref[...] = (keep_ref[:, :own] + first_ref[:, own:].astype(F32)).astype(BF16)


def onward(keep, first, after, carry=()):
    rows, cols = keep.shape
    n = len(after) + 2
    out = call(
        onward_kernel, (keep, first, *carry), [VMEM, VMEM] + [ANY] * len(carry),
        tuple(jax.ShapeDtypeStruct(c.shape, c.dtype) for c in carry)
        + (jax.ShapeDtypeStruct((rows, cols // 2), BF16),),
        after, out_specs=(ANY,) * len(carry) + (VMEM,), name="onward",
        input_output_aliases={n + i: i for i in range(len(carry))},
        flops=rows * cols, moved=rows * cols * 4,
    )
    return out[-1], out[:-1]


def finish_kernel(chunk, keep_ref, first_ref, second_ref, cos_ref, sin_ref, own_ref, send_ref):
    rows = own_ref.shape[0]
    d = HEAD_DIM
    own = keep_ref.shape[1] // 2
    core = lax.axis_index("wide") & 1
    at = pl.ds(pl.multiple_of((2 * chunk + core) * rows, rows), rows)
    cosine, sine = cos_ref[at, :], sin_ref[at, :]

    def turned(x):
        return x * cosine + pltpu.roll(x, d // 2, 1) * sine

    total = keep_ref[:, own:] + first_ref[:, :own].astype(F32) + second_ref[...].astype(F32)
    q0, q1, k = (turned(total[:, i * d : (i + 1) * d]) for i in range(3))
    own_ref[:, :d] = jnp.where(core == 0, q0, q1).astype(BF16)
    send_ref[:, :d] = jnp.where(core == 0, q1, q0).astype(BF16)
    both = jnp.concatenate([k, total[:, 3 * d :]], axis=1).astype(BF16)
    own_ref[:, d:] = both
    send_ref[:, d:] = both


def finish(keep, first, second, tables, chunk, after):
    rows = keep.shape[0]
    shape = jax.ShapeDtypeStruct((rows, 3 * HEAD_DIM), BF16)
    return call(
        functools.partial(finish_kernel, chunk),
        (keep, first, second, *tables), [VMEM] * 5, (shape, shape), after,
        out_specs=(VMEM, VMEM), name="finish", flops=rows * 2048, moved=rows * 8192,
    )


def attend_kernel(chunk, prompts, n_before, n_carry, lengths_ref, sink_ref, *refs):
    count = chunk + 1
    mine_refs, other_refs = refs[:count], refs[count : 2 * count]
    befores = refs[2 * count : 2 * count + n_before]
    outs = refs[2 * count + n_before + 2 * n_carry :][:4]
    q_ref, k_ref, v_ref, out_ref = refs[-4:]
    step = mine_refs[0].shape[0]
    d = HEAD_DIM
    here, z = lax.axis_index("wide"), lax.axis_index("narrow")
    core = here & 1
    for i in range(count):
        mine, other = mine_refs[i][...], other_refs[i][...]
        for half, block in enumerate((jnp.where(core == 0, mine, other), jnp.where(core == 0, other, mine))):
            at = pl.ds((2 * i + half) * step, step)
            k_ref[at, :] = block[:, d : 2 * d]
            v_ref[at, :] = block[:, 2 * d :]
            if i == chunk:
                q_ref[half] = block[:, :d]
    sink = sink_ref[here]
    to = (z, plane(NEXT, z), 3 - z, plane(BEFORE, z))
    part = step // 4
    shift = 0
    for k in range(n_before):
        shift = befores[k].shape[0]
        outs[k][:shift, :] = befores[k][...]
    for block in range(2):
        base = (2 * chunk + block) * step
        q = q_ref[block]
        places = base + lax.broadcasted_iota(jnp.int32, (step, 1), 0)
        _, starts = prompt_of(places, lengths_ref, prompts)
        end = jnp.int32(0)
        low = jnp.int32(0)
        for p in range(prompts - 1):
            end = end + lengths_ref[p]
            low = jnp.where(base >= end, end, low)

        def body(i, carry):
            top, total, summed = carry
            at = pl.multiple_of(i * step, step)
            k = k_ref[pl.ds(at, step), :]
            v = v_ref[pl.ds(at, step), :]
            scores = lax.dot_general(q, k, (((1,), (1,)), ((), ())), preferred_element_type=F32) * score_scale
            keys = at + lax.broadcasted_iota(jnp.int32, (step, step), 1)
            allowed = jnp.logical_and(keys >= starts, keys <= places)
            scores = jnp.where(allowed, scores, -1e30)
            fresh = jnp.maximum(top, jnp.max(scores, axis=1, keepdims=True))
            factor = jnp.exp(top - fresh)
            weights = jnp.exp(scores - fresh)
            total = total * factor + jnp.sum(weights, axis=1, keepdims=True)
            summed = summed * factor + jnp.dot(weights.astype(BF16), v, preferred_element_type=F32)
            return fresh, total, summed

        top = jnp.full((step, 1), sink, F32)
        total = jnp.ones((step, 1), F32)
        summed = jnp.zeros((step, d), F32)
        top, total, summed = lax.fori_loop(
            low // step, 2 * chunk + block + 1, body, (top, total, summed)
        )
        out_ref[...] = (summed / total).astype(BF16)
        for k in range(4):
            at = pl.multiple_of(to[k] * part, part)
            first = shift + block * part
            outs[k][first : first + part, :] = out_ref[pl.ds(at, part), :]


def attend(lengths, sinks, mine, other, chunk, after, before=(), carry=()):
    step = mine[0].shape[0]
    d = HEAD_DIM
    count = chunk + 1
    rows = step // 2 + (before[0].shape[0] if before else 0)
    n = len(after) + 2 + 2 * count + len(before)
    out = call(
        functools.partial(attend_kernel, chunk, lengths.shape[0], len(before), len(carry)),
        (lengths, sinks, *mine[:count], *other[:count], *before, *carry),
        [SMEM, SMEM] + [VMEM] * (2 * count + len(before)) + [ANY] * len(carry),
        tuple(jax.ShapeDtypeStruct(c.shape, c.dtype) for c in carry)
        + (jax.ShapeDtypeStruct((rows, d), BF16),) * 4,
        after,
        scratch=[pltpu.VMEM((2, step, d), BF16)]
        + [pltpu.VMEM((2 * count * step, d), BF16)] * 2
        + [pltpu.VMEM((step, d), BF16)],
        out_specs=(ANY,) * len(carry) + (VMEM,) * 4, name="attend",
        input_output_aliases={n + i: i for i in range(len(carry))},
        flops=2 * step * 768 * 4 * d, moved=step * d * 8 * count, transcendentals=2 * step * 768,
    )
    return out[len(carry) :], out[: len(carry)]


def beside_kernel(*refs):
    out_ref = refs[-1]
    width = refs[0].shape[1]
    for i, ref in enumerate(refs[:-1]):
        out_ref[:, i * width : (i + 1) * width] = ref[...]


def beside(parts, after):
    rows, cols = parts[0].shape
    return call(
        beside_kernel, parts, [VMEM] * len(parts), jax.ShapeDtypeStruct((rows, cols * len(parts)), BF16), after,
        out_specs=VMEM, name="beside", moved=rows * cols * len(parts) * 4,
    )


def output_kernel(before, count, prompts, lengths_ref, *refs):
    blocks = refs[:4]
    weights = refs[4 : 4 + count]
    up_ref, keep_ref, send_ref, acc_ref = refs[4 + count :]
    z = lax.axis_index("narrow")
    core = lax.axis_index("wide") & 1
    rows, cols = acc_ref.shape
    d = HEAD_DIM
    chips, part = keep_ref.shape[:2]
    codes = None
    for k in range(count):
        a = jnp.concatenate([blocks[r][:, k * d : (k + 1) * d] for r in range(4)], axis=1)
        product = lax.dot_general(a, weights[k][:cols, :], (((1,), (1,)), ((), ())), preferred_element_type=F32)
        terms = lax.dot_general(a, weights[k][cols:, :], (((1,), (1,)), ((), ())), preferred_element_type=F32)
        if k == 0:
            acc_ref[...] = product
            codes = terms
        else:
            acc_ref[...] += product
            codes = codes + terms
    row = lax.broadcasted_iota(jnp.int32, (rows, 1), 0)
    places = (row // part) * (4 * part) + (plane(BEFORE, z) if before else z) * part + row % part
    prompt, _ = prompt_of(places, lengths_ref, prompts)
    lane = lax.broadcasted_iota(jnp.int32, codes.shape, 1)
    codes = jnp.where(lane // RANK == prompt, codes, 0.0).astype(BF16)
    acc_ref[...] += jnp.dot(codes, up_ref[...], preferred_element_type=F32)
    for i in range(chips):
        mine = pl.multiple_of(i * 2 * part + core * part, part)
        theirs = pl.multiple_of(i * 2 * part + (1 - core) * part, part)
        keep_ref[i] = acc_ref[pl.ds(mine, part), :]
        send_ref[i] = acc_ref[pl.ds(theirs, part), :].astype(BF16)


def output(lengths, blocks, weights, up, before, after):
    rows = blocks[0].shape[0]
    cols = up.shape[1]
    shape = (CHIPS, rows // (2 * CHIPS), cols)
    return call(
        functools.partial(output_kernel, before, len(weights), lengths.shape[0]),
        (lengths, *blocks, *weights, up),
        [SMEM] + [VMEM] * (5 + len(weights)),
        (jax.ShapeDtypeStruct(shape, F32), jax.ShapeDtypeStruct(shape, BF16)),
        after,
        scratch=[pltpu.VMEM((rows, cols), F32)],
        out_specs=(VMEM, VMEM), name="output",
        flops=2 * rows * 512 * len(weights) * cols, moved=2048 * cols * 2 + rows * 2048 * 2 + rows * cols * 3,
    )


def fold_kernel(*refs):
    total = refs[0][...]
    for ref in refs[1:-1]:
        total = total + ref[...].astype(F32)
    refs[-1][...] = total.astype(BF16)


def fold(keep, *got):
    return call(
        fold_kernel, (keep, *got), [VMEM] * (1 + len(got)), jax.ShapeDtypeStruct(keep.shape, BF16),
        out_specs=VMEM, name="fold", flops=keep.size, moved=keep.size * 8,
    )


def close_kernel(stream_ref, gain_ref, *refs):
    pieces = refs[:4]
    out_ref = refs[4]
    z = lax.axis_index("narrow")
    part = pieces[0].shape[0]
    gain = gain_ref[...].astype(F32)
    for k in range(4):
        at = pl.multiple_of(jnp.bitwise_and(z - k + 4, 3) * part, part)
        rows = pl.ds(at, part)
        out_ref[rows, :] = (stream_ref[rows, :].astype(F32) + pieces[k][...].astype(F32) * gain).astype(BF16)


def close(stream, gain, pieces):
    return call(
        close_kernel, (stream, gain[None, :], *pieces), [VMEM] * 6,
        jax.ShapeDtypeStruct(stream.shape, BF16),
        out_specs=VMEM, name="close", flops=stream.size * 3, moved=stream.size * 6,
    )


def per_device_heads(
    residual,
    pre_gain,
    query_weight,
    key_weight,
    value_weight,
    output_weight,
    adapter_down,
    adapter_up_query,
    adapter_up_key,
    adapter_up_value,
    adapter_down_out,
    adapter_up_out,
    post_gain,
    sink_logits,
    prompt_lengths,
    prompt_adapters,
):
    tok, features = residual.shape
    depth = features // CHIPS
    own_rows = query_weight.shape[0]
    prompts = prompt_lengths.shape[0]
    d = HEAD_DIM
    me = lax.axis_index("wide")
    z = lax.axis_index("narrow")
    core = me & 1
    chip = me >> 1
    wide = 2 * CHIPS
    tokens = tok * wide

    flip = lambda bits: [(i, i ^ bits) for i in range(wide)]
    across = flip(1)
    first_leg = [(i, i ^ (2 if i % 2 == 0 else 4)) for i in range(wide)]
    second_leg = [(i, i ^ (4 if i % 2 == 0 else 2)) for i in range(wide)]
    shift = lambda k: [(i, (i + k) % 4) for i in range(4)]
    to_next = [(i, NEXT[i]) for i in range(4)]
    to_second = [(i, 3 - i) for i in range(4)]
    to_before = [(i, BEFORE[i]) for i in range(4)]
    zflip = lambda bits: [(i, i ^ bits) for i in range(4)]

    _, _, position = token_layout(prompt_lengths, tokens, jnp.int32(0))
    half = d // 2
    exponent = jnp.arange(half, dtype=F32) * (2.0 / d)
    frequency = jnp.power(jnp.float32(rotary_base), -exponent)
    angle = position.astype(F32)[:, None] * frequency[None, :]
    cosine, sine = jnp.cos(angle), jnp.sin(angle)
    cosine = jnp.concatenate([cosine, cosine], axis=1)
    sine = jnp.concatenate([-sine, sine], axis=1)

    down = adapter_down.T
    down_other = lax.ppermute(down, "narrow", zflip(1))
    first, second, own = norm(residual, pre_gain, 4, ())
    w_mine, w_theirs = arrange(query_weight, key_weight, value_weight, output_weight.T, (own,))
    first = lax.ppermute(first, "wide", first_leg)
    second = lax.ppermute(second, "wide", second_leg)
    third = lax.ppermute(first[tok:], "wide", second_leg)
    pieces = (first, third, second, own)

    pack = pick(prompt_adapters, down, down_other, adapter_up_out, (w_mine,))
    up, out_down = ups(
        prompt_adapters, adapter_up_query, adapter_up_key, adapter_up_value, adapter_down_out, (own,)
    )
    w, ring0 = stack(w_mine, lax.ppermute(w_theirs, "wide", across), out_down, (up,))
    pack = merge(pack, lax.ppermute(pack, "narrow", zflip(2)), (w, cosine, sine))
    n_down = 3 * prompts * RANK
    up_out = pack[n_down:]
    up_out = up_out + lax.ppermute(up_out, "narrow", zflip(1))
    pack = join(pack[:n_down], lax.ppermute(pack[:n_down], "wide", across))
    ring1 = lax.ppermute(ring0, "narrow", to_next)

    tables = (cosine, sine)
    part = tok // 4
    sends, keeps, ones, twos, mine, other = [], [], [], [], [], []

    def product(chunk, after, carry=()):
        send, keep, carried = project(prompt_lengths, pieces, w, pack, up, chunk, after, carry)
        sends.append(send)
        keeps.append(keep)
        ones.append(lax.ppermute(send, "wide", first_leg))
        return carried

    def pass_on(chunk, after, carry=()):
        out, carried = onward(keeps[chunk], ones[chunk], after, carry)
        twos.append(lax.ppermute(out, "wide", second_leg))
        return (out, *carried)

    def rotate_chunk(chunk, after):
        own, send = finish(keeps[chunk], ones[chunk], twos[chunk], tables, chunk, after)
        mine.append(own)
        other.append(lax.ppermute(send, "wide", across))
        return own

    def attend_chunk(chunk, after, before=(), carry=()):
        return attend(prompt_lengths, sink_logits, mine, other, chunk, after, before, carry)

    def gather(near0):
        near1 = lax.ppermute(near0, "wide", first_leg)
        near2 = lax.ppermute(near0, "wide", second_leg)
        return near0, near1, near2, lax.ppermute(near1, "wide", second_leg)

    product(0, ())
    for chunk in range(1, CHUNKS):
        product(chunk, (sends[-1],))
    up_out = join(up_out, lax.ppermute(up_out, "wide", across), (sends[-1],))
    (out0,) = pass_on(0, (sends[-1],))
    (out1,) = pass_on(1, (out0,))
    q0 = rotate_chunk(0, (out1,))
    out2, ring1 = pass_on(2, (q0,), (ring1,))
    ring2 = lax.ppermute(ring1, "narrow", to_next)
    q1 = rotate_chunk(1, (out2,))
    sub0, _ = attend_chunk(0, (q1,))
    (out3,) = pass_on(3, (sub0[0],))
    q2 = rotate_chunk(2, (out3,))
    sub1, _ = attend_chunk(1, (q2,), sub0)
    sub2, _ = attend_chunk(2, (sub1[0],), sub1)
    q3 = rotate_chunk(3, (sub2[0],))
    sub3, (ring2,) = attend_chunk(3, (q3,), sub2, (ring2,))
    aside = gather(sub3[3])
    keep, send = output(prompt_lengths, aside, (ring0,), up_out, True, ())
    extra = lax.ppermute(fold(keep, lax.ppermute(send, "wide", across)), "narrow", to_before)
    near0 = beside(
        (sub3[0], lax.ppermute(sub3[1], "narrow", to_next), lax.ppermute(sub3[2], "narrow", to_second)), ()
    )
    keep, send = output(prompt_lengths, gather(near0), (ring0, ring1, ring2), up_out, False, ())
    total = fold(keep, lax.ppermute(send, "wide", across), extra)
    rows_of = lambda to: lax.dynamic_index_in_dim(total, to, 0, keepdims=False)
    full = [rows_of(chip)] + [
        lax.ppermute(rows_of(chip ^ delta), "wide", flip(2 * delta)) for delta in (1, 2, 3)
    ]
    full = jnp.stack(full)
    wide_rows = full.astype(F32)
    mean_square = jnp.sum(wide_rows * wide_rows, axis=(0, 2)) / features
    scaled = (wide_rows * lax.rsqrt(mean_square + epsilon)[None, :, None]).astype(BF16)
    finals = []
    for k in range(4):
        piece = lax.dynamic_index_in_dim(scaled, chip ^ ((z + k) & 3), 0, keepdims=False)
        finals.append(piece if k == 0 else lax.ppermute(piece, "narrow", shift(k)))
    own_width = post_gain.shape[0]
    own_stream = lax.dynamic_slice_in_dim(residual, z * own_width, own_width, 1)
    return close(own_stream, post_gain, finals)
def rotate(values, position):
    half = values.shape[-1] // 2
    exponent = jnp.arange(half, dtype=jnp.float32) * (2.0 / values.shape[-1])
    frequency = jnp.power(jnp.float32(rotary_base), -exponent)
    angle = position.astype(jnp.float32)[:, None] * frequency[None, :]
    cosine = jnp.cos(angle)[:, None, :]
    sine = jnp.sin(angle)[:, None, :]
    first_half = values[..., :half]
    second_half = values[..., half:]
    return jnp.concatenate(
        [first_half * cosine - second_half * sine, second_half * cosine + first_half * sine],
        axis=-1,
    )


def select_codes(codes, adapter, projections, adapters):
    count = codes.shape[0]
    width = codes.shape[1] // (adapters * projections)
    shaped = codes.reshape(count, adapters, projections, width)
    onehot = (adapter[:, None] == jnp.arange(adapters, dtype=jnp.int32)[None, :]).astype(
        codes.dtype
    )
    kept = shaped * onehot[:, :, None, None]
    return [kept[:, :, slot, :].reshape(count, adapters * width) for slot in range(projections)]


def add_adapter(partial_out, adapter_cols, offset, own_width):
    current = lax.dynamic_slice_in_dim(partial_out, offset, own_width, 1)
    return lax.dynamic_update_slice_in_dim(partial_out, current + adapter_cols, offset, 1)


def per_device(
    residual,
    pre_gain,
    query_weight,
    key_weight,
    value_weight,
    output_weight,
    adapter_down,
    adapter_up_query,
    adapter_up_key,
    adapter_up_value,
    adapter_down_out,
    adapter_up_out,
    post_gain,
    sink_logits,
    prompt_lengths,
    prompt_adapters,
):
    tok_rows = residual.shape[0]
    first = lax.axis_index("wide") * tok_rows
    member, prompt, position = token_layout(prompt_lengths, tok_rows, first)
    adapter = jnp.sum(member * prompt_adapters[None, :], axis=1)
    stream = residual.astype(jnp.float32)
    scale_rows = lax.rsqrt(jnp.mean(stream * stream, axis=1, keepdims=True) + epsilon)
    normed = (stream * scale_rows * pre_gain.astype(jnp.float32)[None, :]).astype(jnp.bfloat16)
    query_cols = query_weight.shape[1]
    key_cols = key_weight.shape[1]
    pieces = (
        lax.all_gather(query_weight, "wide", axis=0, tiled=True),
        lax.all_gather(key_weight, "wide", axis=0, tiled=True),
        lax.all_gather(value_weight, "wide", axis=0, tiled=True),
        lax.all_gather(adapter_down, "wide", axis=0, tiled=True),
    )
    query_part, key_part, value_part, code_part = tuple(
        (jnp.dot(normed, piece, preferred_element_type=jnp.float32) for piece in pieces)
    )
    codes = lax.all_gather(code_part.astype(jnp.bfloat16), "narrow", axis=1, tiled=True)
    chosen = select_codes(codes, adapter, 3, ADAPTERS)
    query = query_part + adapter_scale * jnp.dot(
        chosen[0], adapter_up_query, preferred_element_type=jnp.float32
    )
    key = key_part + adapter_scale * jnp.dot(
        chosen[1], adapter_up_key, preferred_element_type=jnp.float32
    )
    value = value_part + adapter_scale * jnp.dot(
        chosen[2], adapter_up_value, preferred_element_type=jnp.float32
    )
    local_heads = query_cols // HEAD_DIM
    local_kv = key_cols // HEAD_DIM
    group = local_heads // local_kv
    queries = (
        rotate(query.reshape(tok_rows, local_heads, HEAD_DIM), position)
        .astype(jnp.bfloat16)
        .reshape(tok_rows, local_kv, group, HEAD_DIM)
    )
    keys = rotate(key.reshape(tok_rows, local_kv, HEAD_DIM), position).astype(jnp.bfloat16)
    values = value.astype(jnp.bfloat16).reshape(tok_rows, local_kv, HEAD_DIM)
    sinks = sink_logits.reshape(local_kv, group)
    own_places = first + jnp.arange(tok_rows, dtype=jnp.int32)
    start_top = jnp.broadcast_to(sinks[None, :, :], (tok_rows, local_kv, group))
    start_total = jnp.ones((tok_rows, local_kv, group), jnp.float32)
    start_sum = jnp.zeros((tok_rows, local_kv, group, HEAD_DIM), jnp.float32)
    top = start_top
    total = start_total
    summed_values = start_sum
    piece_keys = lax.all_gather(keys, "wide", axis=0, tiled=True)
    piece_values = lax.all_gather(values, "wide", axis=0, tiled=True)
    count = piece_keys.shape[0]
    unused, key_prompt, unused_position = token_layout(prompt_lengths, count, jnp.int32(0))
    key_places = jnp.arange(count, dtype=jnp.int32)
    allowed = jnp.logical_and(
        prompt[:, None] == key_prompt[None, :], own_places[:, None] >= key_places[None, :]
    )[:, None, None, :]
    scores = (
        jnp.einsum("qgjd,kgd->qgjk", queries, piece_keys, preferred_element_type=jnp.float32)
        * score_scale
    )
    scores = jnp.where(allowed, scores, -1e30)
    fresh = jnp.maximum(top, jnp.max(scores, axis=-1))
    factor = jnp.exp(top - fresh)
    weights = jnp.where(allowed, jnp.exp(scores - fresh[..., None]), 0.0)
    total = total * factor + jnp.sum(weights, axis=-1)
    update = jnp.einsum(
        "qgjk,kgd->qgjd",
        weights.astype(jnp.bfloat16),
        piece_values,
        preferred_element_type=jnp.float32,
    )
    top, total, summed_values = (fresh, total, summed_values * factor[..., None] + update)
    attended = (
        (summed_values / total[..., None])
        .reshape(tok_rows, local_heads * HEAD_DIM)
        .astype(jnp.bfloat16)
    )
    code_terms = jnp.dot(attended, adapter_down_out, preferred_element_type=jnp.float32)
    codes_out = lax.psum(code_terms.astype(jnp.bfloat16), "narrow")
    chosen_out = select_codes(codes_out, adapter, 1, ADAPTERS)[0]
    adapter_cols = adapter_scale * jnp.dot(
        chosen_out, adapter_up_out, preferred_element_type=jnp.float32
    )
    own_width = adapter_up_out.shape[1]
    offset = lax.axis_index("narrow") * own_width
    partial_out = jnp.dot(
        attended,
        lax.all_gather(output_weight, "wide", axis=1, tiled=True),
        preferred_element_type=jnp.float32,
    )
    partial_out = add_adapter(partial_out, adapter_cols, offset, own_width)
    whole = lax.psum(partial_out.astype(jnp.bfloat16), "narrow").astype(jnp.float32)
    mean_square = jnp.mean(whole * whole, axis=1)
    projected = lax.dynamic_slice_in_dim(whole, offset, own_width, 1)
    factor_rows = lax.rsqrt(mean_square + epsilon)
    own_stream = lax.dynamic_slice_in_dim(stream, offset, own_width, 1)
    mixed = own_stream + projected * factor_rows[:, None] * post_gain.astype(jnp.float32)[None, :]
    return mixed.astype(jnp.bfloat16)


def fits(mesh):
    return mesh.shape["wide"] == 2 * CHIPS and mesh.shape["narrow"] == 4


def solution(mesh):
    return jax.shard_map(
        per_device_heads if fits(mesh) else per_device,
        mesh=mesh,
        in_specs=(
            P("wide", None),
            P(),
            P("wide", "narrow"),
            P("wide", "narrow"),
            P("wide", "narrow"),
            P("narrow", "wide"),
            P("wide", "narrow"),
            P(None, "narrow"),
            P(None, "narrow"),
            P(None, "narrow"),
            P("narrow", None),
            P(None, "narrow"),
            P("narrow"),
            P("narrow"),
            P(),
            P(),
        ),
        out_specs=P("wide", "narrow"),
        check_vma=False,
    )
```

```python
import functools

import jax
import jax.numpy as jnp
from jax import lax
from jax.experimental import pallas as pl
from jax.experimental.pallas import tpu as pltpu
from jax.sharding import PartitionSpec as P

HEAD_DIM = 128
ADAPTERS = 16
RANK = 16

epsilon = 1e-06
adapter_scale = 0.5
rotary_base = 10000.0
score_scale = 1.0 / 12.0

CHIPS = 4
CHUNKS = 2
SPAN = CHIPS // CHUNKS
STEP = 256
LOG2E = 1.4426950408889634
F32 = jnp.float32
BF16 = jnp.bfloat16
SMEM = pl.BlockSpec(memory_space=pltpu.SMEM)
VMEM = pl.BlockSpec(memory_space=pltpu.VMEM)
ANY = pl.BlockSpec(memory_space=pl.ANY)
HBM = pl.BlockSpec(memory_space=pltpu.HBM)


def token_layout(prompt_lengths, count, first):
    ends = jnp.cumsum(prompt_lengths, dtype=jnp.int32)
    starts = ends - prompt_lengths
    places = first + jnp.arange(count, dtype=jnp.int32)
    member = jnp.logical_and(
        places[:, None] >= starts[None, :], places[:, None] < ends[None, :]
    ).astype(jnp.int32)
    labels = jnp.arange(prompt_lengths.shape[0], dtype=jnp.int32)
    prompt = jnp.sum(member * labels[None, :], axis=1)
    position = places - jnp.sum(member * starts[None, :], axis=1)
    return (member, prompt, position)


def call(kernel, operands, specs, out_shape, after=(), scratch=(), name=None, flops=0, moved=0, transcendentals=0, grant=24, **more):
    n = len(after)
    return pl.pallas_call(
        lambda *refs: kernel(*refs[n:]),
        out_shape=out_shape,
        in_specs=[ANY] * n + list(specs),
        scratch_shapes=list(scratch),
        name=name,
        compiler_params=pltpu.CompilerParams(vmem_limit_bytes=grant * 1024 * 1024),
        cost_estimate=pl.CostEstimate(flops=flops, bytes_accessed=moved, transcendentals=transcendentals),
        **more,
    )(*after, *operands)


def prompt_of(places, lengths_ref, prompts):
    end = jnp.int32(0)
    prompt = jnp.zeros_like(places)
    start = jnp.zeros_like(places)
    for p in range(prompts - 1):
        end = end + lengths_ref[p]
        past = places >= end
        prompt = jnp.where(past, p + 1, prompt)
        start = jnp.where(past, end, start)
    return prompt, start


def order(chip, core):
    return (chip ^ (1 + core), chip ^ 3, chip ^ (2 - core), chip)


NEXT = (1, 3, 0, 2)
BEFORE = (2, 0, 3, 1)


def plane(table, z):
    return jnp.where(z == 0, table[0], jnp.where(z == 1, table[1], jnp.where(z == 2, table[2], table[3])))


def near(chip, core):
    return (chip, chip ^ (1 + core), chip ^ (2 - core), chip ^ 3)


def norm_kernel(steps, x_hbm, gain_ref, *refs):
    (first_ref, second_ref, own_ref), (x_ref, y_ref, in_sems, out_sems) = refs[:3], refs[3:]
    me = lax.axis_index("wide")
    chip, core = lax.shift_right_logical(me, 1), me & 1
    depth = own_ref.shape[1]
    rows = x_ref.shape[0]
    step = rows // steps
    loads = [
        pltpu.make_async_copy(x_hbm.at[pl.ds(i * step, step), :], x_ref.at[pl.ds(i * step, step), :], in_sems.at[i])
        for i in range(steps)
    ]
    for load in loads:
        load.start()
    gain = gain_ref[...].astype(F32).reshape(1, -1)
    copies = []
    for i in range(steps):
        loads[i].wait()
        at = i * step
        x = x_ref[at : at + step, :].astype(F32)
        scale = lax.rsqrt(jnp.sum(x * x, axis=1, keepdims=True) / x.shape[1] + epsilon)
        y_ref[at : at + step, :] = (x * scale * gain).astype(BF16)
        for to, out, base in zip(order(chip, core), (first_ref, first_ref, second_ref, own_ref), (0, rows, 0, 0)):
            source = y_ref.at[pl.ds(at, step), pl.ds(pl.multiple_of(to * depth, 128), depth)]
            target = out.at[pl.ds(base + at, step), :]
            copies.append(pltpu.make_async_copy(source, target, out_sems.at[len(copies)]))
            copies[-1].start()
    for copy in copies:
        copy.wait()


def norm(x, gain, steps, after):
    rows, cols = x.shape
    depth = cols // CHIPS
    shape = jax.ShapeDtypeStruct((rows, depth), x.dtype)
    return call(
        functools.partial(norm_kernel, steps), (x, gain), [HBM, VMEM],
        (jax.ShapeDtypeStruct((2 * rows, depth), x.dtype), shape, shape), after,
        scratch=[
            pltpu.VMEM((rows, cols), BF16),
            pltpu.VMEM((rows, cols), BF16),
            pltpu.SemaphoreType.DMA((steps,)),
            pltpu.SemaphoreType.DMA((4 * steps,)),
        ],
        out_specs=(ANY,) * 3, name="norm", grant=60, flops=x.size * 4, moved=x.size * 4,
    )


def arrange_kernel(q_hbm, k_hbm, v_hbm, o_hbm, theirs_ref, q_ref, k_ref, v_ref, o_ref, in_sems, sems):
    me = lax.axis_index("wide")
    chip, own = lax.shift_right_logical(me, 1), me & 1
    d = HEAD_DIM
    loads = [
        pltpu.make_async_copy(source, target, in_sems.at[i])
        for i, (source, target) in enumerate(
            ((q_hbm, q_ref), (k_hbm, k_ref), (v_hbm, v_ref), (o_hbm, o_ref))
        )
    ]
    for one in loads:
        one.start()
    copies = []
    for load, ref, part in zip(loads, (q_ref, k_ref, v_ref, o_ref), range(4)):
        load.wait()
        for source, target in column_copies(ref, theirs_ref, part, chip, 1 - own):
            copies.append(pltpu.make_async_copy(source, target, sems.at[len(copies)]))
            copies[-1].start()
    for one in copies:
        one.wait()


def column_copies(ref, out, part, chip, core):
    d = HEAD_DIM
    if part == 3:
        pairs = [((2 * source + core) * d, (4 * CHIPS + place) * d) for place, source in enumerate(near(chip, core))]
        width = d
    else:
        width, at = ((2 * d, 0), (d, 2 * d), (d, 3 * d))[part]
        pairs = [(to * width, 4 * place * d + at) for place, to in enumerate(order(chip, core))]
    return [
        (ref.at[:, pl.ds(pl.multiple_of(a, d), width)], out.at[:, pl.ds(b, width)]) for a, b in pairs
    ]


def arrange(q, k, v, o, after):
    return call(
        arrange_kernel, (q, k, v, o), [HBM] * 4,
        jax.ShapeDtypeStruct((q.shape[0], 5 * CHIPS * HEAD_DIM), BF16), after,
        scratch=[pltpu.VMEM(x.shape, BF16) for x in (q, k, v, o)]
        + [pltpu.SemaphoreType.DMA((4,)), pltpu.SemaphoreType.DMA((16,))],
        out_specs=ANY, name="arrange", grant=60, moved=q.size * 16,
    )


def lower_kernel(x_ref, out_ref, sem):
    rows = out_ref.shape[0]
    copy = pltpu.make_async_copy(x_ref.at[pl.ds(x_ref.shape[0] - rows, rows), :], out_ref, sem)
    copy.start()
    copy.wait()


def lower(x, after):
    return call(
        lower_kernel, (x,), [ANY], jax.ShapeDtypeStruct((x.shape[0] // 2, x.shape[1]), x.dtype), after,
        scratch=[pltpu.SemaphoreType.DMA(())], out_specs=ANY, name="lower", moved=x.size * 2,
    )


def choose(shape, row_prompt, chosen_ref, prompts):
    adapter = jnp.zeros(shape, jnp.int32)
    for p in range(prompts):
        adapter = jnp.where(row_prompt == p, chosen_ref[p], adapter)
    return adapter


def pick_kernel(prompts, chosen_ref, down_hbm, other_hbm, upo_hbm, pack_ref, down_ref, other_ref, upo_ref, sems):
    me, z = lax.axis_index("wide"), lax.axis_index("narrow")
    chip = lax.shift_right_logical(me, 1)
    core = me & 1
    n_codes = prompts * RANK
    local = down_ref.shape[0] // (3 * RANK)
    rows = down_ref.shape[1]
    copies = [
        pltpu.make_async_copy(down_hbm, down_ref, sems.at[prompts]),
        pltpu.make_async_copy(other_hbm, other_ref, sems.at[prompts + 1]),
    ]
    for p in range(prompts):
        at = pl.ds(pl.multiple_of(chosen_ref[p] * RANK, RANK), RANK)
        copies.append(pltpu.make_async_copy(upo_hbm.at[at, :], upo_ref.at[pl.ds(p * RANK, RANK), :], sems.at[p]))
    for copy in copies:
        copy.start()
    shape = (3 * n_codes, down_ref.shape[0])
    row = lax.broadcasted_iota(jnp.int32, shape, 0)
    col = lax.broadcasted_iota(jnp.int32, shape, 1)
    adapter = choose(shape, (row % n_codes) // RANK, chosen_ref, prompts)

    def pick_of(plane_at):
        wanted = (adapter - plane_at * local) * (3 * RANK) + (row // n_codes) * RANK + row % RANK
        inside = jnp.logical_and(adapter >= plane_at * local, adapter < (plane_at + 1) * local)
        return jnp.where(jnp.logical_and(inside, col == wanted), 1.0, 0.0).astype(BF16)

    mine, theirs = pick_of(z), pick_of(z ^ 1)
    for copy in copies:
        copy.wait()
    down = jnp.dot(mine, down_ref[...], preferred_element_type=F32)
    down = down + jnp.dot(theirs, other_ref[...], preferred_element_type=F32)
    pack_ref[: 3 * n_codes, :] = down.astype(BF16)
    both = upo_ref[...].astype(F32) * adapter_scale
    part = jnp.where(core == 0, both[:, :rows], both[:, rows:])
    pack_ref[3 * n_codes :, :] = jnp.where(z == chip, part, 0.0).astype(BF16)


def pick(chosen, down, other, upo, after):
    prompts = chosen.shape[0]
    n_codes = prompts * RANK
    return call(
        functools.partial(pick_kernel, prompts), (chosen, down, other, upo), [SMEM, HBM, HBM, HBM],
        jax.ShapeDtypeStruct((4 * n_codes, down.shape[1]), BF16),
        after,
        scratch=[
            pltpu.VMEM(down.shape, BF16),
            pltpu.VMEM(down.shape, BF16),
            pltpu.VMEM((n_codes, upo.shape[1]), BF16),
            pltpu.SemaphoreType.DMA((prompts + 2,)),
        ],
        out_specs=VMEM, name="pick", grant=60, flops=down.size * 400, moved=down.size * 6,
    )


def merge_kernel(a_ref, b_ref, out_ref):
    out_ref[...] = (a_ref[...].astype(F32) + b_ref[...].astype(F32)).astype(out_ref.dtype)


def merge(a, b, after=()):
    return call(
        merge_kernel, (a, b), [VMEM, VMEM], jax.ShapeDtypeStruct(a.shape, BF16), after,
        out_specs=VMEM, name="merge", flops=a.size, moved=a.size * 6,
    )


def ups_kernel(prompts, chosen_ref, upq_ref, upk_ref, upv_ref, ado_ref, up_ref, out_ref):
    me = lax.axis_index("wide")
    chip = lax.shift_right_logical(me, 1)
    core = me & 1
    d = HEAD_DIM
    n_codes = prompts * RANK
    up_ref[...] = jnp.zeros_like(up_ref)
    for p in range(prompts):
        rows = pl.ds(pl.multiple_of(chosen_ref[p] * RANK, RANK), RANK)
        for place, to in enumerate(order(chip, core)):
            for slot, (ref, width, at) in enumerate(((upq_ref, 2 * d, 0), (upk_ref, d, 2 * d), (upv_ref, d, 3 * d))):
                part = ref[rows, pl.ds(pl.multiple_of(to * width, d), width)].astype(F32) * adapter_scale
                first = slot * n_codes + p * RANK
                left = 4 * place * d + at
                up_ref[first : first + RANK, left : left + width] = part.astype(BF16)
    shape = (n_codes, ado_ref.shape[1])
    row = lax.broadcasted_iota(jnp.int32, shape, 0)
    col = lax.broadcasted_iota(jnp.int32, shape, 1)
    adapter = choose(shape, row // RANK, chosen_ref, prompts)
    pick = jnp.where(col == adapter * RANK + row % RANK, 1.0, 0.0).astype(BF16)
    for place, source in enumerate(near(chip, core)):
        block = ado_ref[pl.ds(pl.multiple_of((2 * source + core) * d, d), d), :]
        part = lax.dot_general(pick, block, (((1,), (1,)), ((), ())), preferred_element_type=F32)
        out_ref[:, place * d : (place + 1) * d] = part.astype(BF16)


def ups(chosen, upq, upk, upv, ado, after):
    prompts = chosen.shape[0]
    n_codes = prompts * RANK
    return call(
        functools.partial(ups_kernel, prompts), (chosen, upq, upk, upv, ado), [SMEM] + [VMEM] * 4,
        (
            jax.ShapeDtypeStruct((3 * n_codes, 2 * upq.shape[1]), BF16),
            jax.ShapeDtypeStruct((n_codes, CHIPS * HEAD_DIM), BF16),
        ),
        after, out_specs=(VMEM,) * 2, name="ups", flops=upq.size * 100, moved=upq.size * 6,
    )


def stack_kernel(q_ref, k_ref, v_ref, o_ref, got_ref, down_ref, w_ref, ring_ref, sems):
    me = lax.axis_index("wide")
    chip, core = lax.shift_right_logical(me, 1), me & 1
    rows = got_ref.shape[0]
    cols = w_ref.shape[1]
    width = ring_ref.shape[1]
    copies = []

    def copy(source, target):
        copies.append(pltpu.make_async_copy(source, target, sems.at[len(copies)]))
        copies[-1].start()

    mine = pl.ds(pl.multiple_of(core * rows, 16), rows)
    theirs = pl.ds(pl.multiple_of((1 - core) * rows, 16), rows)
    for part, ref in enumerate((q_ref, k_ref, v_ref)):
        for source, target in column_copies(ref, w_ref.at[mine, :], part, chip, core):
            copy(source, target)
    d = HEAD_DIM
    for place, source in enumerate(near(chip, core)):
        at = pl.multiple_of((2 * source + core) * d, d)
        copy(o_ref.at[:, pl.ds(at, d)], ring_ref.at[mine, pl.ds(place * d, d)])
    copy(got_ref.at[:, pl.ds(0, cols)], w_ref.at[theirs, :])
    copy(got_ref.at[:, pl.ds(cols, width)], ring_ref.at[theirs, :])
    copy(down_ref, ring_ref.at[pl.ds(2 * rows, down_ref.shape[0]), :])
    for one in copies:
        one.wait()


def stack(q, k, v, o, got, down, after):
    rows, cols = got.shape
    width = down.shape[1]
    return call(
        stack_kernel, (q, k, v, o, got, down), [ANY] * 6,
        (
            jax.ShapeDtypeStruct((2 * rows, cols - width), got.dtype),
            jax.ShapeDtypeStruct((2 * rows + down.shape[0], width), got.dtype),
        ),
        after,
        scratch=[pltpu.SemaphoreType.DMA((19,))], out_specs=(ANY, ANY), name="stack", moved=rows * cols * 8,
    )


def join_kernel(mine_ref, other_ref, out_ref):
    core = lax.axis_index("wide") & 1
    mine, other = mine_ref[...].astype(F32), other_ref[...].astype(F32)
    left = jnp.where(core == 0, mine, other)
    right = jnp.where(core == 0, other, mine)
    out_ref[...] = jnp.concatenate([left, right], axis=1).astype(out_ref.dtype)


def join(mine, other, after=()):
    rows, cols = mine.shape
    return call(
        join_kernel, (mine, other), [VMEM, VMEM], jax.ShapeDtypeStruct((rows, 2 * cols), mine.dtype), after,
        out_specs=VMEM, name="join", flops=rows * cols * 4, moved=rows * cols * 8,
    )


def project_kernel(chunk, prompts, lengths_ref, *refs):
    x_refs = refs[:4]
    w_ref, pack_ref, up_ref = refs[4:7]
    send_ref, keep_ref, x_ref, sem = refs[-4:]
    me = lax.axis_index("wide")
    chip = lax.shift_right_logical(me, 1)
    core = me & 1
    rows = x_ref.shape[0]
    tok = rows // SPAN
    half = send_ref.shape[1]
    n_codes = prompts * RANK
    for i in range(SPAN):
        for k, held in enumerate((chip ^ (1 + core), chip ^ 3, chip ^ (2 - core), chip)):

            @pl.when(held == SPAN * chunk + i)
            def _():
                pltpu.make_async_copy(
                    x_refs[k].at[pl.ds(0, tok), :], x_ref.at[pl.ds(i * tok, tok), :], sem.at[i]
                ).start()

    for i in range(SPAN):
        pltpu.make_async_copy(x_refs[3], x_ref.at[pl.ds(i * tok, tok), :], sem.at[i]).wait()
    x = x_ref[...]
    codes = lax.dot_general(
        x, pack_ref[...], (((1,), (1,)), ((), ())), preferred_element_type=F32
    )
    row = lax.broadcasted_iota(jnp.int32, (rows, 1), 0)
    places = (2 * (SPAN * chunk + row // tok) + core) * tok + row % tok
    prompt, _ = prompt_of(places, lengths_ref, prompts)
    lane = lax.broadcasted_iota(jnp.int32, codes.shape, 1)
    owner = (lane % n_codes) // RANK
    codes = jnp.where(owner == prompt, codes, 0.0).astype(BF16)
    for part, out in ((0, send_ref), (1, keep_ref)):
        cols = pl.ds(part * half, half)
        product = jnp.dot(x, w_ref[:, cols], preferred_element_type=F32)
        product = product + jnp.dot(codes, up_ref[:, cols], preferred_element_type=F32)
        out[...] = product.astype(out.dtype)


def project(lengths, pieces, w, pack, up, chunk, after, carry=()):
    rows, depth = SPAN * pieces[3].shape[0], pieces[3].shape[1]
    half = w.shape[1] // 2
    n = len(after) + 8
    out = call(
        functools.partial(project_kernel, chunk, lengths.shape[0]),
        (lengths, *pieces, w, pack, up, *carry),
        [SMEM] + [ANY] * 4 + [VMEM] * 3 + [ANY] * len(carry),
        tuple(jax.ShapeDtypeStruct(c.shape, c.dtype) for c in carry)
        + (jax.ShapeDtypeStruct((rows, half), BF16), jax.ShapeDtypeStruct((rows, half), F32)),
        after,
        scratch=[pltpu.VMEM((rows, depth), BF16), pltpu.SemaphoreType.DMA((SPAN,))],
        out_specs=(ANY,) * len(carry) + (VMEM, VMEM), name="project",
        input_output_aliases={n + i: i for i in range(len(carry))},
        flops=2 * rows * depth * w.shape[1], moved=rows * depth * 2 + w.size * 2 + rows * half * 6,
    )
    return out[-2], out[-1], out[:-2]


def onward_kernel(keep_ref, first_ref, *refs):
    out_ref = refs[-1]
    own = out_ref.shape[1]
    out_ref[...] = (keep_ref[:, :own] + first_ref[:, own:].astype(F32)).astype(BF16)


def onward(keep, first, after, carry=()):
    rows, cols = keep.shape
    n = len(after) + 2
    out = call(
        onward_kernel, (keep, first, *carry), [VMEM, VMEM] + [ANY] * len(carry),
        tuple(jax.ShapeDtypeStruct(c.shape, c.dtype) for c in carry)
        + (jax.ShapeDtypeStruct((rows, cols // 2), BF16),),
        after, out_specs=(ANY,) * len(carry) + (VMEM,), name="onward",
        input_output_aliases={n + i: i for i in range(len(carry))},
        flops=rows * cols, moved=rows * cols * 4,
    )
    return out[-1], out[:-1]


def finish_kernel(chunk, keep_ref, first_ref, second_ref, cos_ref, sin_ref, *refs):
    own_ref, send_ref = refs[-2:]
    tok = own_ref.shape[0] // SPAN
    d = HEAD_DIM
    own = keep_ref.shape[1] // 2
    core = lax.axis_index("wide") & 1
    for i in range(SPAN):
        at = pl.ds(pl.multiple_of((2 * (SPAN * chunk + i) + core) * tok, tok), tok)
        rows = slice(i * tok, (i + 1) * tok)
        cosine, sine = cos_ref[at, :], sin_ref[at, :]
        total = keep_ref[rows, own:] + first_ref[rows, :own].astype(F32) + second_ref[rows, :].astype(F32)
        q0, q1, k = (
            x * cosine + pltpu.roll(x, d // 2, 1) * sine for x in (total[:, n * d : (n + 1) * d] for n in range(3))
        )
        q0, q1 = q0 * (score_scale * LOG2E), q1 * (score_scale * LOG2E)
        own_ref[rows, :d] = jnp.where(core == 0, q0, q1).astype(BF16)
        send_ref[rows, :d] = jnp.where(core == 0, q1, q0).astype(BF16)
        both = jnp.concatenate([k, total[:, 3 * d :]], axis=1).astype(BF16)
        own_ref[rows, d:] = both
        send_ref[rows, d:] = both


def finish(keep, first, second, tables, chunk, after, carry=()):
    rows = keep.shape[0]
    shape = jax.ShapeDtypeStruct((rows, 3 * HEAD_DIM), BF16)
    n = len(after) + 5
    out = call(
        functools.partial(finish_kernel, chunk),
        (keep, first, second, *tables, *carry), [VMEM] * 5 + [ANY] * len(carry),
        tuple(jax.ShapeDtypeStruct(c.shape, c.dtype) for c in carry) + (shape, shape), after,
        out_specs=(ANY,) * len(carry) + (VMEM, VMEM), name="finish",
        input_output_aliases={n + i: i for i in range(len(carry))},
        flops=rows * 2048, moved=rows * 8192,
    )
    return out[-2], out[-1], out[:-2]


def attend_kernel(chunk, prompts, n_before, n_carry, lengths_ref, sink_ref, *refs):
    count = chunk + 1
    mine_refs, other_refs = refs[:count], refs[count : 2 * count]
    befores = refs[2 * count : 2 * count + n_before]
    outs = refs[2 * count + n_before + 2 * n_carry :][:4]
    q_ref, k_ref, v_ref, out_ref = refs[-4:]
    step = mine_refs[0].shape[0] // SPAN
    d = HEAD_DIM
    here, z = lax.axis_index("wide"), lax.axis_index("narrow")
    core = here & 1
    for c in range(count):
        for i in range(SPAN):
            mine, other = (refs_of[c][i * step : (i + 1) * step, :] for refs_of in (mine_refs, other_refs))
            for half, block in enumerate((jnp.where(core == 0, mine, other), jnp.where(core == 0, other, mine))):
                at = pl.ds((2 * (SPAN * c + i) + half) * step, step)
                k_ref[at, :] = block[:, d : 2 * d]
                v_ref[at, :] = block[:, 2 * d :]
                if c == chunk:
                    q_ref[(2 * i + half) * step : (2 * i + half + 1) * step, :] = block[:, :d]
    shift = 0
    for k in range(n_before):
        shift = befores[k].shape[0]
        outs[k][:shift, :] = befores[k][...]
    for i in range(SPAN):
        attend_block(
            SPAN * chunk + i, prompts, step, lengths_ref, sink_ref, q_ref.at[pl.ds(2 * i * step, 2 * step), :],
            k_ref, v_ref, out_ref, outs, shift + i * step // 2,
        )


def attend_block(chip, prompts, step, lengths_ref, sink_ref, q_ref, k_ref, v_ref, out_ref, outs, shift):
    d = HEAD_DIM
    here, z = lax.axis_index("wide"), lax.axis_index("narrow")
    top = sink_ref[here] * LOG2E
    to = (z, plane(NEXT, z), 3 - z, plane(BEFORE, z))
    part = step // 4
    rows = 2 * step
    base = chip * rows
    q = q_ref[...]
    places = base + lax.broadcasted_iota(jnp.int32, (rows, 1), 0)
    _, starts = prompt_of(places, lengths_ref, prompts)
    end = jnp.int32(0)
    low = jnp.int32(0)
    high = jnp.int32(0)
    for p in range(prompts - 1):
        end = end + lengths_ref[p]
        low = jnp.where(base >= end, end, low)
        high = jnp.where(base + rows > end, end, high)

    def body(masked):
        def one(i, carry):
            top, total, summed = carry
            at = pl.multiple_of(i * STEP, STEP)
            k = k_ref[pl.ds(at, STEP), :]
            v = v_ref[pl.ds(at, STEP), :]
            scores = lax.dot_general(q, k, (((1,), (1,)), ((), ())), preferred_element_type=F32)
            if masked:
                keys = at + lax.broadcasted_iota(jnp.int32, scores.shape, 1)
                scores = jnp.where(jnp.logical_and(keys >= starts, keys <= places), scores, -1e30)
            fresh = jnp.maximum(top, jnp.max(scores, axis=1, keepdims=True))
            factor = jnp.exp2(top - fresh)
            weights = jnp.exp2(scores - fresh)
            total = total * factor + jnp.sum(weights, axis=1, keepdims=True)
            summed = summed * factor + jnp.dot(weights.astype(BF16), v, preferred_element_type=F32)
            return fresh, total, summed

        return one

    carry = (jnp.full((rows, 1), top, F32), jnp.ones((rows, 1), F32), jnp.zeros((rows, d), F32))
    first = low // STEP
    last = base // STEP
    whole = jnp.minimum((high + STEP - 1) // STEP, last)
    carry = lax.fori_loop(first, whole, body(True), carry)
    carry = lax.fori_loop(whole, last, body(False), carry)
    for i in range(last, (base + rows) // STEP):
        carry = body(True)(i, carry)
    _, total, summed = carry
    out_ref[...] = (summed / total).astype(BF16)
    for block in range(2):
        for k in range(4):
            at = pl.multiple_of(block * step + to[k] * part, part)
            first = shift + block * part
            outs[k][first : first + part, :] = out_ref[pl.ds(at, part), :]


def attend(lengths, sinks, mine, other, chunk, after, before=(), carry=()):
    step = mine[0].shape[0] // SPAN
    d = HEAD_DIM
    count = chunk + 1
    rows = SPAN * step // 2 + (before[0].shape[0] if before else 0)
    n = len(after) + 2 + 2 * count + len(before)
    out = call(
        functools.partial(attend_kernel, chunk, lengths.shape[0], len(before), len(carry)),
        (lengths, sinks, *mine[:count], *other[:count], *before, *carry),
        [SMEM, SMEM] + [VMEM] * (2 * count + len(before)) + [ANY] * len(carry),
        tuple(jax.ShapeDtypeStruct(c.shape, c.dtype) for c in carry)
        + (jax.ShapeDtypeStruct((rows, d), BF16),) * 4,
        after,
        scratch=[pltpu.VMEM((2 * SPAN * step, d), BF16)]
        + [pltpu.VMEM((2 * SPAN * count * step, d), BF16)] * 2
        + [pltpu.VMEM((2 * step, d), BF16)],
        out_specs=(ANY,) * len(carry) + (VMEM,) * 4, name="attend",
        input_output_aliases={n + i: i for i in range(len(carry))},
        flops=2 * SPAN * step * 768 * 4 * d, moved=step * d * 8 * count, transcendentals=2 * SPAN * step * 768,
    )
    return out[len(carry) :], out[: len(carry)]


def beside_kernel(*refs):
    out_ref = refs[-1]
    width = refs[0].shape[1]
    for i, ref in enumerate(refs[:-1]):
        out_ref[:, i * width : (i + 1) * width] = ref[...]


def beside(parts, after):
    rows, cols = parts[0].shape
    return call(
        beside_kernel, parts, [VMEM] * len(parts), jax.ShapeDtypeStruct((rows, cols * len(parts)), BF16), after,
        out_specs=VMEM, name="beside", moved=rows * cols * len(parts) * 4,
    )


def hold_kernel(*refs):
    pass


def hold(arrays, after):
    n = len(after)
    return call(
        hold_kernel, arrays, [ANY] * len(arrays), tuple(jax.ShapeDtypeStruct(a.shape, a.dtype) for a in arrays),
        after, out_specs=(ANY,) * len(arrays), name="hold",
        input_output_aliases={n + i: i for i in range(len(arrays))},
    )


def output_kernel(before, count, prompts, lengths_ref, *refs):
    blocks = refs[:4]
    weights = refs[4 : 4 + count]
    up_ref, keep_ref, send_ref, acc_ref = refs[4 + count :]
    z = lax.axis_index("narrow")
    core = lax.axis_index("wide") & 1
    rows, cols = acc_ref.shape
    d = HEAD_DIM
    chips, part = keep_ref.shape[:2]
    codes = None
    for k in range(count):
        a = jnp.concatenate([blocks[r][:, k * d : (k + 1) * d] for r in range(4)], axis=1)
        product = lax.dot_general(a, weights[k][:cols, :], (((1,), (1,)), ((), ())), preferred_element_type=F32)
        terms = lax.dot_general(a, weights[k][cols:, :], (((1,), (1,)), ((), ())), preferred_element_type=F32)
        if k == 0:
            acc_ref[...] = product
            codes = terms
        else:
            acc_ref[...] += product
            codes = codes + terms
    row = lax.broadcasted_iota(jnp.int32, (rows, 1), 0)
    places = (row // part) * (4 * part) + (plane(BEFORE, z) if before else z) * part + row % part
    prompt, _ = prompt_of(places, lengths_ref, prompts)
    lane = lax.broadcasted_iota(jnp.int32, codes.shape, 1)
    codes = jnp.where(lane // RANK == prompt, codes, 0.0).astype(BF16)
    acc_ref[...] += jnp.dot(codes, up_ref[...], preferred_element_type=F32)
    for i in range(chips):
        mine = pl.multiple_of(i * 2 * part + core * part, part)
        theirs = pl.multiple_of(i * 2 * part + (1 - core) * part, part)
        keep_ref[i] = acc_ref[pl.ds(mine, part), :]
        send_ref[i] = acc_ref[pl.ds(theirs, part), :].astype(BF16)


def output(lengths, blocks, weights, up, before, after):
    rows = blocks[0].shape[0]
    cols = up.shape[1]
    shape = (CHIPS, rows // (2 * CHIPS), cols)
    return call(
        functools.partial(output_kernel, before, len(weights), lengths.shape[0]),
        (lengths, *blocks, *weights, up),
        [SMEM] + [VMEM] * (5 + len(weights)),
        (jax.ShapeDtypeStruct(shape, F32), jax.ShapeDtypeStruct(shape, BF16)),
        after,
        scratch=[pltpu.VMEM((rows, cols), F32)],
        out_specs=(VMEM, VMEM), name="output",
        flops=2 * rows * 512 * len(weights) * cols, moved=2048 * cols * 2 + rows * 2048 * 2 + rows * cols * 3,
    )


def fold_kernel(*refs):
    total = refs[0][...]
    for ref in refs[1:-1]:
        total = total + ref[...].astype(F32)
    refs[-1][...] = total.astype(BF16)


def fold(keep, *got):
    return call(
        fold_kernel, (keep, *got), [VMEM] * (1 + len(got)), jax.ShapeDtypeStruct(keep.shape, BF16),
        out_specs=VMEM, name="fold", flops=keep.size, moved=keep.size * 8,
    )


def close_kernel(stream_ref, gain_ref, *refs):
    pieces = refs[:4]
    out_ref = refs[4]
    z = lax.axis_index("narrow")
    part = pieces[0].shape[0]
    gain = gain_ref[...].astype(F32)
    for k in range(4):
        at = pl.multiple_of(jnp.bitwise_and(z - k + 4, 3) * part, part)
        rows = pl.ds(at, part)
        out_ref[rows, :] = (stream_ref[rows, :].astype(F32) + pieces[k][...].astype(F32) * gain).astype(BF16)


def close(stream, gain, pieces):
    return call(
        close_kernel, (stream, gain[None, :], *pieces), [VMEM] * 6,
        jax.ShapeDtypeStruct(stream.shape, BF16),
        out_specs=VMEM, name="close", flops=stream.size * 3, moved=stream.size * 6,
    )


def per_device_heads(
    residual,
    pre_gain,
    query_weight,
    key_weight,
    value_weight,
    output_weight,
    adapter_down,
    adapter_up_query,
    adapter_up_key,
    adapter_up_value,
    adapter_down_out,
    adapter_up_out,
    post_gain,
    sink_logits,
    prompt_lengths,
    prompt_adapters,
):
    tok, features = residual.shape
    depth = features // CHIPS
    own_rows = query_weight.shape[0]
    prompts = prompt_lengths.shape[0]
    d = HEAD_DIM
    me = lax.axis_index("wide")
    z = lax.axis_index("narrow")
    core = me & 1
    chip = me >> 1
    wide = 2 * CHIPS
    tokens = tok * wide

    flip = lambda bits: [(i, i ^ bits) for i in range(wide)]
    across = flip(1)
    first_leg = [(i, i ^ (2 if i % 2 == 0 else 4)) for i in range(wide)]
    second_leg = [(i, i ^ (4 if i % 2 == 0 else 2)) for i in range(wide)]
    shift = lambda k: [(i, (i + k) % 4) for i in range(4)]
    to_next = [(i, NEXT[i]) for i in range(4)]
    to_second = [(i, 3 - i) for i in range(4)]
    to_before = [(i, BEFORE[i]) for i in range(4)]
    zflip = lambda bits: [(i, i ^ bits) for i in range(4)]

    _, _, position = token_layout(prompt_lengths, tokens, jnp.int32(0))
    half = d // 2
    exponent = jnp.arange(half, dtype=F32) * (2.0 / d)
    frequency = jnp.power(jnp.float32(rotary_base), -exponent)
    angle = position.astype(F32)[:, None] * frequency[None, :]
    cosine, sine = jnp.cos(angle), jnp.sin(angle)
    cosine = jnp.concatenate([cosine, cosine], axis=1)
    sine = jnp.concatenate([-sine, sine], axis=1)

    down = adapter_down.T
    down_other = lax.ppermute(down, "narrow", zflip(1))
    first, second, own = norm(residual, pre_gain, 4, ())
    w_theirs = arrange(query_weight, key_weight, value_weight, output_weight.T, (own,))
    first = lax.ppermute(first, "wide", first_leg)
    second = lax.ppermute(second, "wide", second_leg)
    pack = pick(prompt_adapters, down, down_other, adapter_up_out, (w_theirs,))
    up, out_down = ups(
        prompt_adapters, adapter_up_query, adapter_up_key, adapter_up_value, adapter_down_out, (w_theirs,)
    )
    w, ring0 = stack(
        query_weight, key_weight, value_weight, output_weight.T, lax.ppermute(w_theirs, "wide", across), out_down, (up,)
    )
    third = lax.ppermute(lower(first, (w,)), "wide", second_leg)
    pieces = (first, third, second, own)
    pack = merge(pack, lax.ppermute(pack, "narrow", zflip(2)), (w, cosine, sine))
    n_down = 3 * prompts * RANK
    up_out = pack[n_down:]
    up_out = up_out + lax.ppermute(up_out, "narrow", zflip(1))
    pack = join(pack[:n_down], lax.ppermute(pack[:n_down], "wide", across))
    ring1 = lax.ppermute(ring0, "narrow", to_next)

    tables = (cosine, sine)
    part = tok // 4
    sends, keeps, ones, twos, mine, other = [], [], [], [], [], []

    def product(chunk, after, carry=()):
        send, keep, carried = project(prompt_lengths, pieces, w, pack, up, chunk, after, carry)
        sends.append(send)
        keeps.append(keep)
        ones.append(lax.ppermute(send, "wide", first_leg))
        return carried

    def pass_on(chunk, after, carry=()):
        out, carried = onward(keeps[chunk], ones[chunk], after, carry)
        twos.append(lax.ppermute(out, "wide", second_leg))
        return (out, *carried)

    def rotate_chunk(chunk, after, carry=()):
        own, send, carried = finish(keeps[chunk], ones[chunk], twos[chunk], tables, chunk, after, carry)
        mine.append(own)
        other.append(lax.ppermute(send, "wide", across))
        return (own, *carried)

    def attend_chunk(chunk, after, before=(), carry=()):
        return attend(prompt_lengths, sink_logits, mine, other, chunk, after, before, carry)

    def gather(near0):
        near1 = lax.ppermute(near0, "wide", first_leg)
        near2 = lax.ppermute(near0, "wide", second_leg)
        return near0, near1, near2, lax.ppermute(near1, "wide", second_leg)

    product(0, ())
    product(1, (sends[-1],))
    up_out = join(up_out, lax.ppermute(up_out, "wide", across), (sends[-1],))
    out0, ring1 = pass_on(0, (sends[-1],), (ring1,))
    ring2 = lax.ppermute(ring1, "narrow", to_next)
    (q0,) = rotate_chunk(0, (out0,))
    (out1,) = pass_on(1, (q0,))
    sub0, _ = attend_chunk(0, (out1,))
    (q1,) = rotate_chunk(1, (sub0[0],))
    sub, _ = attend_chunk(1, (q1,), sub0)
    aside = gather(sub[3])
    sub = hold(sub[:3], (ring2,))
    keep, send = output(prompt_lengths, aside, (ring0,), up_out, True, ())
    extra = lax.ppermute(fold(keep, lax.ppermute(send, "wide", across)), "narrow", to_before)
    near0 = beside(
        (sub[0], lax.ppermute(sub[1], "narrow", to_next), lax.ppermute(sub[2], "narrow", to_second)), ()
    )
    keep, send = output(prompt_lengths, gather(near0), (ring0, ring1, ring2), up_out, False, ())
    total = fold(keep, lax.ppermute(send, "wide", across), extra)
    rows_of = lambda to: lax.dynamic_index_in_dim(total, to, 0, keepdims=False)
    full = [rows_of(chip)] + [
        lax.ppermute(rows_of(chip ^ delta), "wide", flip(2 * delta)) for delta in (1, 2, 3)
    ]
    full = jnp.stack(full)
    wide_rows = full.astype(F32)
    mean_square = jnp.sum(wide_rows * wide_rows, axis=(0, 2)) / features
    scaled = (wide_rows * lax.rsqrt(mean_square + epsilon)[None, :, None]).astype(BF16)
    finals = []
    for k in range(4):
        piece = lax.dynamic_index_in_dim(scaled, chip ^ ((z + k) & 3), 0, keepdims=False)
        finals.append(piece if k == 0 else lax.ppermute(piece, "narrow", shift(k)))
    own_width = post_gain.shape[0]
    own_stream = lax.dynamic_slice_in_dim(residual, z * own_width, own_width, 1)
    return close(own_stream, post_gain, finals)
def rotate(values, position):
    half = values.shape[-1] // 2
    exponent = jnp.arange(half, dtype=jnp.float32) * (2.0 / values.shape[-1])
    frequency = jnp.power(jnp.float32(rotary_base), -exponent)
    angle = position.astype(jnp.float32)[:, None] * frequency[None, :]
    cosine = jnp.cos(angle)[:, None, :]
    sine = jnp.sin(angle)[:, None, :]
    first_half = values[..., :half]
    second_half = values[..., half:]
    return jnp.concatenate(
        [first_half * cosine - second_half * sine, second_half * cosine + first_half * sine],
        axis=-1,
    )


def select_codes(codes, adapter, projections, adapters):
    count = codes.shape[0]
    width = codes.shape[1] // (adapters * projections)
    shaped = codes.reshape(count, adapters, projections, width)
    onehot = (adapter[:, None] == jnp.arange(adapters, dtype=jnp.int32)[None, :]).astype(
        codes.dtype
    )
    kept = shaped * onehot[:, :, None, None]
    return [kept[:, :, slot, :].reshape(count, adapters * width) for slot in range(projections)]


def add_adapter(partial_out, adapter_cols, offset, own_width):
    current = lax.dynamic_slice_in_dim(partial_out, offset, own_width, 1)
    return lax.dynamic_update_slice_in_dim(partial_out, current + adapter_cols, offset, 1)


def per_device(
    residual,
    pre_gain,
    query_weight,
    key_weight,
    value_weight,
    output_weight,
    adapter_down,
    adapter_up_query,
    adapter_up_key,
    adapter_up_value,
    adapter_down_out,
    adapter_up_out,
    post_gain,
    sink_logits,
    prompt_lengths,
    prompt_adapters,
):
    tok_rows = residual.shape[0]
    first = lax.axis_index("wide") * tok_rows
    member, prompt, position = token_layout(prompt_lengths, tok_rows, first)
    adapter = jnp.sum(member * prompt_adapters[None, :], axis=1)
    stream = residual.astype(jnp.float32)
    scale_rows = lax.rsqrt(jnp.mean(stream * stream, axis=1, keepdims=True) + epsilon)
    normed = (stream * scale_rows * pre_gain.astype(jnp.float32)[None, :]).astype(jnp.bfloat16)
    query_cols = query_weight.shape[1]
    key_cols = key_weight.shape[1]
    pieces = (
        lax.all_gather(query_weight, "wide", axis=0, tiled=True),
        lax.all_gather(key_weight, "wide", axis=0, tiled=True),
        lax.all_gather(value_weight, "wide", axis=0, tiled=True),
        lax.all_gather(adapter_down, "wide", axis=0, tiled=True),
    )
    query_part, key_part, value_part, code_part = tuple(
        (jnp.dot(normed, piece, preferred_element_type=jnp.float32) for piece in pieces)
    )
    codes = lax.all_gather(code_part.astype(jnp.bfloat16), "narrow", axis=1, tiled=True)
    chosen = select_codes(codes, adapter, 3, ADAPTERS)
    query = query_part + adapter_scale * jnp.dot(
        chosen[0], adapter_up_query, preferred_element_type=jnp.float32
    )
    key = key_part + adapter_scale * jnp.dot(
        chosen[1], adapter_up_key, preferred_element_type=jnp.float32
    )
    value = value_part + adapter_scale * jnp.dot(
        chosen[2], adapter_up_value, preferred_element_type=jnp.float32
    )
    local_heads = query_cols // HEAD_DIM
    local_kv = key_cols // HEAD_DIM
    group = local_heads // local_kv
    queries = (
        rotate(query.reshape(tok_rows, local_heads, HEAD_DIM), position)
        .astype(jnp.bfloat16)
        .reshape(tok_rows, local_kv, group, HEAD_DIM)
    )
    keys = rotate(key.reshape(tok_rows, local_kv, HEAD_DIM), position).astype(jnp.bfloat16)
    values = value.astype(jnp.bfloat16).reshape(tok_rows, local_kv, HEAD_DIM)
    sinks = sink_logits.reshape(local_kv, group)
    own_places = first + jnp.arange(tok_rows, dtype=jnp.int32)
    start_top = jnp.broadcast_to(sinks[None, :, :], (tok_rows, local_kv, group))
    start_total = jnp.ones((tok_rows, local_kv, group), jnp.float32)
    start_sum = jnp.zeros((tok_rows, local_kv, group, HEAD_DIM), jnp.float32)
    top = start_top
    total = start_total
    summed_values = start_sum
    piece_keys = lax.all_gather(keys, "wide", axis=0, tiled=True)
    piece_values = lax.all_gather(values, "wide", axis=0, tiled=True)
    count = piece_keys.shape[0]
    unused, key_prompt, unused_position = token_layout(prompt_lengths, count, jnp.int32(0))
    key_places = jnp.arange(count, dtype=jnp.int32)
    allowed = jnp.logical_and(
        prompt[:, None] == key_prompt[None, :], own_places[:, None] >= key_places[None, :]
    )[:, None, None, :]
    scores = (
        jnp.einsum("qgjd,kgd->qgjk", queries, piece_keys, preferred_element_type=jnp.float32)
        * score_scale
    )
    scores = jnp.where(allowed, scores, -1e30)
    fresh = jnp.maximum(top, jnp.max(scores, axis=-1))
    factor = jnp.exp(top - fresh)
    weights = jnp.where(allowed, jnp.exp(scores - fresh[..., None]), 0.0)
    total = total * factor + jnp.sum(weights, axis=-1)
    update = jnp.einsum(
        "qgjk,kgd->qgjd",
        weights.astype(jnp.bfloat16),
        piece_values,
        preferred_element_type=jnp.float32,
    )
    top, total, summed_values = (fresh, total, summed_values * factor[..., None] + update)
    attended = (
        (summed_values / total[..., None])
        .reshape(tok_rows, local_heads * HEAD_DIM)
        .astype(jnp.bfloat16)
    )
    code_terms = jnp.dot(attended, adapter_down_out, preferred_element_type=jnp.float32)
    codes_out = lax.psum(code_terms.astype(jnp.bfloat16), "narrow")
    chosen_out = select_codes(codes_out, adapter, 1, ADAPTERS)[0]
    adapter_cols = adapter_scale * jnp.dot(
        chosen_out, adapter_up_out, preferred_element_type=jnp.float32
    )
    own_width = adapter_up_out.shape[1]
    offset = lax.axis_index("narrow") * own_width
    partial_out = jnp.dot(
        attended,
        lax.all_gather(output_weight, "wide", axis=1, tiled=True),
        preferred_element_type=jnp.float32,
    )
    partial_out = add_adapter(partial_out, adapter_cols, offset, own_width)
    whole = lax.psum(partial_out.astype(jnp.bfloat16), "narrow").astype(jnp.float32)
    mean_square = jnp.mean(whole * whole, axis=1)
    projected = lax.dynamic_slice_in_dim(whole, offset, own_width, 1)
    factor_rows = lax.rsqrt(mean_square + epsilon)
    own_stream = lax.dynamic_slice_in_dim(stream, offset, own_width, 1)
    mixed = own_stream + projected * factor_rows[:, None] * post_gain.astype(jnp.float32)[None, :]
    return mixed.astype(jnp.bfloat16)


def fits(mesh):
    return mesh.shape["wide"] == 2 * CHIPS and mesh.shape["narrow"] == 4


def solution(mesh):
    return jax.shard_map(
        per_device_heads if fits(mesh) else per_device,
        mesh=mesh,
        in_specs=(
            P("wide", None),
            P(),
            P("wide", "narrow"),
            P("wide", "narrow"),
            P("wide", "narrow"),
            P("narrow", "wide"),
            P("wide", "narrow"),
            P(None, "narrow"),
            P(None, "narrow"),
            P(None, "narrow"),
            P("narrow", None),
            P(None, "narrow"),
            P("narrow"),
            P("narrow"),
            P(),
            P(),
        ),
        out_specs=P("wide", "narrow"),
        check_vma=False,
    )
```

```python
import functools

import jax
import jax.numpy as jnp
from jax import lax
from jax.experimental import pallas as pl
from jax.experimental.pallas import tpu as pltpu
from jax.sharding import PartitionSpec as P

HEAD_DIM = 128
ADAPTERS = 16
RANK = 16

epsilon = 1e-06
adapter_scale = 0.5
rotary_base = 10000.0
score_scale = 1.0 / 12.0

CHIPS = 4
CHUNKS = 2
SPAN = CHIPS // CHUNKS
STEP = 256
LOG2E = 1.4426950408889634
F32 = jnp.float32
BF16 = jnp.bfloat16
SMEM = pl.BlockSpec(memory_space=pltpu.SMEM)
VMEM = pl.BlockSpec(memory_space=pltpu.VMEM)
ANY = pl.BlockSpec(memory_space=pl.ANY)
HBM = pl.BlockSpec(memory_space=pltpu.HBM)


def token_layout(prompt_lengths, count, first):
    ends = jnp.cumsum(prompt_lengths, dtype=jnp.int32)
    starts = ends - prompt_lengths
    places = first + jnp.arange(count, dtype=jnp.int32)
    member = jnp.logical_and(
        places[:, None] >= starts[None, :], places[:, None] < ends[None, :]
    ).astype(jnp.int32)
    labels = jnp.arange(prompt_lengths.shape[0], dtype=jnp.int32)
    prompt = jnp.sum(member * labels[None, :], axis=1)
    position = places - jnp.sum(member * starts[None, :], axis=1)
    return (member, prompt, position)


def call(kernel, operands, specs, out_shape, after=(), scratch=(), name=None, flops=0, moved=0, transcendentals=0, grant=24, **more):
    n = len(after)
    return pl.pallas_call(
        lambda *refs: kernel(*refs[n:]),
        out_shape=out_shape,
        in_specs=[ANY] * n + list(specs),
        scratch_shapes=list(scratch),
        name=name,
        compiler_params=pltpu.CompilerParams(vmem_limit_bytes=grant * 1024 * 1024),
        cost_estimate=pl.CostEstimate(flops=flops, bytes_accessed=moved, transcendentals=transcendentals),
        **more,
    )(*after, *operands)


def prompt_of(places, lengths_ref, prompts):
    end = jnp.int32(0)
    prompt = jnp.zeros_like(places)
    start = jnp.zeros_like(places)
    for p in range(prompts - 1):
        end = end + lengths_ref[p]
        past = places >= end
        prompt = jnp.where(past, p + 1, prompt)
        start = jnp.where(past, end, start)
    return prompt, start


def order(chip, core):
    return (chip ^ (1 + core), chip ^ 3, chip ^ (2 - core), chip)


NEXT = (1, 3, 0, 2)
BEFORE = (2, 0, 3, 1)


def plane(table, z):
    return jnp.where(z == 0, table[0], jnp.where(z == 1, table[1], jnp.where(z == 2, table[2], table[3])))


def near(chip, core):
    return (chip, chip ^ (1 + core), chip ^ (2 - core), chip ^ 3)


def norm_kernel(steps, x_hbm, gain_ref, *refs):
    (first_ref, second_ref, own_ref), (x_ref, y_ref, in_sems, out_sems) = refs[:3], refs[3:]
    me = lax.axis_index("wide")
    chip, core = lax.shift_right_logical(me, 1), me & 1
    depth = own_ref.shape[1]
    rows = x_ref.shape[0]
    step = rows // steps
    loads = [
        pltpu.make_async_copy(x_hbm.at[pl.ds(i * step, step), :], x_ref.at[pl.ds(i * step, step), :], in_sems.at[i])
        for i in range(steps)
    ]
    for load in loads:
        load.start()
    gain = gain_ref[...].astype(F32).reshape(1, -1)
    copies = []
    for i in range(steps):
        loads[i].wait()
        at = i * step
        x = x_ref[at : at + step, :].astype(F32)
        scale = lax.rsqrt(jnp.sum(x * x, axis=1, keepdims=True) / x.shape[1] + epsilon)
        y_ref[at : at + step, :] = (x * scale * gain).astype(BF16)
        for to, out, base in zip(order(chip, core), (first_ref, first_ref, second_ref, own_ref), (0, rows, 0, 0)):
            source = y_ref.at[pl.ds(at, step), pl.ds(pl.multiple_of(to * depth, 128), depth)]
            target = out.at[pl.ds(base + at, step), :]
            copies.append(pltpu.make_async_copy(source, target, out_sems.at[len(copies)]))
            copies[-1].start()
    for copy in copies:
        copy.wait()


def norm(x, gain, steps, after):
    rows, cols = x.shape
    depth = cols // CHIPS
    shape = jax.ShapeDtypeStruct((rows, depth), x.dtype)
    return call(
        functools.partial(norm_kernel, steps), (x, gain), [HBM, VMEM],
        (jax.ShapeDtypeStruct((2 * rows, depth), x.dtype), shape, shape), after,
        scratch=[
            pltpu.VMEM((rows, cols), BF16),
            pltpu.VMEM((rows, cols), BF16),
            pltpu.SemaphoreType.DMA((steps,)),
            pltpu.SemaphoreType.DMA((4 * steps,)),
        ],
        out_specs=(ANY,) * 3, name="norm", grant=60, flops=x.size * 4, moved=x.size * 4,
    )


def arrange_kernel(q_hbm, k_hbm, v_hbm, o_hbm, theirs_ref, q_ref, k_ref, v_ref, o_ref, in_sems, sems):
    me = lax.axis_index("wide")
    chip, own = lax.shift_right_logical(me, 1), me & 1
    d = HEAD_DIM
    loads = [
        pltpu.make_async_copy(source, target, in_sems.at[i])
        for i, (source, target) in enumerate(
            ((q_hbm, q_ref), (k_hbm, k_ref), (v_hbm, v_ref), (o_hbm, o_ref))
        )
    ]
    for one in loads:
        one.start()
    copies = []
    for load, ref, part in zip(loads, (q_ref, k_ref, v_ref, o_ref), range(4)):
        load.wait()
        for source, target in column_copies(ref, theirs_ref, part, chip, 1 - own):
            copies.append(pltpu.make_async_copy(source, target, sems.at[len(copies)]))
            copies[-1].start()
    for one in copies:
        one.wait()


def column_copies(ref, out, part, chip, core):
    d = HEAD_DIM
    if part == 3:
        pairs = [((2 * source + core) * d, (4 * CHIPS + place) * d) for place, source in enumerate(near(chip, core))]
        width = d
    else:
        width, at = ((2 * d, 0), (d, 2 * d), (d, 3 * d))[part]
        pairs = [(to * width, 4 * place * d + at) for place, to in enumerate(order(chip, core))]
    return [
        (ref.at[:, pl.ds(pl.multiple_of(a, d), width)], out.at[:, pl.ds(b, width)]) for a, b in pairs
    ]


def arrange(q, k, v, o, after):
    return call(
        arrange_kernel, (q, k, v, o), [HBM] * 4,
        jax.ShapeDtypeStruct((q.shape[0], 5 * CHIPS * HEAD_DIM), BF16), after,
        scratch=[pltpu.VMEM(x.shape, BF16) for x in (q, k, v, o)]
        + [pltpu.SemaphoreType.DMA((4,)), pltpu.SemaphoreType.DMA((16,))],
        out_specs=ANY, name="arrange", grant=60, moved=q.size * 16,
    )


def lower_kernel(x_ref, out_ref, sem):
    rows = out_ref.shape[0]
    copy = pltpu.make_async_copy(x_ref.at[pl.ds(x_ref.shape[0] - rows, rows), :], out_ref, sem)
    copy.start()
    copy.wait()


def lower(x, after):
    return call(
        lower_kernel, (x,), [ANY], jax.ShapeDtypeStruct((x.shape[0] // 2, x.shape[1]), x.dtype), after,
        scratch=[pltpu.SemaphoreType.DMA(())], out_specs=ANY, name="lower", moved=x.size * 2,
    )


def choose(shape, row_prompt, chosen_ref, prompts):
    adapter = jnp.zeros(shape, jnp.int32)
    for p in range(prompts):
        adapter = jnp.where(row_prompt == p, chosen_ref[p], adapter)
    return adapter


def pick_kernel(prompts, chosen_ref, down_ref, other_ref, upo_hbm, pack_ref, upo_ref, sems):
    me, z = lax.axis_index("wide"), lax.axis_index("narrow")
    chip = lax.shift_right_logical(me, 1)
    core = me & 1
    n_codes = prompts * RANK
    local = down_ref.shape[0] // (3 * RANK)
    rows = down_ref.shape[1]
    copies = []
    for p in range(prompts):
        at = pl.ds(pl.multiple_of(chosen_ref[p] * RANK, RANK), RANK)
        copies.append(pltpu.make_async_copy(upo_hbm.at[at, :], upo_ref.at[pl.ds(p * RANK, RANK), :], sems.at[p]))
    for copy in copies:
        copy.start()
    shape = (3 * n_codes, down_ref.shape[0])
    row = lax.broadcasted_iota(jnp.int32, shape, 0)
    col = lax.broadcasted_iota(jnp.int32, shape, 1)
    adapter = choose(shape, (row % n_codes) // RANK, chosen_ref, prompts)

    def pick_of(plane_at):
        wanted = (adapter - plane_at * local) * (3 * RANK) + (row // n_codes) * RANK + row % RANK
        inside = jnp.logical_and(adapter >= plane_at * local, adapter < (plane_at + 1) * local)
        return jnp.where(jnp.logical_and(inside, col == wanted), 1.0, 0.0).astype(BF16)

    mine, theirs = pick_of(z), pick_of(z ^ 1)
    for copy in copies:
        copy.wait()
    down = jnp.dot(mine, down_ref[...], preferred_element_type=F32)
    down = down + jnp.dot(theirs, other_ref[...], preferred_element_type=F32)
    pack_ref[: 3 * n_codes, :] = down.astype(BF16)
    both = upo_ref[...].astype(F32) * adapter_scale
    part = jnp.where(core == 0, both[:, :rows], both[:, rows:])
    pack_ref[3 * n_codes :, :] = jnp.where(z == chip, part, 0.0).astype(BF16)


def pick(chosen, down, other, upo, after):
    prompts = chosen.shape[0]
    n_codes = prompts * RANK
    return call(
        functools.partial(pick_kernel, prompts), (chosen, down, other, upo), [SMEM, VMEM, VMEM, ANY],
        jax.ShapeDtypeStruct((4 * n_codes, down.shape[1]), BF16),
        after,
        scratch=[
            pltpu.VMEM((n_codes, upo.shape[1]), BF16),
            pltpu.SemaphoreType.DMA((prompts,)),
        ],
        out_specs=VMEM, name="pick", flops=down.size * 400, moved=down.size * 6,
    )


def merge_kernel(a_ref, b_ref, out_ref):
    out_ref[...] = (a_ref[...].astype(F32) + b_ref[...].astype(F32)).astype(out_ref.dtype)


def merge(a, b, after=()):
    return call(
        merge_kernel, (a, b), [VMEM, VMEM], jax.ShapeDtypeStruct(a.shape, BF16), after,
        out_specs=VMEM, name="merge", flops=a.size, moved=a.size * 6,
    )


def ups_kernel(prompts, chosen_ref, upq_ref, upk_ref, upv_ref, ado_ref, up_ref, out_ref):
    me = lax.axis_index("wide")
    chip = lax.shift_right_logical(me, 1)
    core = me & 1
    d = HEAD_DIM
    n_codes = prompts * RANK
    up_ref[...] = jnp.zeros_like(up_ref)
    for p in range(prompts):
        rows = pl.ds(pl.multiple_of(chosen_ref[p] * RANK, RANK), RANK)
        for place, to in enumerate(order(chip, core)):
            for slot, (ref, width, at) in enumerate(((upq_ref, 2 * d, 0), (upk_ref, d, 2 * d), (upv_ref, d, 3 * d))):
                part = ref[rows, pl.ds(pl.multiple_of(to * width, d), width)].astype(F32) * adapter_scale
                first = slot * n_codes + p * RANK
                left = 4 * place * d + at
                up_ref[first : first + RANK, left : left + width] = part.astype(BF16)
    shape = (n_codes, ado_ref.shape[1])
    row = lax.broadcasted_iota(jnp.int32, shape, 0)
    col = lax.broadcasted_iota(jnp.int32, shape, 1)
    adapter = choose(shape, row // RANK, chosen_ref, prompts)
    pick = jnp.where(col == adapter * RANK + row % RANK, 1.0, 0.0).astype(BF16)
    for place, source in enumerate(near(chip, core)):
        block = ado_ref[pl.ds(pl.multiple_of((2 * source + core) * d, d), d), :]
        part = lax.dot_general(pick, block, (((1,), (1,)), ((), ())), preferred_element_type=F32)
        out_ref[:, place * d : (place + 1) * d] = part.astype(BF16)


def ups(chosen, upq, upk, upv, ado, after):
    prompts = chosen.shape[0]
    n_codes = prompts * RANK
    return call(
        functools.partial(ups_kernel, prompts), (chosen, upq, upk, upv, ado), [SMEM] + [VMEM] * 4,
        (
            jax.ShapeDtypeStruct((3 * n_codes, 2 * upq.shape[1]), BF16),
            jax.ShapeDtypeStruct((n_codes, CHIPS * HEAD_DIM), BF16),
        ),
        after, out_specs=(VMEM,) * 2, name="ups", flops=upq.size * 100, moved=upq.size * 6,
    )


def stack_kernel(q_ref, k_ref, v_ref, o_ref, got_ref, down_ref, w_ref, ring_ref, sems):
    me = lax.axis_index("wide")
    chip, core = lax.shift_right_logical(me, 1), me & 1
    rows = got_ref.shape[0]
    cols = w_ref.shape[1]
    width = ring_ref.shape[1]
    copies = []

    def copy(source, target):
        copies.append(pltpu.make_async_copy(source, target, sems.at[len(copies)]))
        copies[-1].start()

    mine = pl.ds(pl.multiple_of(core * rows, 16), rows)
    theirs = pl.ds(pl.multiple_of((1 - core) * rows, 16), rows)
    for part, ref in enumerate((q_ref, k_ref, v_ref)):
        for source, target in column_copies(ref, w_ref.at[mine, :], part, chip, core):
            copy(source, target)
    d = HEAD_DIM
    for place, source in enumerate(near(chip, core)):
        at = pl.multiple_of((2 * source + core) * d, d)
        copy(o_ref.at[:, pl.ds(at, d)], ring_ref.at[mine, pl.ds(place * d, d)])
    copy(got_ref.at[:, pl.ds(0, cols)], w_ref.at[theirs, :])
    copy(got_ref.at[:, pl.ds(cols, width)], ring_ref.at[theirs, :])
    copy(down_ref, ring_ref.at[pl.ds(2 * rows, down_ref.shape[0]), :])
    for one in copies:
        one.wait()


def stack(q, k, v, o, got, down, after):
    rows, cols = got.shape
    width = down.shape[1]
    return call(
        stack_kernel, (q, k, v, o, got, down), [ANY] * 6,
        (
            jax.ShapeDtypeStruct((2 * rows, cols - width), got.dtype),
            jax.ShapeDtypeStruct((2 * rows + down.shape[0], width), got.dtype),
        ),
        after,
        scratch=[pltpu.SemaphoreType.DMA((19,))], out_specs=(ANY, ANY), name="stack", moved=rows * cols * 8,
    )


def join_kernel(mine_ref, other_ref, out_ref):
    core = lax.axis_index("wide") & 1
    mine, other = mine_ref[...].astype(F32), other_ref[...].astype(F32)
    left = jnp.where(core == 0, mine, other)
    right = jnp.where(core == 0, other, mine)
    out_ref[...] = jnp.concatenate([left, right], axis=1).astype(out_ref.dtype)


def join(mine, other, after=()):
    rows, cols = mine.shape
    return call(
        join_kernel, (mine, other), [VMEM, VMEM], jax.ShapeDtypeStruct((rows, 2 * cols), mine.dtype), after,
        out_specs=VMEM, name="join", flops=rows * cols * 4, moved=rows * cols * 8,
    )


def project_kernel(chunk, prompts, lengths_ref, *refs):
    x_refs = refs[:4]
    w_ref, pack_ref, up_ref = refs[4:7]
    send_ref, keep_ref, x_ref, sem = refs[-4:]
    me = lax.axis_index("wide")
    chip = lax.shift_right_logical(me, 1)
    core = me & 1
    rows = x_ref.shape[0]
    tok = rows // SPAN
    half = send_ref.shape[1]
    n_codes = prompts * RANK
    for i in range(SPAN):
        for k, held in enumerate((chip ^ (1 + core), chip ^ 3, chip ^ (2 - core), chip)):

            @pl.when(held == SPAN * chunk + i)
            def _():
                pltpu.make_async_copy(
                    x_refs[k].at[pl.ds(0, tok), :], x_ref.at[pl.ds(i * tok, tok), :], sem.at[i]
                ).start()

    for i in range(SPAN):
        pltpu.make_async_copy(x_refs[3], x_ref.at[pl.ds(i * tok, tok), :], sem.at[i]).wait()
    x = x_ref[...]
    codes = lax.dot_general(
        x, pack_ref[...], (((1,), (1,)), ((), ())), preferred_element_type=F32
    )
    row = lax.broadcasted_iota(jnp.int32, (rows, 1), 0)
    places = (2 * (SPAN * chunk + row // tok) + core) * tok + row % tok
    prompt, _ = prompt_of(places, lengths_ref, prompts)
    lane = lax.broadcasted_iota(jnp.int32, codes.shape, 1)
    owner = (lane % n_codes) // RANK
    codes = jnp.where(owner == prompt, codes, 0.0).astype(BF16)
    for part, out in ((0, send_ref), (1, keep_ref)):
        cols = pl.ds(part * half, half)
        product = jnp.dot(x, w_ref[:, cols], preferred_element_type=F32)
        product = product + jnp.dot(codes, up_ref[:, cols], preferred_element_type=F32)
        out[...] = product.astype(out.dtype)


def project(lengths, pieces, w, pack, up, chunk, after, carry=()):
    rows, depth = SPAN * pieces[3].shape[0], pieces[3].shape[1]
    half = w.shape[1] // 2
    n = len(after) + 8
    out = call(
        functools.partial(project_kernel, chunk, lengths.shape[0]),
        (lengths, *pieces, w, pack, up, *carry),
        [SMEM] + [ANY] * 4 + [VMEM] * 3 + [ANY] * len(carry),
        tuple(jax.ShapeDtypeStruct(c.shape, c.dtype) for c in carry)
        + (jax.ShapeDtypeStruct((rows, half), BF16), jax.ShapeDtypeStruct((rows, half), F32)),
        after,
        scratch=[pltpu.VMEM((rows, depth), BF16), pltpu.SemaphoreType.DMA((SPAN,))],
        out_specs=(ANY,) * len(carry) + (VMEM, VMEM), name="project",
        input_output_aliases={n + i: i for i in range(len(carry))},
        flops=2 * rows * depth * w.shape[1], moved=rows * depth * 2 + w.size * 2 + rows * half * 6,
    )
    return out[-2], out[-1], out[:-2]


def onward_kernel(keep_ref, first_ref, *refs):
    out_ref = refs[-1]
    own = out_ref.shape[1]
    out_ref[...] = (keep_ref[:, :own] + first_ref[:, own:].astype(F32)).astype(BF16)


def onward(keep, first, after, carry=()):
    rows, cols = keep.shape
    n = len(after) + 2
    out = call(
        onward_kernel, (keep, first, *carry), [VMEM, VMEM] + [ANY] * len(carry),
        tuple(jax.ShapeDtypeStruct(c.shape, c.dtype) for c in carry)
        + (jax.ShapeDtypeStruct((rows, cols // 2), BF16),),
        after, out_specs=(ANY,) * len(carry) + (VMEM,), name="onward",
        input_output_aliases={n + i: i for i in range(len(carry))},
        flops=rows * cols, moved=rows * cols * 4,
    )
    return out[-1], out[:-1]


def finish_kernel(chunk, keep_ref, first_ref, second_ref, cos_ref, sin_ref, *refs):
    own_ref, send_ref = refs[-2:]
    tok = own_ref.shape[0] // SPAN
    d = HEAD_DIM
    own = keep_ref.shape[1] // 2
    core = lax.axis_index("wide") & 1
    for i in range(SPAN):
        at = pl.ds(pl.multiple_of((2 * (SPAN * chunk + i) + core) * tok, tok), tok)
        rows = slice(i * tok, (i + 1) * tok)
        cosine, sine = cos_ref[at, :], sin_ref[at, :]
        total = keep_ref[rows, own:] + first_ref[rows, :own].astype(F32) + second_ref[rows, :].astype(F32)
        q0, q1, k = (
            x * cosine + pltpu.roll(x, d // 2, 1) * sine for x in (total[:, n * d : (n + 1) * d] for n in range(3))
        )
        q0, q1 = q0 * (score_scale * LOG2E), q1 * (score_scale * LOG2E)
        own_ref[rows, :d] = jnp.where(core == 0, q0, q1).astype(BF16)
        send_ref[rows, :d] = jnp.where(core == 0, q1, q0).astype(BF16)
        both = jnp.concatenate([k, total[:, 3 * d :]], axis=1).astype(BF16)
        own_ref[rows, d:] = both
        send_ref[rows, d:] = both


def finish(keep, first, second, tables, chunk, after, carry=()):
    rows = keep.shape[0]
    shape = jax.ShapeDtypeStruct((rows, 3 * HEAD_DIM), BF16)
    n = len(after) + 5
    out = call(
        functools.partial(finish_kernel, chunk),
        (keep, first, second, *tables, *carry), [VMEM] * 5 + [ANY] * len(carry),
        tuple(jax.ShapeDtypeStruct(c.shape, c.dtype) for c in carry) + (shape, shape), after,
        out_specs=(ANY,) * len(carry) + (VMEM, VMEM), name="finish",
        input_output_aliases={n + i: i for i in range(len(carry))},
        flops=rows * 2048, moved=rows * 8192,
    )
    return out[-2], out[-1], out[:-2]


def attend_kernel(chunk, prompts, n_before, n_carry, lengths_ref, sink_ref, *refs):
    count = chunk + 1
    mine_refs, other_refs = refs[:count], refs[count : 2 * count]
    befores = refs[2 * count : 2 * count + n_before]
    outs = refs[2 * count + n_before + 2 * n_carry :][:4]
    q_ref, k_ref, v_ref, out_ref = refs[-4:]
    step = mine_refs[0].shape[0] // SPAN
    d = HEAD_DIM
    here, z = lax.axis_index("wide"), lax.axis_index("narrow")
    core = here & 1
    for c in range(count):
        for i in range(SPAN):
            mine, other = (refs_of[c][i * step : (i + 1) * step, :] for refs_of in (mine_refs, other_refs))
            for half, block in enumerate((jnp.where(core == 0, mine, other), jnp.where(core == 0, other, mine))):
                at = pl.ds((2 * (SPAN * c + i) + half) * step, step)
                k_ref[at, :] = block[:, d : 2 * d]
                v_ref[at, :] = block[:, 2 * d :]
                if c == chunk:
                    q_ref[(2 * i + half) * step : (2 * i + half + 1) * step, :] = block[:, :d]
    shift = 0
    for k in range(n_before):
        shift = befores[k].shape[0]
        outs[k][:shift, :] = befores[k][...]
    for i in range(SPAN):
        attend_block(
            SPAN * chunk + i, prompts, step, lengths_ref, sink_ref, q_ref.at[pl.ds(2 * i * step, 2 * step), :],
            k_ref, v_ref, out_ref, outs, shift + i * step // 2,
        )


def attend_block(chip, prompts, step, lengths_ref, sink_ref, q_ref, k_ref, v_ref, out_ref, outs, shift):
    d = HEAD_DIM
    here, z = lax.axis_index("wide"), lax.axis_index("narrow")
    top = sink_ref[here] * LOG2E
    to = (z, plane(NEXT, z), 3 - z, plane(BEFORE, z))
    part = step // 4
    rows = 2 * step
    base = chip * rows
    q = q_ref[...]
    places = base + lax.broadcasted_iota(jnp.int32, (rows, 1), 0)
    _, starts = prompt_of(places, lengths_ref, prompts)
    end = jnp.int32(0)
    low = jnp.int32(0)
    high = jnp.int32(0)
    for p in range(prompts - 1):
        end = end + lengths_ref[p]
        low = jnp.where(base >= end, end, low)
        high = jnp.where(base + rows > end, end, high)

    def body(masked):
        def one(i, carry):
            top, total, summed = carry
            at = pl.multiple_of(i * STEP, STEP)
            k = k_ref[pl.ds(at, STEP), :]
            v = v_ref[pl.ds(at, STEP), :]
            scores = lax.dot_general(q, k, (((1,), (1,)), ((), ())), preferred_element_type=F32)
            if masked:
                keys = at + lax.broadcasted_iota(jnp.int32, scores.shape, 1)
                scores = jnp.where(jnp.logical_and(keys >= starts, keys <= places), scores, -1e30)
            fresh = jnp.maximum(top, jnp.max(scores, axis=1, keepdims=True))
            factor = jnp.exp2(top - fresh)
            weights = jnp.exp2(scores - fresh)
            total = total * factor + jnp.sum(weights, axis=1, keepdims=True)
            summed = summed * factor + jnp.dot(weights.astype(BF16), v, preferred_element_type=F32)
            return fresh, total, summed

        return one

    carry = (jnp.full((rows, 1), top, F32), jnp.ones((rows, 1), F32), jnp.zeros((rows, d), F32))
    first = low // STEP
    last = base // STEP
    whole = jnp.minimum((high + STEP - 1) // STEP, last)
    carry = lax.fori_loop(first, whole, body(True), carry)
    carry = lax.fori_loop(whole, last, body(False), carry)
    for i in range(last, (base + rows) // STEP):
        carry = body(True)(i, carry)
    _, total, summed = carry
    out_ref[...] = (summed / total).astype(BF16)
    for block in range(2):
        for k in range(4):
            at = pl.multiple_of(block * step + to[k] * part, part)
            first = shift + block * part
            outs[k][first : first + part, :] = out_ref[pl.ds(at, part), :]


def attend(lengths, sinks, mine, other, chunk, after, before=(), carry=()):
    step = mine[0].shape[0] // SPAN
    d = HEAD_DIM
    count = chunk + 1
    rows = SPAN * step // 2 + (before[0].shape[0] if before else 0)
    n = len(after) + 2 + 2 * count + len(before)
    out = call(
        functools.partial(attend_kernel, chunk, lengths.shape[0], len(before), len(carry)),
        (lengths, sinks, *mine[:count], *other[:count], *before, *carry),
        [SMEM, SMEM] + [VMEM] * (2 * count + len(before)) + [ANY] * len(carry),
        tuple(jax.ShapeDtypeStruct(c.shape, c.dtype) for c in carry)
        + (jax.ShapeDtypeStruct((rows, d), BF16),) * 4,
        after,
        scratch=[pltpu.VMEM((2 * SPAN * step, d), BF16)]
        + [pltpu.VMEM((2 * SPAN * count * step, d), BF16)] * 2
        + [pltpu.VMEM((2 * step, d), BF16)],
        out_specs=(ANY,) * len(carry) + (VMEM,) * 4, name="attend",
        input_output_aliases={n + i: i for i in range(len(carry))},
        flops=2 * SPAN * step * 768 * 4 * d, moved=step * d * 8 * count, transcendentals=2 * SPAN * step * 768,
    )
    return out[len(carry) :], out[: len(carry)]


def beside_kernel(*refs):
    out_ref = refs[-1]
    width = refs[0].shape[1]
    for i, ref in enumerate(refs[:-1]):
        out_ref[:, i * width : (i + 1) * width] = ref[...]


def beside(parts, after):
    rows, cols = parts[0].shape
    return call(
        beside_kernel, parts, [VMEM] * len(parts), jax.ShapeDtypeStruct((rows, cols * len(parts)), BF16), after,
        out_specs=VMEM, name="beside", moved=rows * cols * len(parts) * 4,
    )


def hold_kernel(*refs):
    pass


def hold(arrays, after):
    n = len(after)
    return call(
        hold_kernel, arrays, [ANY] * len(arrays), tuple(jax.ShapeDtypeStruct(a.shape, a.dtype) for a in arrays),
        after, out_specs=(ANY,) * len(arrays), name="hold",
        input_output_aliases={n + i: i for i in range(len(arrays))},
    )


def output_kernel(before, count, prompts, lengths_ref, *refs):
    blocks = refs[:4]
    weights = refs[4 : 4 + count]
    up_ref, keep_ref, send_ref, acc_ref = refs[4 + count :]
    z = lax.axis_index("narrow")
    core = lax.axis_index("wide") & 1
    rows, cols = acc_ref.shape
    d = HEAD_DIM
    chips, part = keep_ref.shape[:2]
    codes = None
    for k in range(count):
        a = jnp.concatenate([blocks[r][:, k * d : (k + 1) * d] for r in range(4)], axis=1)
        product = lax.dot_general(a, weights[k][:cols, :], (((1,), (1,)), ((), ())), preferred_element_type=F32)
        terms = lax.dot_general(a, weights[k][cols:, :], (((1,), (1,)), ((), ())), preferred_element_type=F32)
        if k == 0:
            acc_ref[...] = product
            codes = terms
        else:
            acc_ref[...] += product
            codes = codes + terms
    row = lax.broadcasted_iota(jnp.int32, (rows, 1), 0)
    places = (row // part) * (4 * part) + (plane(BEFORE, z) if before else z) * part + row % part
    prompt, _ = prompt_of(places, lengths_ref, prompts)
    lane = lax.broadcasted_iota(jnp.int32, codes.shape, 1)
    codes = jnp.where(lane // RANK == prompt, codes, 0.0).astype(BF16)
    acc_ref[...] += jnp.dot(codes, up_ref[...], preferred_element_type=F32)
    for i in range(chips):
        mine = pl.multiple_of(i * 2 * part + core * part, part)
        theirs = pl.multiple_of(i * 2 * part + (1 - core) * part, part)
        keep_ref[i] = acc_ref[pl.ds(mine, part), :]
        send_ref[i] = acc_ref[pl.ds(theirs, part), :].astype(BF16)


def output(lengths, blocks, weights, up, before, after):
    rows = blocks[0].shape[0]
    cols = up.shape[1]
    shape = (CHIPS, rows // (2 * CHIPS), cols)
    return call(
        functools.partial(output_kernel, before, len(weights), lengths.shape[0]),
        (lengths, *blocks, *weights, up),
        [SMEM] + [VMEM] * (5 + len(weights)),
        (jax.ShapeDtypeStruct(shape, F32), jax.ShapeDtypeStruct(shape, BF16)),
        after,
        scratch=[pltpu.VMEM((rows, cols), F32)],
        out_specs=(VMEM, VMEM), name="output",
        flops=2 * rows * 512 * len(weights) * cols, moved=2048 * cols * 2 + rows * 2048 * 2 + rows * cols * 3,
    )


def fold_kernel(*refs):
    total = refs[0][...]
    for ref in refs[1:-1]:
        total = total + ref[...].astype(F32)
    refs[-1][...] = total.astype(BF16)


def fold(keep, *got):
    return call(
        fold_kernel, (keep, *got), [VMEM] * (1 + len(got)), jax.ShapeDtypeStruct(keep.shape, BF16),
        out_specs=VMEM, name="fold", flops=keep.size, moved=keep.size * 8,
    )


def total_kernel(keep_ref, got_ref, extra_ref, *outs):
    chip = lax.shift_right_logical(lax.axis_index("wide"), 1)
    for delta in range(CHIPS):
        at = chip ^ delta
        outs[delta][...] = (keep_ref[at] + got_ref[at].astype(F32) + extra_ref[at].astype(F32)).astype(BF16)


def total_rows(keep, got, extra):
    shape = jax.ShapeDtypeStruct(keep.shape[1:], BF16)
    return call(
        total_kernel, (keep, got, extra), [VMEM] * 3, (shape,) * CHIPS,
        out_specs=(VMEM,) * CHIPS, name="total_rows", flops=keep.size, moved=keep.size * 8,
    )


def settle_kernel(*refs):
    pieces, outs, held = refs[:4], refs[4:8], refs[8]
    chip, z = lax.shift_right_logical(lax.axis_index("wide"), 1), lax.axis_index("narrow")
    count = 4 * held.shape[2]
    total = 0.0
    for ref in pieces:
        x = ref[...].astype(F32)
        total = total + jnp.sum(x * x, axis=1, keepdims=True)
    scale = lax.rsqrt(total / count + epsilon)
    for delta, ref in enumerate(pieces):
        held[delta] = (ref[...].astype(F32) * scale).astype(BF16)
    for k in range(4):
        outs[k][...] = held[chip ^ ((z + k) & 3)]


def settle(pieces):
    shape = jax.ShapeDtypeStruct(pieces[0].shape, BF16)
    return call(
        settle_kernel, pieces, [VMEM] * 4, (shape,) * 4, scratch=[pltpu.VMEM((4, *shape.shape), BF16)],
        out_specs=(VMEM,) * 4, name="settle", flops=shape.size * 16, moved=shape.size * 16,
    )


def close_kernel(stream_ref, gain_ref, *refs):
    pieces = refs[:4]
    out_ref = refs[4]
    z = lax.axis_index("narrow")
    part = pieces[0].shape[0]
    gain = gain_ref[...].astype(F32)
    for k in range(4):
        at = pl.multiple_of(jnp.bitwise_and(z - k + 4, 3) * part, part)
        rows = pl.ds(at, part)
        out_ref[rows, :] = (stream_ref[rows, :].astype(F32) + pieces[k][...].astype(F32) * gain).astype(BF16)


def close(stream, gain, pieces):
    return call(
        close_kernel, (stream, gain[None, :], *pieces), [VMEM] * 6,
        jax.ShapeDtypeStruct(stream.shape, BF16),
        out_specs=VMEM, name="close", flops=stream.size * 3, moved=stream.size * 6,
    )


def per_device_heads(
    residual,
    pre_gain,
    query_weight,
    key_weight,
    value_weight,
    output_weight,
    adapter_down,
    adapter_up_query,
    adapter_up_key,
    adapter_up_value,
    adapter_down_out,
    adapter_up_out,
    post_gain,
    sink_logits,
    prompt_lengths,
    prompt_adapters,
):
    tok, features = residual.shape
    depth = features // CHIPS
    own_rows = query_weight.shape[0]
    prompts = prompt_lengths.shape[0]
    d = HEAD_DIM
    me = lax.axis_index("wide")
    z = lax.axis_index("narrow")
    core = me & 1
    chip = me >> 1
    wide = 2 * CHIPS
    tokens = tok * wide

    flip = lambda bits: [(i, i ^ bits) for i in range(wide)]
    across = flip(1)
    first_leg = [(i, i ^ (2 if i % 2 == 0 else 4)) for i in range(wide)]
    second_leg = [(i, i ^ (4 if i % 2 == 0 else 2)) for i in range(wide)]
    shift = lambda k: [(i, (i + k) % 4) for i in range(4)]
    to_next = [(i, NEXT[i]) for i in range(4)]
    to_second = [(i, 3 - i) for i in range(4)]
    to_before = [(i, BEFORE[i]) for i in range(4)]
    zflip = lambda bits: [(i, i ^ bits) for i in range(4)]

    _, _, position = token_layout(prompt_lengths, tokens, jnp.int32(0))
    half = d // 2
    exponent = jnp.arange(half, dtype=F32) * (2.0 / d)
    frequency = jnp.power(jnp.float32(rotary_base), -exponent)
    angle = position.astype(F32)[:, None] * frequency[None, :]
    cosine, sine = jnp.cos(angle), jnp.sin(angle)
    cosine = jnp.concatenate([cosine, cosine], axis=1)
    sine = jnp.concatenate([-sine, sine], axis=1)

    down = adapter_down.T
    down_other = lax.ppermute(down, "narrow", zflip(1))
    first, second, own = norm(residual, pre_gain, 4, ())
    w_theirs = arrange(query_weight, key_weight, value_weight, output_weight.T, (own,))
    first = lax.ppermute(first, "wide", first_leg)
    second = lax.ppermute(second, "wide", second_leg)
    pack = pick(prompt_adapters, down, down_other, adapter_up_out, (w_theirs,))
    up, out_down = ups(
        prompt_adapters, adapter_up_query, adapter_up_key, adapter_up_value, adapter_down_out, (w_theirs,)
    )
    w, ring0 = stack(
        query_weight, key_weight, value_weight, output_weight.T, lax.ppermute(w_theirs, "wide", across), out_down, (up,)
    )
    third = lax.ppermute(lower(first, (w,)), "wide", second_leg)
    pieces = (first, third, second, own)
    pack = merge(pack, lax.ppermute(pack, "narrow", zflip(2)), (w, cosine, sine))
    n_down = 3 * prompts * RANK
    up_out = pack[n_down:]
    up_out = up_out + lax.ppermute(up_out, "narrow", zflip(1))
    pack = join(pack[:n_down], lax.ppermute(pack[:n_down], "wide", across))
    ring1 = lax.ppermute(ring0, "narrow", to_next)

    tables = (cosine, sine)
    part = tok // 4
    sends, keeps, ones, twos, mine, other = [], [], [], [], [], []

    def product(chunk, after, carry=()):
        send, keep, carried = project(prompt_lengths, pieces, w, pack, up, chunk, after, carry)
        sends.append(send)
        keeps.append(keep)
        ones.append(lax.ppermute(send, "wide", first_leg))
        return carried

    def pass_on(chunk, after, carry=()):
        out, carried = onward(keeps[chunk], ones[chunk], after, carry)
        twos.append(lax.ppermute(out, "wide", second_leg))
        return (out, *carried)

    def rotate_chunk(chunk, after, carry=()):
        own, send, carried = finish(keeps[chunk], ones[chunk], twos[chunk], tables, chunk, after, carry)
        mine.append(own)
        other.append(lax.ppermute(send, "wide", across))
        return (own, *carried)

    def attend_chunk(chunk, after, before=(), carry=()):
        return attend(prompt_lengths, sink_logits, mine, other, chunk, after, before, carry)

    def gather(near0):
        near1 = lax.ppermute(near0, "wide", first_leg)
        near2 = lax.ppermute(near0, "wide", second_leg)
        return near0, near1, near2, lax.ppermute(near1, "wide", second_leg)

    product(0, ())
    product(1, (sends[-1],))
    up_out = join(up_out, lax.ppermute(up_out, "wide", across), (sends[-1],))
    out0, ring1 = pass_on(0, (sends[-1],), (ring1,))
    ring2 = lax.ppermute(ring1, "narrow", to_next)
    (q0,) = rotate_chunk(0, (out0,))
    (out1,) = pass_on(1, (q0,))
    sub0, _ = attend_chunk(0, (out1,))
    (q1,) = rotate_chunk(1, (sub0[0],))
    sub, _ = attend_chunk(1, (q1,), sub0)
    aside = gather(sub[3])
    sub = hold(sub[:3], (ring2,))
    keep, send = output(prompt_lengths, aside, (ring0,), up_out, True, ())
    extra = lax.ppermute(fold(keep, lax.ppermute(send, "wide", across)), "narrow", to_before)
    near0 = beside(
        (sub[0], lax.ppermute(sub[1], "narrow", to_next), lax.ppermute(sub[2], "narrow", to_second)), ()
    )
    keep, send = output(prompt_lengths, gather(near0), (ring0, ring1, ring2), up_out, False, ())
    cuts = total_rows(keep, lax.ppermute(send, "wide", across), extra)
    full = [cuts[0]] + [lax.ppermute(cuts[delta], "wide", flip(2 * delta)) for delta in (1, 2, 3)]
    scaled = settle(full)
    finals = [scaled[0]] + [lax.ppermute(scaled[k], "narrow", shift(k)) for k in (1, 2, 3)]
    own_width = post_gain.shape[0]
    own_stream = lax.dynamic_slice_in_dim(residual, z * own_width, own_width, 1)
    return close(own_stream, post_gain, finals)
def rotate(values, position):
    half = values.shape[-1] // 2
    exponent = jnp.arange(half, dtype=jnp.float32) * (2.0 / values.shape[-1])
    frequency = jnp.power(jnp.float32(rotary_base), -exponent)
    angle = position.astype(jnp.float32)[:, None] * frequency[None, :]
    cosine = jnp.cos(angle)[:, None, :]
    sine = jnp.sin(angle)[:, None, :]
    first_half = values[..., :half]
    second_half = values[..., half:]
    return jnp.concatenate(
        [first_half * cosine - second_half * sine, second_half * cosine + first_half * sine],
        axis=-1,
    )


def select_codes(codes, adapter, projections, adapters):
    count = codes.shape[0]
    width = codes.shape[1] // (adapters * projections)
    shaped = codes.reshape(count, adapters, projections, width)
    onehot = (adapter[:, None] == jnp.arange(adapters, dtype=jnp.int32)[None, :]).astype(
        codes.dtype
    )
    kept = shaped * onehot[:, :, None, None]
    return [kept[:, :, slot, :].reshape(count, adapters * width) for slot in range(projections)]


def add_adapter(partial_out, adapter_cols, offset, own_width):
    current = lax.dynamic_slice_in_dim(partial_out, offset, own_width, 1)
    return lax.dynamic_update_slice_in_dim(partial_out, current + adapter_cols, offset, 1)


def per_device(
    residual,
    pre_gain,
    query_weight,
    key_weight,
    value_weight,
    output_weight,
    adapter_down,
    adapter_up_query,
    adapter_up_key,
    adapter_up_value,
    adapter_down_out,
    adapter_up_out,
    post_gain,
    sink_logits,
    prompt_lengths,
    prompt_adapters,
):
    tok_rows = residual.shape[0]
    first = lax.axis_index("wide") * tok_rows
    member, prompt, position = token_layout(prompt_lengths, tok_rows, first)
    adapter = jnp.sum(member * prompt_adapters[None, :], axis=1)
    stream = residual.astype(jnp.float32)
    scale_rows = lax.rsqrt(jnp.mean(stream * stream, axis=1, keepdims=True) + epsilon)
    normed = (stream * scale_rows * pre_gain.astype(jnp.float32)[None, :]).astype(jnp.bfloat16)
    query_cols = query_weight.shape[1]
    key_cols = key_weight.shape[1]
    pieces = (
        lax.all_gather(query_weight, "wide", axis=0, tiled=True),
        lax.all_gather(key_weight, "wide", axis=0, tiled=True),
        lax.all_gather(value_weight, "wide", axis=0, tiled=True),
        lax.all_gather(adapter_down, "wide", axis=0, tiled=True),
    )
    query_part, key_part, value_part, code_part = tuple(
        (jnp.dot(normed, piece, preferred_element_type=jnp.float32) for piece in pieces)
    )
    codes = lax.all_gather(code_part.astype(jnp.bfloat16), "narrow", axis=1, tiled=True)
    chosen = select_codes(codes, adapter, 3, ADAPTERS)
    query = query_part + adapter_scale * jnp.dot(
        chosen[0], adapter_up_query, preferred_element_type=jnp.float32
    )
    key = key_part + adapter_scale * jnp.dot(
        chosen[1], adapter_up_key, preferred_element_type=jnp.float32
    )
    value = value_part + adapter_scale * jnp.dot(
        chosen[2], adapter_up_value, preferred_element_type=jnp.float32
    )
    local_heads = query_cols // HEAD_DIM
    local_kv = key_cols // HEAD_DIM
    group = local_heads // local_kv
    queries = (
        rotate(query.reshape(tok_rows, local_heads, HEAD_DIM), position)
        .astype(jnp.bfloat16)
        .reshape(tok_rows, local_kv, group, HEAD_DIM)
    )
    keys = rotate(key.reshape(tok_rows, local_kv, HEAD_DIM), position).astype(jnp.bfloat16)
    values = value.astype(jnp.bfloat16).reshape(tok_rows, local_kv, HEAD_DIM)
    sinks = sink_logits.reshape(local_kv, group)
    own_places = first + jnp.arange(tok_rows, dtype=jnp.int32)
    start_top = jnp.broadcast_to(sinks[None, :, :], (tok_rows, local_kv, group))
    start_total = jnp.ones((tok_rows, local_kv, group), jnp.float32)
    start_sum = jnp.zeros((tok_rows, local_kv, group, HEAD_DIM), jnp.float32)
    top = start_top
    total = start_total
    summed_values = start_sum
    piece_keys = lax.all_gather(keys, "wide", axis=0, tiled=True)
    piece_values = lax.all_gather(values, "wide", axis=0, tiled=True)
    count = piece_keys.shape[0]
    unused, key_prompt, unused_position = token_layout(prompt_lengths, count, jnp.int32(0))
    key_places = jnp.arange(count, dtype=jnp.int32)
    allowed = jnp.logical_and(
        prompt[:, None] == key_prompt[None, :], own_places[:, None] >= key_places[None, :]
    )[:, None, None, :]
    scores = (
        jnp.einsum("qgjd,kgd->qgjk", queries, piece_keys, preferred_element_type=jnp.float32)
        * score_scale
    )
    scores = jnp.where(allowed, scores, -1e30)
    fresh = jnp.maximum(top, jnp.max(scores, axis=-1))
    factor = jnp.exp(top - fresh)
    weights = jnp.where(allowed, jnp.exp(scores - fresh[..., None]), 0.0)
    total = total * factor + jnp.sum(weights, axis=-1)
    update = jnp.einsum(
        "qgjk,kgd->qgjd",
        weights.astype(jnp.bfloat16),
        piece_values,
        preferred_element_type=jnp.float32,
    )
    top, total, summed_values = (fresh, total, summed_values * factor[..., None] + update)
    attended = (
        (summed_values / total[..., None])
        .reshape(tok_rows, local_heads * HEAD_DIM)
        .astype(jnp.bfloat16)
    )
    code_terms = jnp.dot(attended, adapter_down_out, preferred_element_type=jnp.float32)
    codes_out = lax.psum(code_terms.astype(jnp.bfloat16), "narrow")
    chosen_out = select_codes(codes_out, adapter, 1, ADAPTERS)[0]
    adapter_cols = adapter_scale * jnp.dot(
        chosen_out, adapter_up_out, preferred_element_type=jnp.float32
    )
    own_width = adapter_up_out.shape[1]
    offset = lax.axis_index("narrow") * own_width
    partial_out = jnp.dot(
        attended,
        lax.all_gather(output_weight, "wide", axis=1, tiled=True),
        preferred_element_type=jnp.float32,
    )
    partial_out = add_adapter(partial_out, adapter_cols, offset, own_width)
    whole = lax.psum(partial_out.astype(jnp.bfloat16), "narrow").astype(jnp.float32)
    mean_square = jnp.mean(whole * whole, axis=1)
    projected = lax.dynamic_slice_in_dim(whole, offset, own_width, 1)
    factor_rows = lax.rsqrt(mean_square + epsilon)
    own_stream = lax.dynamic_slice_in_dim(stream, offset, own_width, 1)
    mixed = own_stream + projected * factor_rows[:, None] * post_gain.astype(jnp.float32)[None, :]
    return mixed.astype(jnp.bfloat16)


def fits(mesh):
    return mesh.shape["wide"] == 2 * CHIPS and mesh.shape["narrow"] == 4


def solution(mesh):
    return jax.shard_map(
        per_device_heads if fits(mesh) else per_device,
        mesh=mesh,
        in_specs=(
            P("wide", None),
            P(),
            P("wide", "narrow"),
            P("wide", "narrow"),
            P("wide", "narrow"),
            P("narrow", "wide"),
            P("wide", "narrow"),
            P(None, "narrow"),
            P(None, "narrow"),
            P(None, "narrow"),
            P("narrow", None),
            P(None, "narrow"),
            P("narrow"),
            P("narrow"),
            P(),
            P(),
        ),
        out_specs=P("wide", "narrow"),
        check_vma=False,
    )
```
